32 devices in a mesh: dp: 8 (over y, x, core), inner: 4 (over z).
Axes of the slice: x: 2, y: 2, z: 4, core: 2. Of those that a mesh axis runs over, the one named last changes fastest.
Arguments:
- image: bfloat16 [4096, 1152], P(('dp', 'inner')), may hold values from -0.059814453 to 0.059814453
- text: bfloat16 [4096, 1152], P(('dp', 'inner')), may hold values from -0.059814453 to 0.059814453
- logarithm_scale: float32 [1], replicated, may hold values from 1.8 to 2.6
- bias: float32 [1], replicated, may hold values from -4 to -2
Outputs:
- image_gradient: float32 [4096, 1152], P(('dp', 'inner'))
- text_gradient: float32 [4096, 1152], P(('dp', 'inner'))
- image_loss: float32 [4096], P(('dp', 'inner'))
The draws below stay inside these ranges and needn't reach their ends.
All inputs are finite; a program needn't handle non-finite values.
Results may differ from the reference program's by a relative error of at most 0.0044.
Values may be sent and summed in bfloat16 or wider, within the bound.
No kernel may reach another device: no remote copies, remote signals or barrier semaphores. Data moves between devices by JAX's collectives and lax.ppermute only.
A program may use at most 64 MiB of HBM per device.

```python
import jax
import jax.numpy as jnp
from jax import lax

EMBED_WIDTH = 1152
ROWS = 128
PAIR_BATCH = 4096
N_INNER = 4


def level_of(key, dims, shards, low, high):
    gain, own = 1.0, jax.random.fold_in(key, 6)
    for dim, parts in shards:
        draws = jnp.exp(jax.random.uniform(jax.random.fold_in(own, dim), (parts,), jnp.float32, low / len(shards), high / len(shards)))
        gain = gain * jnp.repeat(draws, dims[dim] // parts).reshape([-1 if axis == dim else 1 for axis in range(len(dims))])
    return gain


def noise(key, shape, width, limit, cuts=(), kind=jnp.bfloat16):
    gain = level_of(key, shape, cuts, -0.22, 0.18) if cuts else 1.0
    entries = jax.random.normal(key, shape, jnp.float32) * width * gain
    return jnp.minimum(jnp.maximum(entries, -limit), limit).astype(kind)


def setup_inputs(seed: int = 0) -> dict:
    keys = jax.random.split(jax.random.key(seed), 5)
    return {
        "image": noise(keys[0], (PAIR_BATCH, EMBED_WIDTH), 0.01, 0.059814453, ((0, 32),)),
        "text": noise(keys[1], (PAIR_BATCH, EMBED_WIDTH), 0.01, 0.059814453, ((0, 32),)),
        "logarithm_scale": jnp.clip(jax.random.uniform(keys[2], (1,), jnp.float32, 1.8, 2.6), 1.8, 2.6),
        "bias": jnp.clip(jax.random.uniform(keys[3], (1,), jnp.float32, -4.0, -2.0), -4.0, -2.0),
    }


epsilon = 1e-06

def normalize(values):
    wide = values.astype(jnp.float32)
    inverse = lax.rsqrt(lax.optimization_barrier(jnp.sum(wide * wide, axis=-1, keepdims=True)) + epsilon)
    return (wide * inverse, inverse)

def reference(image, text, logarithm_scale, bias):
    normalized_image, image_inverse_norm = normalize(image)
    normalized_text, text_inverse_norm = normalize(text)
    image_emb = normalized_image.astype(jnp.bfloat16)
    text_embedding = normalized_text.astype(jnp.bfloat16)
    logit_scale = jnp.exp(logarithm_scale[0])
    logit_bias = bias[0]
    block_rows = ROWS * N_INNER
    block_count = PAIR_BATCH // block_rows
    image_blocks = image_emb.reshape(block_count, block_rows, EMBED_WIDTH)
    text_ids = jnp.arange(PAIR_BATCH, dtype=jnp.int32)

    def advance(caption_total, inputs):
        picture_block, block_index = inputs
        pair_logits = logit_scale * jnp.dot(picture_block, text_embedding.T, preferred_element_type=jnp.float32) + logit_bias
        image_ids = block_index * block_rows + jnp.arange(block_rows, dtype=jnp.int32)
        match = (image_ids[:, None] == text_ids[None, :]).astype(jnp.float32)
        loss_rows = lax.optimization_barrier(jnp.sum(jax.nn.softplus(pair_logits) - match * pair_logits, axis=1))
        slopes = (jax.nn.sigmoid(pair_logits) - match).astype(jnp.bfloat16)
        image_grad = jnp.dot(slopes, text_embedding, preferred_element_type=jnp.float32)
        caption_total = caption_total + jnp.dot(slopes.T, picture_block, preferred_element_type=jnp.float32)
        return (caption_total, (image_grad, loss_rows))
    start_total = jnp.zeros((PAIR_BATCH, EMBED_WIDTH), jnp.float32)
    caption_total, (picture_gradients, loss_rows) = lax.scan(advance, start_total, (image_blocks, jnp.arange(block_count, dtype=jnp.int32)))
    normalized_image_gradient = logit_scale * picture_gradients.reshape(PAIR_BATCH, EMBED_WIDTH)
    normalized_text_gradient = logit_scale * caption_total
    image_gradient = (normalized_image_gradient - normalized_image * lax.optimization_barrier(jnp.sum(normalized_image * normalized_image_gradient, axis=-1, keepdims=True))) * image_inverse_norm
    text_gradient = (normalized_text_gradient - normalized_text * lax.optimization_barrier(jnp.sum(normalized_text * normalized_text_gradient, axis=-1, keepdims=True))) * text_inverse_norm
    image_loss = loss_rows.reshape(PAIR_BATCH) / PAIR_BATCH
    return (image_gradient, text_gradient, image_loss)
```

```python
import functools

import jax
import jax.numpy as jnp
from jax import lax
from jax.experimental import pallas as pl
from jax.experimental.pallas import tpu as pltpu
from jax.sharding import PartitionSpec as P

epsilon = 1e-06
f32, bf16 = jnp.float32, jnp.bfloat16
lanes = 128
extra = 16
VMEM = pl.BlockSpec(memory_space=pltpu.VMEM)
SMEM = pl.BlockSpec(memory_space=pltpu.SMEM)


def swapped(value, axis, step):
    return lax.ppermute(value, axis, [(place, place ^ step) for place in range(lax.axis_size(axis))])


def call(kernel, out_shape, *operands, flops=0, in_specs=None):
    moved = sum(o.size * o.dtype.itemsize for o in operands)
    moved += sum(o.size * o.dtype.itemsize for o in jax.tree.leaves(out_shape))
    return pl.pallas_call(
        kernel,
        out_shape=out_shape,
        in_specs=in_specs or [VMEM] * len(operands),
        out_specs=jax.tree.map(lambda _: VMEM, out_shape),
        compiler_params=pltpu.CompilerParams(vmem_limit_bytes=40 * 1024 * 1024),
        cost_estimate=pl.CostEstimate(flops=flops, bytes_accessed=moved, transcendentals=0),
    )(*operands)


def shape(dims, kind):
    return jax.ShapeDtypeStruct(dims, kind)


def unit_of(rows):
    wide = rows.astype(f32)
    inverse = lax.rsqrt(jnp.sum(wide * wide, axis=-1, keepdims=True) + epsilon)
    return wide * inverse, inverse


def pair_terms(scale, offset, texts, image_emb, slopes_ref, own):
    rows = image_emb.shape[0]
    total = jnp.zeros((1, rows), f32)
    step = 256
    for start in range(0, texts.shape[0], step):
        logits = (
            scale
            * lax.dot_general(
                texts[start : start + step, :],
                image_emb,
                (((1,), (1,)), ((), ())),
                preferred_element_type=f32,
            )
            + offset
        )
        shrunk = jnp.exp(-jnp.abs(logits))
        softplus = jnp.maximum(logits, 0.0) + jnp.log1p(shrunk)
        sigmoid = jnp.where(logits >= 0.0, 1.0, shrunk) / (1.0 + shrunk)
        if own and start == 0:
            text_ids = lax.broadcasted_iota(jnp.int32, logits.shape, 0)
            image_ids = lax.broadcasted_iota(jnp.int32, logits.shape, 1)
            match = (text_ids == image_ids).astype(f32)
            softplus = softplus - match * logits
            sigmoid = sigmoid - match
        slopes_ref[start : start + step, :] = sigmoid.astype(bf16)
        total = total + jnp.sum(softplus, axis=0, keepdims=True)
    return total


def image_sums(slopes_ref, texts_ref):
    return lax.dot_general(
        slopes_ref[...], texts_ref[...], (((0,), (0,)), ((), ())), preferred_element_type=f32
    )


def own_kernel(count, scale_ref, bias_ref, image_ref, *refs):
    raw_refs = refs[:count]
    texts_ref, slopes_ref, emb_ref, grad_ref, loss_ref = refs[count:]
    rows = image_ref.shape[0]
    for place, raw in enumerate(raw_refs):
        texts_ref[place * rows : (place + 1) * rows, :] = unit_of(raw[...])[0].astype(bf16)
    emb_ref[...] = unit_of(image_ref[...])[0].astype(bf16)
    loss_ref[...] = pair_terms(
        scale_ref[0], bias_ref[0], texts_ref, emb_ref[...], slopes_ref, True
    )
    grad_ref[...] = image_sums(slopes_ref, texts_ref)


def peer_kernel(scale_ref, bias_ref, image_ref, texts_ref, slopes_ref, emb_ref, sent_ref):
    rows, width = image_ref.shape
    emb_ref[...] = unit_of(image_ref[...])[0].astype(bf16)
    loss = pair_terms(scale_ref[0], bias_ref[0], texts_ref, emb_ref[...], slopes_ref, False)
    sums = image_sums(slopes_ref, texts_ref)
    for panel in range(width // lanes):
        sent_ref[panel * rows : (panel + 1) * rows, :] = sums[
            :, panel * lanes : (panel + 1) * lanes
        ].astype(bf16)
    high = loss.astype(bf16).astype(f32)
    which = lax.broadcasted_iota(jnp.int32, (extra, rows), 0)
    sent_ref[width // lanes * rows :, :] = jnp.where(which == 0, high, loss - high).astype(bf16)


def text_sums(slopes, embs, place, rows):
    left = jnp.concatenate([s[place * rows : (place + 1) * rows, :] for s in slopes], axis=1)
    return jnp.dot(left, embs, preferred_element_type=f32)


def other_core_kernel(count, *refs):
    slopes, emb_refs, sent_ref = refs[:count], refs[count : 2 * count], refs[2 * count]
    rows = emb_refs[0].shape[0]
    embs = jnp.concatenate([e[...] for e in emb_refs], axis=0)
    for k in range(slopes[0].shape[0] // rows // 2):
        sent_ref[k * rows : (k + 1) * rows, :] = text_sums(slopes, embs, 2 * k + 1, rows).astype(bf16)


def own_core_kernel(count, received_ref, *refs):
    slopes, emb_refs = refs[:count], refs[count : 2 * count]
    own_ref, sent_refs = refs[2 * count], refs[2 * count + 1 :]
    rows = emb_refs[0].shape[0]
    embs = jnp.concatenate([e[...] for e in emb_refs], axis=0)
    for k, out in enumerate((own_ref, *sent_refs)):
        sums = text_sums(slopes, embs, 2 * k, rows) + received_ref[k * rows : (k + 1) * rows, :].astype(f32)
        out[...] = sums.astype(out.dtype)


def row_gradient(rows, sums, scale, out_ref):
    unit_rows, inverse = unit_of(rows)
    unit_grad = scale * sums
    out_ref[...] = (
        unit_grad - unit_rows * jnp.sum(unit_rows * unit_grad, axis=-1, keepdims=True)
    ) * inverse


def image_end_kernel(batch, scale_ref, image_ref, grad_ref, loss_ref, *refs):
    received, out_ref, out_loss_ref, sums_ref = refs[:-3], refs[-3], refs[-2], refs[-1]
    rows, width = image_ref.shape
    for panel in range(width // lanes):
        cut = slice(panel * lanes, (panel + 1) * lanes)
        sums = grad_ref[:, cut]
        for r in received:
            sums = sums + r[panel * rows : (panel + 1) * rows, :].astype(f32)
        sums_ref[:, cut] = sums
    loss = loss_ref[...]
    for r in received:
        tail = r[width // lanes * rows :, :].astype(f32)
        loss = loss + (tail[0:1, :] + tail[1:2, :])
    row_gradient(image_ref[...], sums_ref[...], scale_ref[0], out_ref)
    out_loss_ref[...] = loss / batch


def text_end_kernel(scale_ref, text_ref, grad_ref, *refs):
    received, out_ref = refs[:-1], refs[-1]
    sums = grad_ref[...]
    for r in received:
        sums = sums + r[...].astype(f32)
    row_gradient(text_ref[...], sums, scale_ref[0], out_ref)


def body(image, text, logarithm_scale, bias):
    rows, width = image.shape
    dp_count, inner_count = lax.axis_size("dp"), lax.axis_size("inner")
    batch = rows * dp_count * inner_count
    texts_held = rows * dp_count
    scale = jnp.exp(logarithm_scale)
    block = shape((rows, width), bf16)
    block_flops = 2 * rows * texts_held * width

    images = {r: swapped(image, "inner", r) for r in reversed(range(1, inner_count))}
    texts = [text, swapped(text, "dp", 1)]
    for s in range(2, dp_count, 2):
        fetched = swapped(text, "dp", s)
        texts += [fetched, swapped(fetched, "dp", 1)]

    text_embs, slopes, emb, image_grad, loss = call(
        functools.partial(own_kernel, dp_count),
        (
            shape((texts_held, width), bf16),
            shape((texts_held, rows), bf16),
            block,
            shape((rows, width), f32),
            shape((1, rows), f32),
        ),
        scale,
        bias,
        image,
        *texts,
        flops=2 * block_flops,
        in_specs=[SMEM, SMEM] + [VMEM] * (1 + dp_count),
    )
    all_slopes, embs, image_parts = [slopes], [emb], []
    for r, peer_image in images.items():
        slopes, emb, sent = call(
            peer_kernel,
            (
                shape((texts_held, rows), bf16),
                block,
                shape((width // lanes * rows + extra, lanes), bf16),
            ),
            scale,
            bias,
            peer_image,
            text_embs,
            flops=2 * block_flops,
            in_specs=[SMEM, SMEM, VMEM, VMEM],
        )
        all_slopes.append(slopes)
        embs.append(emb)
        image_parts.append(swapped(sent, "inner", r))

    crossing = call(
        functools.partial(other_core_kernel, inner_count),
        shape((texts_held // 2, width), bf16),
        *all_slopes,
        *embs,
        flops=inner_count * block_flops // 2,
    )
    crossed = swapped(crossing, "dp", 1)
    text_grad, *text_sent = call(
        functools.partial(own_core_kernel, inner_count),
        (shape((rows, width), f32),) + (block,) * (dp_count // 2 - 1),
        crossed,
        *all_slopes,
        *embs,
        flops=inner_count * block_flops // 2,
    )
    text_parts = [swapped(part, "dp", 2 * k + 2) for k, part in enumerate(text_sent)]

    image_gradient, image_loss = pl.pallas_call(
        functools.partial(image_end_kernel, batch),
        out_shape=(shape((rows, width), f32), shape((1, rows), f32)),
        in_specs=[SMEM] + [VMEM] * (3 + len(image_parts)),
        out_specs=(VMEM, VMEM),
        scratch_shapes=[pltpu.VMEM((rows, width), f32)],
        compiler_params=pltpu.CompilerParams(vmem_limit_bytes=40 * 1024 * 1024),
    )(scale, image, image_grad, loss, *image_parts)
    text_gradient = call(
        text_end_kernel,
        shape((rows, width), f32),
        scale,
        text,
        text_grad,
        *text_parts,
        in_specs=[SMEM] + [VMEM] * (2 + len(text_parts)),
    )
    return (image_gradient, text_gradient, image_loss.reshape(rows))


def solution(mesh):
    return jax.shard_map(
        body,
        mesh=mesh,
        in_specs=(P(("dp", "inner"), None), P(("dp", "inner"), None), P(), P()),
        out_specs=(P(("dp", "inner"), None), P(("dp", "inner"), None), P(("dp", "inner"))),
        check_vma=False,
    )
```

```python
import functools

import jax
import jax.numpy as jnp
from jax import lax
from jax.experimental import pallas as pl
from jax.experimental.pallas import tpu as pltpu
from jax.sharding import PartitionSpec as P

epsilon = 1e-06
f32, bf16 = jnp.float32, jnp.bfloat16
lanes = 128
extra = 16
direct_panels = 5
VMEM = pl.BlockSpec(memory_space=pltpu.VMEM)
SMEM = pl.BlockSpec(memory_space=pltpu.SMEM)


def swapped(value, axis, step):
    return lax.ppermute(value, axis, [(place, place ^ step) for place in range(lax.axis_size(axis))])


def swapped_both(value, dp_step, inner_step):
    dp_count, inner_count = lax.axis_size("dp"), lax.axis_size("inner")
    pairs = [
        (d * inner_count + i, (d ^ dp_step) * inner_count + (i ^ inner_step))
        for d in range(dp_count)
        for i in range(inner_count)
    ]
    return lax.ppermute(value, ("dp", "inner"), pairs)


def call(kernel, out_shape, *operands, flops=0, scalars=0, scratch=()):
    moved = sum(o.size * o.dtype.itemsize for o in operands)
    moved += sum(o.size * o.dtype.itemsize for o in jax.tree.leaves(out_shape))
    return pl.pallas_call(
        kernel,
        out_shape=out_shape,
        in_specs=[SMEM] * scalars + [VMEM] * (len(operands) - scalars),
        out_specs=jax.tree.map(lambda _: VMEM, out_shape),
        scratch_shapes=scratch,
        compiler_params=pltpu.CompilerParams(vmem_limit_bytes=40 * 1024 * 1024),
        cost_estimate=pl.CostEstimate(flops=flops, bytes_accessed=moved, transcendentals=0),
    )(*operands)


def shape(dims, kind):
    return jax.ShapeDtypeStruct(dims, kind)


def unit_of(rows):
    wide = rows.astype(f32)
    inverse = lax.rsqrt(jnp.sum(wide * wide, axis=-1, keepdims=True) + epsilon)
    return wide * inverse, inverse


def pair_terms(scale, offset, texts, image_emb, slopes_ref, own):
    rows = image_emb.shape[0]
    total = jnp.zeros((1, rows), f32)
    step = 256
    for start in range(0, texts.shape[0], step):
        logits = (
            scale
            * lax.dot_general(
                texts[start : start + step, :],
                image_emb,
                (((1,), (1,)), ((), ())),
                preferred_element_type=f32,
            )
            + offset
        )
        shrunk = jnp.exp(-jnp.abs(logits))
        softplus = jnp.maximum(logits, 0.0) + jnp.log1p(shrunk)
        sigmoid = jnp.where(logits >= 0.0, 1.0, shrunk) / (1.0 + shrunk)
        if own and start == 0:
            text_ids = lax.broadcasted_iota(jnp.int32, logits.shape, 0)
            image_ids = lax.broadcasted_iota(jnp.int32, logits.shape, 1)
            match = (text_ids == image_ids).astype(f32)
            softplus = softplus - match * logits
            sigmoid = sigmoid - match
        slopes_ref[start : start + step, :] = sigmoid.astype(bf16)
        total = total + jnp.sum(softplus, axis=0, keepdims=True)
    return total


def image_sums(slopes_ref, texts_ref):
    return lax.dot_general(
        slopes_ref[...], texts_ref[...], (((0,), (0,)), ((), ())), preferred_element_type=f32
    )


def texts_kernel(*refs):
    out_ref, rows = refs[-1], refs[0].shape[0]
    for place, raw in enumerate(refs[:-1]):
        out_ref[place * rows : (place + 1) * rows, :] = unit_of(raw[...])[0].astype(bf16)


def own_kernel(scale_ref, bias_ref, image_ref, texts_ref, slopes_ref, emb_ref, grad_ref, loss_ref):
    emb_ref[...] = unit_of(image_ref[...])[0].astype(bf16)
    loss_ref[...] = pair_terms(
        scale_ref[0], bias_ref[0], texts_ref, emb_ref[...], slopes_ref, True
    )
    grad_ref[...] = image_sums(slopes_ref, texts_ref)


def peer_kernel(scale_ref, bias_ref, image_ref, texts_ref, slopes_ref, emb_ref, head_ref, tail_ref):
    rows = image_ref.shape[0]
    panels = (head_ref.shape[0] - extra) // rows
    emb_ref[...] = unit_of(image_ref[...])[0].astype(bf16)
    loss = pair_terms(scale_ref[0], bias_ref[0], texts_ref, emb_ref[...], slopes_ref, False)
    sums = image_sums(slopes_ref, texts_ref)
    for panel in range(panels):
        head_ref[panel * rows : (panel + 1) * rows, :] = sums[
            :, panel * lanes : (panel + 1) * lanes
        ].astype(bf16)
    tail_ref[...] = sums[:, panels * lanes :].astype(tail_ref.dtype)
    high = loss.astype(bf16).astype(f32)
    which = lax.broadcasted_iota(jnp.int32, (extra, rows), 0)
    head_ref[panels * rows :, :] = jnp.where(which == 0, high, loss - high).astype(bf16)


def text_sums(slopes, embs, place, rows):
    left = jnp.concatenate([s[place * rows : (place + 1) * rows, :] for s in slopes], axis=1)
    return jnp.dot(left, embs, preferred_element_type=f32)


def other_core_kernel(count, *refs):
    slopes, emb_refs, sent_ref = refs[:count], refs[count : 2 * count], refs[2 * count]
    rows = emb_refs[0].shape[0]
    embs = jnp.concatenate([e[...] for e in emb_refs], axis=0)
    for k in range(slopes[0].shape[0] // rows // 2):
        sent_ref[k * rows : (k + 1) * rows, :] = text_sums(slopes, embs, 2 * k + 1, rows).astype(bf16)


def own_core_kernel(count, received_ref, *refs):
    slopes, emb_refs = refs[:count], refs[count : 2 * count]
    rows = emb_refs[0].shape[0]
    embs = jnp.concatenate([e[...] for e in emb_refs], axis=0)
    for k, out in enumerate(refs[2 * count :]):
        sums = text_sums(slopes, embs, 2 * k, rows) + received_ref[k * rows : (k + 1) * rows, :].astype(f32)
        out[...] = sums.astype(out.dtype)


def add_kernel(*refs):
    total = refs[0][...].astype(f32)
    for part in refs[1:-1]:
        total = total + part[...].astype(f32)
    refs[-1][...] = total.astype(refs[-1].dtype)


def row_gradient(rows, sums, scale, out_ref):
    unit_rows, inverse = unit_of(rows)
    unit_grad = scale * sums
    out_ref[...] = (
        unit_grad - unit_rows * jnp.sum(unit_rows * unit_grad, axis=-1, keepdims=True)
    ) * inverse


def image_end_kernel(batch, heads, scale_ref, image_ref, grad_ref, loss_ref, *refs):
    out_ref, out_loss_ref, sums_ref = refs[-3:]
    head_refs, tail_refs = refs[:heads], refs[heads:-3]
    rows = image_ref.shape[0]
    panels = (head_refs[0].shape[0] - extra) // rows
    loss = loss_ref[...]
    for panel in range(panels):
        cut = slice(panel * lanes, (panel + 1) * lanes)
        sums = grad_ref[:, cut]
        for r in head_refs:
            sums = sums + r[panel * rows : (panel + 1) * rows, :].astype(f32)
        sums_ref[:, cut] = sums
    for r in head_refs:
        last = r[panels * rows :, :].astype(f32)
        loss = loss + (last[0:1, :] + last[1:2, :])
    sums = grad_ref[:, panels * lanes :]
    for r in tail_refs:
        sums = sums + r[...].astype(f32)
    sums_ref[:, panels * lanes :] = sums
    row_gradient(image_ref[...], sums_ref[...], scale_ref[0], out_ref)
    out_loss_ref[...] = loss / batch


def text_end_kernel(scale_ref, text_ref, grad_ref, *refs):
    sums = grad_ref[...]
    for r in refs[:-1]:
        sums = sums + r[...].astype(f32)
    row_gradient(text_ref[...], sums, scale_ref[0], refs[-1])


def body(image, text, logarithm_scale, bias):
    rows, width = image.shape
    dp_count, inner_count = lax.axis_size("dp"), lax.axis_size("inner")
    batch = rows * dp_count * inner_count
    scale = jnp.exp(logarithm_scale)
    block = shape((rows, width), bf16)
    wide_block = shape((rows, width), f32)

    text_dp, text_inner = (0, 2), (0, 1)
    image_dp, image_inner = range(0, dp_count, 4), range(0, inner_count, 2)

    image_near = {q: swapped(image, "inner", q) if q else image for q in image_inner}
    text_near = {q: swapped(text, "inner", q) if q else text for q in text_inner}
    texts = []
    for q in text_inner:
        for p in text_dp:
            fetched = swapped(text_near[q], "dp", p) if p else text_near[q]
            texts += [fetched, swapped(fetched, "dp", 1)]
    images = {
        (p, q): swapped(image_near[q], "dp", p) if p else image_near[q]
        for q in image_inner
        for p in image_dp
    }

    texts_held = rows * len(texts)
    block_flops = 2 * rows * texts_held * width
    text_embs = call(texts_kernel, shape((texts_held, width), bf16), *texts, flops=block_flops // 3)
    slopes, embs, heads, tails = {}, {}, {}, {}
    head_rows = direct_panels * rows + extra
    tail_width = width - direct_panels * lanes
    for place in sorted(images, key=lambda place: (place[0] and place[1], place[0], -place[1])):
        p, q = place
        if p or q:
            slopes[place], embs[place], heads[place], tails[place] = call(
                peer_kernel,
                (
                    shape((texts_held, rows), bf16),
                    block,
                    shape((head_rows, lanes), bf16),
                    shape((rows, tail_width), bf16 if p else f32),
                ),
                scale,
                bias,
                images[place],
                text_embs,
                flops=2 * block_flops,
                scalars=2,
            )
        else:
            slopes[place], embs[place], image_grad, loss = call(
                own_kernel,
                (shape((texts_held, rows), bf16), block, wide_block, shape((1, rows), f32)),
                scale,
                bias,
                image,
                text_embs,
                flops=2 * block_flops,
                scalars=2,
            )

    head_parts = [
        swapped_both(heads[p, q], p, q) if p and q else swapped(heads[p, q], *(("dp", p) if p else ("inner", q)))
        for p, q in heads
    ]
    tail_parts = []
    for q in image_inner:
        moved = [swapped(tails[p, q], "dp", p) for p in image_dp if p]
        if q:
            summed = call(add_kernel, shape((rows, tail_width), bf16), tails[0, q], *moved)
            moved = [swapped(summed, "inner", q)]
        tail_parts += moved

    ordered = sorted(slopes)
    pieces = [slopes[place] for place in ordered] + [embs[place] for place in ordered]
    crossing = call(
        functools.partial(other_core_kernel, len(ordered)),
        shape((texts_held // 2, width), bf16),
        *pieces,
        flops=len(ordered) * block_flops // 2,
    )
    crossed = swapped(crossing, "dp", 1)
    text_grad, *text_sent = call(
        functools.partial(own_core_kernel, len(ordered)),
        (wide_block,) + (block,) * (len(texts) // 2 - 1),
        crossed,
        *pieces,
        flops=len(ordered) * block_flops // 2,
    )
    text_places = [(p, q) for q in text_inner for p in text_dp][1:]
    text_parts = [
        swapped_both(part, p, q) if p and q else swapped(part, *(("dp", p) if p else ("inner", q)))
        for part, (p, q) in zip(text_sent, text_places)
    ]

    image_gradient, image_loss = call(
        functools.partial(image_end_kernel, batch, len(head_parts)),
        (wide_block, shape((1, rows), f32)),
        scale,
        image,
        image_grad,
        loss,
        *head_parts,
        *tail_parts,
        scalars=1,
        scratch=[pltpu.VMEM((rows, width), f32)],
    )
    text_gradient = call(text_end_kernel, wide_block, scale, text, text_grad, *text_parts, scalars=1)
    return (image_gradient, text_gradient, image_loss.reshape(rows))


def solution(mesh):
    return jax.shard_map(
        body,
        mesh=mesh,
        in_specs=(P(("dp", "inner"), None), P(("dp", "inner"), None), P(), P()),
        out_specs=(P(("dp", "inner"), None), P(("dp", "inner"), None), P(("dp", "inner"))),
        check_vma=False,
    )
```

```python
import functools

import jax
import jax.numpy as jnp
from jax import lax
from jax.experimental import pallas as pl
from jax.experimental.pallas import tpu as pltpu
from jax.sharding import PartitionSpec as P

epsilon = 1e-06
f32, bf16 = jnp.float32, jnp.bfloat16
lanes = 128
extra = 16
direct_panels = 5
VMEM = pl.BlockSpec(memory_space=pltpu.VMEM)
SMEM = pl.BlockSpec(memory_space=pltpu.SMEM)
ANY = pl.BlockSpec(memory_space=pl.ANY)


def swapped(value, axis, step):
    return lax.ppermute(value, axis, [(place, place ^ step) for place in range(lax.axis_size(axis))])


def swapped_both(value, dp_step, inner_step):
    dp_count, inner_count = lax.axis_size("dp"), lax.axis_size("inner")
    pairs = [
        (d * inner_count + i, (d ^ dp_step) * inner_count + (i ^ inner_step))
        for d in range(dp_count)
        for i in range(inner_count)
    ]
    return lax.ppermute(value, ("dp", "inner"), pairs)


def call(kernel, out_shape, *operands, flops=0, scalars=0, scratch=(), after=()):
    moved = sum(o.size * o.dtype.itemsize for o in operands)
    moved += sum(o.size * o.dtype.itemsize for o in jax.tree.leaves(out_shape))
    body_of = kernel
    if after:
        body_of = lambda *refs: kernel(*refs[len(after) :])
    return pl.pallas_call(
        body_of,
        out_shape=out_shape,
        in_specs=[ANY] * len(after) + [SMEM] * scalars + [VMEM] * (len(operands) - scalars),
        out_specs=jax.tree.map(lambda _: VMEM, out_shape),
        scratch_shapes=scratch,
        compiler_params=pltpu.CompilerParams(vmem_limit_bytes=40 * 1024 * 1024),
        cost_estimate=pl.CostEstimate(flops=flops, bytes_accessed=moved, transcendentals=0),
    )(*after, *operands)


def shape(dims, kind):
    return jax.ShapeDtypeStruct(dims, kind)


def unit_of(rows):
    wide = rows.astype(f32)
    inverse = lax.rsqrt(jnp.sum(wide * wide, axis=-1, keepdims=True) + epsilon)
    return wide * inverse, inverse


def pair_terms(scale, offset, text_refs, image_emb, slopes_ref, own):
    rows = image_emb.shape[0]
    total = jnp.zeros((1, rows), f32)
    step = 256
    done = 0
    for texts in text_refs:
        for start in range(0, texts.shape[0], step):
            chunk = texts[start : min(start + step, texts.shape[0]), :]
            logits = (
                scale
                * lax.dot_general(
                    chunk, image_emb, (((1,), (1,)), ((), ())), preferred_element_type=f32
                )
                + offset
            )
            shrunk = jnp.exp(-jnp.abs(logits))
            softplus = jnp.maximum(logits, 0.0) + jnp.log1p(shrunk)
            sigmoid = jnp.where(logits >= 0.0, 1.0, shrunk) / (1.0 + shrunk)
            if own and done == 0:
                text_ids = lax.broadcasted_iota(jnp.int32, logits.shape, 0)
                image_ids = lax.broadcasted_iota(jnp.int32, logits.shape, 1)
                match = (text_ids == image_ids).astype(f32)
                softplus = softplus - match * logits
                sigmoid = sigmoid - match
            slopes_ref[done : done + chunk.shape[0], :] = sigmoid.astype(bf16)
            total = total + jnp.sum(softplus, axis=0, keepdims=True)
            done += chunk.shape[0]
    return total


def image_sums(slopes_ref, text_refs):
    total, done = None, 0
    for texts in text_refs:
        count = texts.shape[0]
        part = lax.dot_general(
            slopes_ref[done : done + count, :],
            texts[...],
            (((0,), (0,)), ((), ())),
            preferred_element_type=f32,
        )
        total, done = part if total is None else total + part, done + count
    return total


def stage_kernel(fetched, *refs):
    text_refs, image_ref = refs[: 2 + fetched], refs[2 + fetched]
    out_ref, half_ref, forward_refs = refs[3 + fetched], refs[4 + fetched], refs[5 + fetched :]
    rows = image_ref.shape[0]
    for place, raw in enumerate(text_refs):
        emb = unit_of(raw[...])[0].astype(bf16)
        out_ref[place * rows : (place + 1) * rows, :] = emb
        if place >= 2:
            forward_refs[place - 2][...] = emb
    half_ref[...] = unit_of(image_ref[rows // 2 :, :])[0].astype(bf16)


def own_kernel(scale_ref, bias_ref, image_ref, *refs):
    text_refs, (slopes_ref, emb_ref, grad_ref, loss_ref) = refs[:-4], refs[-4:]
    emb_ref[...] = unit_of(image_ref[...])[0].astype(bf16)
    loss_ref[...] = pair_terms(
        scale_ref[0], bias_ref[0], text_refs, emb_ref[...], slopes_ref, True
    )
    grad_ref[...] = image_sums(slopes_ref, text_refs)


def peer_kernel(texts, halves, scale_ref, bias_ref, *refs):
    text_refs, image_refs = refs[:texts], refs[texts : texts + (2 if halves else 1)]
    slopes_ref, emb_ref, head_ref, *tail_ref = refs[texts + len(image_refs) :]
    rows = emb_ref.shape[0]
    panels = (head_ref.shape[0] - extra) // rows
    if halves:
        emb_ref[: rows // 2, :] = unit_of(image_refs[0][...])[0].astype(bf16)
        emb_ref[rows // 2 :, :] = image_refs[1][...]
    else:
        emb_ref[...] = unit_of(image_refs[0][...])[0].astype(bf16)
    loss = pair_terms(scale_ref[0], bias_ref[0], text_refs, emb_ref[...], slopes_ref, False)
    sums = image_sums(slopes_ref, text_refs)
    for panel in range(panels):
        head_ref[panel * rows : (panel + 1) * rows, :] = sums[
            :, panel * lanes : (panel + 1) * lanes
        ].astype(bf16)
    if tail_ref:
        tail_ref[0][...] = sums[:, panels * lanes :].astype(tail_ref[0].dtype)
    high = loss.astype(bf16).astype(f32)
    which = lax.broadcasted_iota(jnp.int32, (extra, rows), 0)
    head_ref[panels * rows :, :] = jnp.where(which == 0, high, loss - high).astype(bf16)


def text_sums(slopes, embs, place, rows):
    left = jnp.concatenate([s[place * rows : (place + 1) * rows, :] for s in slopes], axis=1)
    return jnp.dot(left, embs, preferred_element_type=f32)


def other_core_kernel(count, *refs):
    slopes, emb_refs, sent_ref = refs[:count], refs[count : 2 * count], refs[2 * count]
    rows = emb_refs[0].shape[0]
    embs = jnp.concatenate([e[...] for e in emb_refs], axis=0)
    places = slopes[0].shape[0] // rows // 2
    for k in range(places):
        sent_ref[k * rows : (k + 1) * rows, :] = text_sums(slopes, embs, places + k, rows).astype(bf16)


def own_core_kernel(count, received_ref, *refs):
    slopes, emb_refs = refs[:count], refs[count : 2 * count]
    rows = emb_refs[0].shape[0]
    embs = jnp.concatenate([e[...] for e in emb_refs], axis=0)
    for k, out in enumerate(refs[2 * count :]):
        sums = text_sums(slopes, embs, k, rows) + received_ref[k * rows : (k + 1) * rows, :].astype(f32)
        out[...] = sums.astype(out.dtype)


def late_kernel(sums, parts, *refs):
    payloads = (len(refs) - 2 * sums - sums * parts) // 2
    own, received = refs[:sums], refs[sums : sums + sums * parts]
    passed, outs = refs[sums + sums * parts :][:payloads], refs[sums + sums * parts + payloads :]
    for k in range(sums):
        total = own[k][...]
        for part in received[k * parts : (k + 1) * parts]:
            total = total + part[...].astype(f32)
        outs[k][...] = total.astype(bf16)
    for source, target in zip(passed, outs[sums:]):
        target[...] = source[...]


def row_gradient(rows, sums, scale, out_ref):
    unit_rows, inverse = unit_of(rows)
    unit_grad = scale * sums
    out_ref[...] = (
        unit_grad - unit_rows * jnp.sum(unit_rows * unit_grad, axis=-1, keepdims=True)
    ) * inverse


def image_end_kernel(batch, heads, scale_ref, image_ref, grad_ref, loss_ref, *refs):
    out_ref, out_loss_ref, sums_ref = refs[-3:]
    head_refs, tail_refs = refs[:heads], refs[heads:-3]
    rows, width = image_ref.shape
    loss = loss_ref[...]
    for panel in range(width // lanes):
        cut = slice(panel * lanes, (panel + 1) * lanes)
        sums = grad_ref[:, cut]
        for r in head_refs:
            if (panel + 1) * rows <= r.shape[0] - extra:
                sums = sums + r[panel * rows : (panel + 1) * rows, :].astype(f32)
        for r in tail_refs:
            first = panel * lanes - (width - r.shape[1])
            if first >= 0:
                sums = sums + r[:, first : first + lanes].astype(f32)
        sums_ref[:, cut] = sums
    for r in head_refs:
        last = r[r.shape[0] - extra :, :].astype(f32)
        loss = loss + (last[0:1, :] + last[1:2, :])
    row_gradient(image_ref[...], sums_ref[...], scale_ref[0], out_ref)
    out_loss_ref[...] = loss / batch


def text_end_kernel(scale_ref, text_ref, grad_ref, *refs):
    sums = grad_ref[...]
    for r in refs[:-1]:
        sums = sums + r[...].astype(f32)
    row_gradient(text_ref[...], sums, scale_ref[0], refs[-1])


def body(image, text, logarithm_scale, bias):
    rows, width = image.shape
    dp_count, inner_count = lax.axis_size("dp"), lax.axis_size("inner")
    batch = rows * dp_count * inner_count
    scale = jnp.exp(logarithm_scale)
    block = shape((rows, width), bf16)
    wide_block = shape((rows, width), f32)

    text_places = [(0, 0), (2, 0), (0, 1), (2, 1)]
    image_dp, image_inner = range(4, dp_count, 4), range(2, inner_count, 2)

    first_half = image[: rows // 2]
    halves = {q: swapped(first_half, "inner", q) for q in image_inner}
    text_z = swapped(text, "inner", 1)
    text_x = swapped(text, "dp", 2)
    images = {(p, 0): (swapped(image, "dp", p),) for p in image_dp}
    near_texts, second_half, text_z_emb = call(
        functools.partial(stage_kernel, 1),
        (shape((3 * rows, width), bf16), shape((rows // 2, width), bf16), block),
        text,
        text_x,
        text_z,
        image,
        after=[*halves.values(), *(i for (i,) in images.values())],
    )

    far_text = swapped(text_z_emb, "dp", 2)
    near_swapped = swapped(near_texts, "dp", 1)
    second_halves = {q: swapped(second_half, "inner", q) for q in image_inner}
    for q in image_inner:
        images[0, q] = (halves[q], second_halves[q])
        for p in image_dp:
            images[p, q] = (swapped(halves[q], "dp", p), swapped(second_halves[q], "dp", p))
    far_swapped = swapped(far_text, "dp", 1)
    texts = [near_texts, far_text, near_swapped, far_swapped]

    texts_held = 2 * len(text_places) * rows
    block_flops = 2 * rows * texts_held * width
    slopes, embs, heads, tails, whole = {}, {}, {}, {}, {}
    head_rows = direct_panels * rows + extra
    tail_width = width - direct_panels * lanes
    first = [images[p, q][0] for p in image_dp for q in image_inner]
    for q in image_inner:
        slopes[0, q], embs[0, q], heads[0, q], tails[0, q] = call(
            functools.partial(peer_kernel, len(texts), True),
            (
                shape((texts_held, rows), bf16),
                block,
                shape((head_rows, lanes), bf16),
                shape((rows, tail_width), f32),
            ),
            scale,
            bias,
            *texts,
            *images[0, q],
            flops=2 * block_flops,
            scalars=2,
            after=first,
        )
    first = [heads[0, q] for q in image_inner]
    for p in image_dp:
        slopes[p, 0], embs[p, 0], whole[p] = call(
            functools.partial(peer_kernel, len(texts), False),
            (
                shape((texts_held, rows), bf16),
                block,
                shape((width // lanes * rows + extra, lanes), bf16),
            ),
            scale,
            bias,
            *texts,
            *images[p, 0],
            flops=2 * block_flops,
            scalars=2,
            after=first,
        )
    slopes[0, 0], embs[0, 0], image_grad, loss = call(
        own_kernel,
        (shape((texts_held, rows), bf16), block, wide_block, shape((1, rows), f32)),
        scale,
        bias,
        image,
        *texts,
        flops=2 * block_flops,
        scalars=2,
        after=first,
    )
    for p in image_dp:
        for q in image_inner:
            slopes[p, q], embs[p, q], heads[p, q], tails[p, q] = call(
                functools.partial(peer_kernel, len(texts), True),
                (
                    shape((texts_held, rows), bf16),
                    block,
                    shape((head_rows, lanes), bf16),
                    shape((rows, tail_width), bf16),
                ),
                scale,
                bias,
                *texts,
                *images[p, q],
                flops=2 * block_flops,
                scalars=2,
                after=[image_grad],
            )

    near_heads = [swapped(heads[0, q], "inner", q) for q in image_inner]
    far_heads = [swapped_both(heads[p, q], p, q) for p in image_dp for q in image_inner]
    moved_tails = [swapped(tails[p, q], "dp", p) for q in image_inner for p in image_dp]
    late = call(
        functools.partial(late_kernel, len(image_inner), len(image_dp)),
        [shape((rows, tail_width), bf16)] * len(image_inner)
        + [shape(whole[p].shape, bf16) for p in image_dp],
        *(tails[0, q] for q in image_inner),
        *moved_tails,
        *whole.values(),
        after=near_heads,
    )
    tail_parts = [swapped(part, "inner", q) for part, q in zip(late, image_inner)]
    whole_parts = [swapped(part, "dp", p) for part, p in zip(late[len(image_inner) :], image_dp)]

    ordered = sorted(slopes)
    pieces = [slopes[place] for place in ordered] + [embs[place] for place in ordered]
    crossing = call(
        functools.partial(other_core_kernel, len(ordered)),
        shape((texts_held // 2, width), bf16),
        *pieces,
        flops=len(ordered) * block_flops // 2,
    )
    crossed = swapped(crossing, "dp", 1)
    text_grad, *text_sent = call(
        functools.partial(own_core_kernel, len(ordered)),
        (wide_block,) + (block,) * (len(text_places) - 1),
        crossed,
        *pieces,
        flops=len(ordered) * block_flops // 2,
    )
    text_parts = [
        swapped_both(part, p, q) if p and q else swapped(part, *(("dp", p) if p else ("inner", q)))
        for part, (p, q) in zip(text_sent, text_places[1:])
    ]

    head_parts = near_heads + far_heads + whole_parts
    image_gradient, image_loss = call(
        functools.partial(image_end_kernel, batch, len(head_parts)),
        (wide_block, shape((1, rows), f32)),
        scale,
        image,
        image_grad,
        loss,
        *head_parts,
        *tail_parts,
        scalars=1,
        scratch=[pltpu.VMEM((rows, width), f32)],
    )
    text_gradient = call(text_end_kernel, wide_block, scale, text, text_grad, *text_parts, scalars=1)
    return (image_gradient, text_gradient, image_loss.reshape(rows))


def solution(mesh):
    return jax.shard_map(
        body,
        mesh=mesh,
        in_specs=(P(("dp", "inner"), None), P(("dp", "inner"), None), P(), P()),
        out_specs=(P(("dp", "inner"), None), P(("dp", "inner"), None), P(("dp", "inner"))),
        check_vma=False,
    )
```

```python
import functools

import jax
import jax.numpy as jnp
from jax import lax
from jax.experimental import pallas as pl
from jax.experimental.pallas import tpu as pltpu
from jax.sharding import PartitionSpec as P

epsilon = 1e-06
f32, bf16 = jnp.float32, jnp.bfloat16
lanes = 128
extra = 16
direct_panels = 2
VMEM = pl.BlockSpec(memory_space=pltpu.VMEM)
SMEM = pl.BlockSpec(memory_space=pltpu.SMEM)
ANY = pl.BlockSpec(memory_space=pl.ANY)


def swapped(value, axis, step):
    return lax.ppermute(value, axis, [(place, place ^ step) for place in range(lax.axis_size(axis))])


def swapped_both(value, dp_step, inner_step):
    dp_count, inner_count = lax.axis_size("dp"), lax.axis_size("inner")
    pairs = [
        (d * inner_count + i, (d ^ dp_step) * inner_count + (i ^ inner_step))
        for d in range(dp_count)
        for i in range(inner_count)
    ]
    return lax.ppermute(value, ("dp", "inner"), pairs)


def call(kernel, out_shape, *operands, flops=0, scalars=0, scratch=(), after=()):
    moved = sum(o.size * o.dtype.itemsize for o in operands)
    moved += sum(o.size * o.dtype.itemsize for o in jax.tree.leaves(out_shape))
    body_of = kernel
    if after:
        body_of = lambda *refs: kernel(*refs[len(after) :])
    return pl.pallas_call(
        body_of,
        out_shape=out_shape,
        in_specs=[ANY] * len(after) + [SMEM] * scalars + [VMEM] * (len(operands) - scalars),
        out_specs=jax.tree.map(lambda _: VMEM, out_shape),
        scratch_shapes=scratch,
        compiler_params=pltpu.CompilerParams(vmem_limit_bytes=40 * 1024 * 1024),
        cost_estimate=pl.CostEstimate(flops=flops, bytes_accessed=moved, transcendentals=0),
    )(*after, *operands)


def shape(dims, kind):
    return jax.ShapeDtypeStruct(dims, kind)


def unit_of(rows):
    wide = rows.astype(f32)
    inverse = lax.rsqrt(jnp.sum(wide * wide, axis=-1, keepdims=True) + epsilon)
    return wide * inverse, inverse


def pair_terms(scale, offset, text_refs, images_ref, slopes_ref, own):
    step = 256
    totals = []
    for left in range(0, images_ref.shape[0], step):
        images = images_ref[left : left + step, :]
        total, done = jnp.zeros((1, images.shape[0]), f32), 0
        for texts in text_refs:
            for start in range(0, texts.shape[0], step):
                chunk = texts[start : min(start + step, texts.shape[0]), :]
                logits = (
                    scale
                    * lax.dot_general(
                        chunk, images, (((1,), (1,)), ((), ())), preferred_element_type=f32
                    )
                    + offset
                )
                shrunk = jnp.exp(-jnp.abs(logits))
                softplus = jnp.maximum(logits, 0.0) + jnp.log1p(shrunk)
                sigmoid = jnp.where(logits >= 0.0, 1.0, shrunk) / (1.0 + shrunk)
                if own and done == 0 and left == 0:
                    text_ids = lax.broadcasted_iota(jnp.int32, logits.shape, 0)
                    image_ids = lax.broadcasted_iota(jnp.int32, logits.shape, 1)
                    match = ((text_ids == image_ids) & (text_ids < own)).astype(f32)
                    softplus = softplus - match * logits
                    sigmoid = sigmoid - match
                slopes_ref[done : done + chunk.shape[0], left : left + step] = sigmoid.astype(bf16)
                total = total + jnp.sum(softplus, axis=0, keepdims=True)
                done += chunk.shape[0]
        totals.append(total)
    return jnp.concatenate(totals, axis=1)


def own_rows_kernel(text_ref, image_ref, text_emb_ref, image_emb_ref):
    text_emb_ref[...] = unit_of(text_ref[...])[0].astype(bf16)
    image_emb_ref[...] = unit_of(image_ref[...])[0].astype(bf16)


def first_stage_kernel(own_ref, beside_ref, above_ref, *refs):
    count = (len(refs) - 2) // 2
    raw_refs, texts_ref, above_emb_ref, emb_refs = refs[:count], refs[count], refs[count + 1], refs[count + 2 :]
    rows = own_ref.shape[0]
    texts_ref[:rows, :] = own_ref[...]
    texts_ref[rows : 2 * rows, :] = unit_of(beside_ref[...])[0].astype(bf16)
    above = unit_of(above_ref[...])[0].astype(bf16)
    texts_ref[2 * rows :, :] = above
    above_emb_ref[...] = above
    for raw, emb in zip(raw_refs, emb_refs):
        emb[...] = unit_of(raw[...])[0].astype(bf16)


def copy_kernel(source_ref, target_ref):
    target_ref[...] = source_ref[...]


def own_core_pairs_kernel(scale_ref, bias_ref, near_ref, far_ref, *refs):
    image_refs, (images_ref, slopes_ref, loss_ref) = refs[:-3], refs[-3:]
    rows = far_ref.shape[0]
    for place, block in enumerate(image_refs):
        images_ref[place * rows : (place + 1) * rows, :] = block[...]
    loss_ref[...] = pair_terms(
        scale_ref[0], bias_ref[0], (near_ref, far_ref), images_ref, slopes_ref, rows
    )


def other_core_pairs_kernel(
    scale_ref, bias_ref, near_ref, far_ref, images_ref, first_loss_ref, slopes_ref, loss_ref, sent_ref
):
    loss_ref[...] = first_loss_ref[...] + pair_terms(
        scale_ref[0], bias_ref[0], (near_ref, far_ref), images_ref, slopes_ref, 0
    )
    sent_ref[...] = jnp.dot(slopes_ref[...], images_ref[...], preferred_element_type=f32).astype(bf16)


def loss_rows(loss):
    high = loss.astype(bf16).astype(f32)
    which = lax.broadcasted_iota(jnp.int32, (extra, loss.shape[1]), 0)
    return jnp.where(which == 0, high, loss - high).astype(bf16)


def image_sums_kernel(plain, loss_ref, *refs):
    slope_refs, text_refs, refs = refs[:2], refs[2:6], refs[6:]
    own_ref, own_loss_ref, plain_refs, head_refs, tail_refs = (
        refs[0],
        refs[1],
        refs[2 : 2 + plain],
        refs[2 + plain :: 2],
        refs[3 + plain :: 2],
    )
    rows, width = own_ref.shape
    step = 3 * lanes
    for left in range(0, width, step):
        total = None
        for slopes, texts in zip(slope_refs, (text_refs[:2], text_refs[2:])):
            done = 0
            for block in texts:
                part = lax.dot_general(
                    slopes[done : done + block.shape[0], :],
                    block[:, left : left + step],
                    (((0,), (0,)), ((), ())),
                    preferred_element_type=f32,
                )
                total, done = part if total is None else total + part, done + block.shape[0]
        own_ref[:, left : left + step] = total[:rows, :]
        for place, out in enumerate((*plain_refs, *head_refs), 1):
            panels = (out.shape[0] - extra) // rows
            sums = total[place * rows : (place + 1) * rows, :]
            for at in range(left, left + step, lanes):
                piece = sums[:, at - left : at - left + lanes]
                if at < panels * lanes:
                    out[at // lanes * rows : (at // lanes + 1) * rows, :] = piece.astype(bf16)
                else:
                    tail = tail_refs[place - 1 - plain]
                    tail[:, at - panels * lanes : at - panels * lanes + lanes] = piece.astype(tail.dtype)
    own_loss_ref[...] = loss_ref[:, :rows]
    for place, out in enumerate((*plain_refs, *head_refs), 1):
        out[out.shape[0] - extra :, :] = loss_rows(loss_ref[:, place * rows : (place + 1) * rows])


def text_sums_kernel(received_ref, slopes_ref, images_ref, *outs):
    rows = outs[0].shape[0]
    for k, out in enumerate(outs):
        cut = slice(k * rows, (k + 1) * rows)
        sums = jnp.dot(slopes_ref[cut, :], images_ref[...], preferred_element_type=f32)
        out[...] = (sums + received_ref[cut, :].astype(f32)).astype(out.dtype)


def late_kernel(sums, parts, *refs):
    payloads = (len(refs) - 2 * sums - sums * parts) // 2
    own, received = refs[:sums], refs[sums : sums + sums * parts]
    passed, outs = refs[sums + sums * parts :][:payloads], refs[sums + sums * parts + payloads :]
    for k in range(sums):
        total = own[k][...]
        for part in received[k * parts : (k + 1) * parts]:
            total = total + part[...].astype(f32)
        outs[k][...] = total.astype(bf16)
    for source, target in zip(passed, outs[sums:]):
        target[...] = source[...]


def row_gradient(rows, sums, scale, out_ref):
    unit_rows, inverse = unit_of(rows)
    unit_grad = scale * sums
    out_ref[...] = (
        unit_grad - unit_rows * jnp.sum(unit_rows * unit_grad, axis=-1, keepdims=True)
    ) * inverse


def image_end_kernel(batch, heads, scale_ref, image_ref, grad_ref, loss_ref, *refs):
    out_ref, out_loss_ref, sums_ref = refs[-3:]
    head_refs, tail_refs = refs[:heads], refs[heads:-3]
    rows, width = image_ref.shape
    loss = loss_ref[...]
    for panel in range(width // lanes):
        cut = slice(panel * lanes, (panel + 1) * lanes)
        sums = grad_ref[:, cut]
        for r in head_refs:
            if (panel + 1) * rows <= r.shape[0] - extra:
                sums = sums + r[panel * rows : (panel + 1) * rows, :].astype(f32)
        for r in tail_refs:
            first = panel * lanes - (width - r.shape[1])
            if first >= 0:
                sums = sums + r[:, first : first + lanes].astype(f32)
        sums_ref[:, cut] = sums
    for r in head_refs:
        last = r[r.shape[0] - extra :, :].astype(f32)
        loss = loss + (last[0:1, :] + last[1:2, :])
    row_gradient(image_ref[...], sums_ref[...], scale_ref[0], out_ref)
    out_loss_ref[...] = loss / batch


def text_end_kernel(scale_ref, text_ref, grad_ref, *refs):
    sums = grad_ref[...]
    for r in refs[:-1]:
        sums = sums + r[...].astype(f32)
    row_gradient(text_ref[...], sums, scale_ref[0], refs[-1])


def body(image, text, logarithm_scale, bias):
    rows, width = image.shape
    dp_count, inner_count = lax.axis_size("dp"), lax.axis_size("inner")
    batch = rows * dp_count * inner_count
    scale = jnp.exp(logarithm_scale)
    block = shape((rows, width), bf16)
    wide_block = shape((rows, width), f32)

    image_dp, image_inner = range(4, dp_count, 4), range(2, inner_count, 2)

    images_z = [swapped(image, "inner", q) for q in image_inner]
    text_z = swapped(text, "inner", 1)
    text_x = swapped(text, "dp", 2)
    images_y = [swapped(image, "dp", p) for p in image_dp]
    text_emb, image_emb = call(own_rows_kernel, (block, block), text, image)
    near_texts, text_z_emb, *embs = call(
        first_stage_kernel,
        (shape((3 * rows, width), bf16), block) + (block,) * (len(images_y) + len(images_z)),
        text_emb,
        text_x,
        text_z,
        *images_y,
        *images_z,
    )
    embs_y, embs_z = embs[: len(images_y)], embs[len(images_y) :]

    far_text = swapped(text_z_emb, "dp", 2)
    embs_yz = [swapped(emb, "dp", p) for emb in embs_z for p in image_dp]
    near_swapped = swapped(near_texts, "dp", 1)
    far_text = call(copy_kernel, block, far_text, after=embs_yz)
    far_swapped = swapped(far_text, "dp", 1)

    embs = [image_emb, *embs_y, *embs_z, *embs_yz]
    held, texts_half = len(embs) * rows, 4 * rows
    slopes_shape = shape((texts_half, held), bf16)
    pair_flops = 2 * held * texts_half * width
    images, own_core_slopes, loss = call(
        own_core_pairs_kernel,
        (shape((held, width), bf16), slopes_shape, shape((1, held), f32)),
        scale,
        bias,
        near_texts,
        far_text,
        *embs,
        flops=pair_flops,
        scalars=2,
    )
    other_core_slopes, loss, crossing = call(
        other_core_pairs_kernel,
        (slopes_shape, shape((1, held), f32), shape((texts_half, width), bf16)),
        scale,
        bias,
        near_swapped,
        far_swapped,
        images,
        loss,
        flops=2 * pair_flops,
        scalars=2,
    )
    crossed = swapped(crossing, "dp", 1)

    head_rows = direct_panels * rows + extra
    tail_width = width - direct_panels * lanes
    out_shapes = [wide_block, shape((1, rows), f32)]
    out_shapes += [shape((width // lanes * rows + extra, lanes), bf16)] * len(embs_y)
    for kind, count in ((f32, len(embs_z)), (bf16, len(embs_yz))):
        out_shapes += [shape((head_rows, lanes), bf16), shape((rows, tail_width), kind)] * count
    image_grad, own_loss, *sent = call(
        functools.partial(image_sums_kernel, len(embs_y)),
        out_shapes,
        loss,
        own_core_slopes,
        other_core_slopes,
        near_texts,
        far_text,
        near_swapped,
        far_swapped,
        flops=2 * pair_flops,
    )
    payloads_y, heads, tails = sent[: len(embs_y)], sent[len(embs_y) :: 2], sent[len(embs_y) + 1 :: 2]

    moved_tails = [
        swapped(tail, "dp", p)
        for tail, p in zip(tails[len(embs_z) :], [p for _ in image_inner for p in image_dp])
    ]
    z_heads = [swapped(head, "inner", q) for head, q in zip(heads, image_inner)]
    yz_heads = [
        swapped_both(head, p, q)
        for head, (p, q) in zip(heads[len(embs_z) :], [(p, q) for q in image_inner for p in image_dp])
    ]
    text_grad, text_x_sums, text_z_sums, text_xz_sums = call(
        text_sums_kernel,
        (wide_block, block, wide_block, block),
        crossed,
        own_core_slopes,
        images,
        flops=pair_flops,
        after=[image_grad],
    )
    moved_text = swapped(text_xz_sums, "dp", 2)

    late = call(
        functools.partial(late_kernel, len(image_inner), len(image_dp)),
        [shape((rows, tail_width), bf16)] * len(image_inner) + [shape(p.shape, bf16) for p in payloads_y],
        *tails[: len(embs_z)],
        *moved_tails,
        *payloads_y,
        after=z_heads + yz_heads,
    )
    tail_parts = [swapped(part, "inner", q) for part, q in zip(late, image_inner)]
    y_parts = [swapped(part, "dp", p) for part, p in zip(late[len(image_inner) :], image_dp)]
    late_text_z, late_text_x = call(
        functools.partial(late_kernel, 1, 1), [block, block], text_z_sums, moved_text, text_x_sums
    )
    text_parts = [swapped(late_text_z, "inner", 1), swapped(late_text_x, "dp", 2)]

    head_parts = z_heads + yz_heads + y_parts
    image_gradient, image_loss = call(
        functools.partial(image_end_kernel, batch, len(head_parts)),
        (wide_block, shape((1, rows), f32)),
        scale,
        image,
        image_grad,
        own_loss,
        *head_parts,
        *tail_parts,
        scalars=1,
        scratch=[pltpu.VMEM((rows, width), f32)],
    )
    text_gradient = call(text_end_kernel, wide_block, scale, text, text_grad, *text_parts, scalars=1)
    return (image_gradient, text_gradient, image_loss.reshape(rows))


def solution(mesh):
    return jax.shard_map(
        body,
        mesh=mesh,
        in_specs=(P(("dp", "inner"), None), P(("dp", "inner"), None), P(), P()),
        out_specs=(P(("dp", "inner"), None), P(("dp", "inner"), None), P(("dp", "inner"))),
        check_vma=False,
    )
```

```python
import functools

import jax
import jax.numpy as jnp
from jax import lax
from jax.experimental import pallas as pl
from jax.experimental.pallas import tpu as pltpu
from jax.sharding import PartitionSpec as P

epsilon = 1e-06
f32, bf16 = jnp.float32, jnp.bfloat16
lanes = 128
extra = 16
direct_panels = 4
weights = {"z": 10, "p1": 10, "heads": 10, "late": 2, "far heads": 2, "end": 5, "text": 4}
VMEM = pl.BlockSpec(memory_space=pltpu.VMEM)
SMEM = pl.BlockSpec(memory_space=pltpu.SMEM)
ANY = pl.BlockSpec(memory_space=pl.ANY)


def swapped(value, axis, step):
    return lax.ppermute(value, axis, [(place, place ^ step) for place in range(lax.axis_size(axis))])


def swapped_both(value, dp_step, inner_step):
    dp_count, inner_count = lax.axis_size("dp"), lax.axis_size("inner")
    pairs = [
        (d * inner_count + i, (d ^ dp_step) * inner_count + (i ^ inner_step))
        for d in range(dp_count)
        for i in range(inner_count)
    ]
    return lax.ppermute(value, ("dp", "inner"), pairs)


def call(kernel, out_shape, *operands, flops=0, weight=0, scalars=0, scratch=(), after=()):
    moved = sum(o.size * o.dtype.itemsize for o in operands)
    moved += sum(o.size * o.dtype.itemsize for o in jax.tree.leaves(out_shape))
    body_of = kernel
    if after:
        body_of = lambda *refs: kernel(*refs[len(after) :])
    return pl.pallas_call(
        body_of,
        out_shape=out_shape,
        in_specs=[ANY] * len(after) + [SMEM] * scalars + [VMEM] * (len(operands) - scalars),
        out_specs=jax.tree.map(lambda _: VMEM, out_shape),
        scratch_shapes=scratch,
        compiler_params=pltpu.CompilerParams(vmem_limit_bytes=40 * 1024 * 1024),
        cost_estimate=pl.CostEstimate(flops=flops + weight * 1_000_000_000, bytes_accessed=moved, transcendentals=0),
    )(*after, *operands)


def shape(dims, kind):
    return jax.ShapeDtypeStruct(dims, kind)


def unit_of(rows):
    wide = rows.astype(f32)
    inverse = lax.rsqrt(jnp.sum(wide * wide, axis=-1, keepdims=True) + epsilon)
    return wide * inverse, inverse


def pair_terms(scale, offset, text_refs, images_ref, slopes_ref, own):
    step = 256
    totals = []
    for left in range(0, images_ref.shape[0], step):
        images = images_ref[left : left + step, :]
        total, done = jnp.zeros((1, images.shape[0]), f32), 0
        for texts in text_refs:
            for start in range(0, texts.shape[0], step):
                chunk = texts[start : min(start + step, texts.shape[0]), :]
                logits = (
                    scale
                    * lax.dot_general(
                        chunk, images, (((1,), (1,)), ((), ())), preferred_element_type=f32
                    )
                    + offset
                )
                shrunk = jnp.exp(-jnp.abs(logits))
                softplus = jnp.maximum(logits, 0.0) + jnp.log1p(shrunk)
                sigmoid = jnp.where(logits >= 0.0, 1.0, shrunk) / (1.0 + shrunk)
                if own and done == 0 and left == 0:
                    text_ids = lax.broadcasted_iota(jnp.int32, logits.shape, 0)
                    image_ids = lax.broadcasted_iota(jnp.int32, logits.shape, 1)
                    match = ((text_ids == image_ids) & (text_ids < own)).astype(f32)
                    softplus = softplus - match * logits
                    sigmoid = sigmoid - match
                slopes_ref[done : done + chunk.shape[0], left : left + images.shape[0]] = sigmoid.astype(bf16)
                total = total + jnp.sum(softplus, axis=0, keepdims=True)
                done += chunk.shape[0]
        totals.append(total)
    return jnp.concatenate(totals, axis=1)


def own_rows_kernel(text_ref, image_ref, text_emb_ref, image_emb_ref):
    text_emb_ref[...] = unit_of(text_ref[...])[0].astype(bf16)
    image_emb_ref[...] = unit_of(image_ref[...])[0].astype(bf16)


def near_texts_kernel(own_ref, beside_ref, above_ref, texts_ref, above_emb_ref):
    rows = own_ref.shape[0]
    texts_ref[:rows, :] = own_ref[...]
    texts_ref[rows : 2 * rows, :] = unit_of(beside_ref[...])[0].astype(bf16)
    above = unit_of(above_ref[...])[0].astype(bf16)
    texts_ref[2 * rows :, :] = above
    above_emb_ref[...] = above


def unit_kernel(*refs):
    for raw, emb in zip(refs[: len(refs) // 2], refs[len(refs) // 2 :]):
        emb[...] = unit_of(raw[...])[0].astype(bf16)


def far_pairs_kernel(scale_ref, bias_ref, *refs):
    text_refs, near_images_ref, near_slopes_ref, refs = refs[:4], refs[4], refs[5], refs[6:]
    image_refs, (images_ref, own_slopes_ref, other_slopes_ref, loss_ref, sent_ref) = refs[:-5], refs[-5:]
    rows = image_refs[0].shape[0]
    for place, block in enumerate(image_refs):
        images_ref[place * rows : (place + 1) * rows, :] = block[...]
    loss = pair_terms(scale_ref[0], bias_ref[0], text_refs[2:], images_ref, other_slopes_ref, 0)
    sums = jnp.dot(near_slopes_ref[...], near_images_ref[...], preferred_element_type=f32)
    sums = sums + jnp.dot(other_slopes_ref[...], images_ref[...], preferred_element_type=f32)
    sent_ref[...] = sums.astype(bf16)
    loss_ref[...] = loss + pair_terms(
        scale_ref[0], bias_ref[0], text_refs[:2], images_ref, own_slopes_ref, 0
    )


def own_core_pairs_kernel(scale_ref, bias_ref, near_ref, far_ref, *refs):
    image_refs, (images_ref, slopes_ref, loss_ref) = refs[:-3], refs[-3:]
    rows = far_ref.shape[0]
    for place, block in enumerate(image_refs):
        images_ref[place * rows : (place + 1) * rows, :] = block[...]
    loss_ref[...] = pair_terms(
        scale_ref[0], bias_ref[0], (near_ref, far_ref), images_ref, slopes_ref, rows
    )


def other_core_pairs_kernel(
    scale_ref, bias_ref, near_ref, far_ref, images_ref, first_loss_ref, slopes_ref, loss_ref
):
    loss_ref[...] = first_loss_ref[...] + pair_terms(
        scale_ref[0], bias_ref[0], (near_ref, far_ref), images_ref, slopes_ref, 0
    )


def loss_rows(loss):
    high = loss.astype(bf16).astype(f32)
    which = lax.broadcasted_iota(jnp.int32, (extra, loss.shape[1]), 0)
    return jnp.where(which == 0, high, loss - high).astype(bf16)


def image_sums_kernel(own, plain, loss_ref, *refs):
    slope_refs, text_refs, refs = refs[:2], refs[2:6], refs[6:]
    own_refs, refs = refs[: 2 * own], refs[2 * own :]
    whole_refs = (*refs[:plain], *refs[plain::2])
    tail_refs = (None,) * plain + tuple(refs[plain + 1 :: 2])
    rows, width = text_refs[1].shape
    step = 3 * lanes
    for left in range(0, width, step):
        total = None
        for slopes, texts in zip(slope_refs, (text_refs[:2], text_refs[2:])):
            done = 0
            for block in texts:
                part = lax.dot_general(
                    slopes[done : done + block.shape[0], :],
                    block[:, left : left + step],
                    (((0,), (0,)), ((), ())),
                    preferred_element_type=f32,
                )
                total, done = part if total is None else total + part, done + block.shape[0]
        if own:
            own_refs[0][:, left : left + step] = total[:rows, :]
        for place, (out, tail) in enumerate(zip(whole_refs, tail_refs), own):
            first = (out.shape[0] - extra) // rows * lanes
            for at in range(left, left + step, lanes):
                piece = total[place * rows : (place + 1) * rows, at - left : at - left + lanes]
                if at < first:
                    out[at // lanes * rows : (at // lanes + 1) * rows, :] = piece.astype(bf16)
                else:
                    tail[:, at - first : at - first + lanes] = piece.astype(tail.dtype)
    if own:
        own_refs[1][...] = loss_ref[:, :rows]
    for place, out in enumerate(whole_refs, own):
        out[out.shape[0] - extra :, :] = loss_rows(loss_ref[:, place * rows : (place + 1) * rows])


def text_sums_kernel(groups, received_ref, *refs):
    slope_refs, image_refs, outs = refs[:groups], refs[groups : 2 * groups], refs[2 * groups :]
    rows = outs[0].shape[0]
    for k, out in enumerate(outs):
        cut = slice(k * rows, (k + 1) * rows)
        sums = received_ref[cut, :].astype(f32)
        for slopes, images in zip(slope_refs, image_refs):
            sums = sums + jnp.dot(slopes[cut, :], images[...], preferred_element_type=f32)
        out[...] = sums.astype(out.dtype)


def late_heads_kernel(*refs):
    for source, target in zip(refs[: len(refs) // 2], refs[len(refs) // 2 :]):
        target[...] = source[...]


def late_kernel(sums, parts, *refs):
    payloads = (len(refs) - 2 * sums - sums * parts) // 2
    own, received = refs[:sums], refs[sums : sums + sums * parts]
    passed, outs = refs[sums + sums * parts :][:payloads], refs[sums + sums * parts + payloads :]
    for k in range(sums):
        total = own[k][...]
        for part in received[k * parts : (k + 1) * parts]:
            total = total + part[...].astype(f32)
        outs[k][...] = total.astype(bf16)
    for source, target in zip(passed, outs[sums:]):
        target[...] = source[...]


def row_gradient(rows, sums, scale, out_ref):
    unit_rows, inverse = unit_of(rows)
    unit_grad = scale * sums
    out_ref[...] = (
        unit_grad - unit_rows * jnp.sum(unit_rows * unit_grad, axis=-1, keepdims=True)
    ) * inverse


def image_end_kernel(batch, heads, scale_ref, image_ref, grad_ref, loss_ref, *refs):
    out_ref, out_loss_ref, sums_ref = refs[-3:]
    head_refs, tail_refs = refs[:heads], refs[heads:-3]
    rows, width = image_ref.shape
    loss = loss_ref[...]
    for panel in range(width // lanes):
        cut = slice(panel * lanes, (panel + 1) * lanes)
        sums = grad_ref[:, cut]
        for r in head_refs:
            if (panel + 1) * rows <= r.shape[0] - extra:
                sums = sums + r[panel * rows : (panel + 1) * rows, :].astype(f32)
        for r in tail_refs:
            first = panel * lanes - (width - r.shape[1])
            if first >= 0:
                sums = sums + r[:, first : first + lanes].astype(f32)
        sums_ref[:, cut] = sums
    for r in head_refs:
        last = r[r.shape[0] - extra :, :].astype(f32)
        loss = loss + (last[0:1, :] + last[1:2, :])
    row_gradient(image_ref[...], sums_ref[...], scale_ref[0], out_ref)
    out_loss_ref[...] = loss / batch


def text_end_kernel(scale_ref, text_ref, grad_ref, *refs):
    sums = grad_ref[...]
    for r in refs[:-1]:
        sums = sums + r[...].astype(f32)
    row_gradient(text_ref[...], sums, scale_ref[0], refs[-1])


def body(image, text, logarithm_scale, bias):
    rows, width = image.shape
    dp_count, inner_count = lax.axis_size("dp"), lax.axis_size("inner")
    batch = rows * dp_count * inner_count
    scale = jnp.exp(logarithm_scale)
    block = shape((rows, width), bf16)
    wide_block = shape((rows, width), f32)

    image_dp, image_inner = range(4, dp_count, 4), range(2, inner_count, 2)

    text_z = swapped(text, "inner", 1)
    images_z = [swapped(image, "inner", q) for q in image_inner]
    text_x = swapped(text, "dp", 2)
    images_y = [swapped(image, "dp", p) for p in image_dp]
    text_emb, image_emb = call(own_rows_kernel, (block, block), text, image)

    near_texts, text_z_emb = call(
        near_texts_kernel, (shape((3 * rows, width), bf16), block), text_emb, text_x, text_z, after=images_y
    )
    far_text = swapped(text_z_emb, "dp", 2)
    near_swapped = swapped(near_texts, "dp", 1)
    embs_z = call(unit_kernel, [block] * len(images_z), *images_z, weight=weights["z"])
    embs_yz = [swapped(emb, "dp", p) for emb in embs_z for p in image_dp]
    far_swapped = swapped(far_text, "dp", 1)
    embs_y = call(unit_kernel, [block] * len(images_y), *images_y)

    near, far = [image_emb, *embs_y, *embs_z], embs_yz
    near_rows, far_rows, texts_half = len(near) * rows, len(far) * rows, 4 * rows
    texts = [near_texts, far_text, near_swapped, far_swapped]
    pair_flops = 2 * rows * texts_half * width
    images, own_core_slopes, loss = call(
        own_core_pairs_kernel,
        (shape((near_rows, width), bf16), shape((texts_half, near_rows), bf16), shape((1, near_rows), f32)),
        scale,
        bias,
        *texts[:2],
        *near,
        flops=pair_flops * len(near),
        weight=weights["p1"],
        scalars=2,
    )
    other_core_slopes, loss = call(
        other_core_pairs_kernel,
        (shape((texts_half, near_rows), bf16), shape((1, near_rows), f32)),
        scale,
        bias,
        *texts[2:],
        images,
        loss,
        flops=pair_flops * len(near),
        scalars=2,
    )
    head_rows = direct_panels * rows + extra
    tail_width = width - direct_panels * lanes
    image_grad, own_loss, *sent = call(
        functools.partial(image_sums_kernel, 1, len(embs_y)),
        [wide_block, shape((1, rows), f32)]
        + [shape((width // lanes * rows + extra, lanes), bf16)] * len(embs_y)
        + [shape((head_rows, lanes), bf16), shape((rows, tail_width), f32)] * len(embs_z),
        loss,
        own_core_slopes,
        other_core_slopes,
        *texts,
        flops=2 * pair_flops * len(near),
    )
    payloads_y, heads, tails = sent[: len(embs_y)], sent[len(embs_y) :: 2], sent[len(embs_y) + 1 :: 2]
    z_heads = [swapped(head, "inner", q) for head, q in zip(heads, image_inner)]

    far_images, far_own_slopes, far_other_slopes, loss, crossing = call(
        far_pairs_kernel,
        (
            shape((far_rows, width), bf16),
            shape((texts_half, far_rows), bf16),
            shape((texts_half, far_rows), bf16),
            shape((1, far_rows), f32),
            shape((texts_half, width), bf16),
        ),
        scale,
        bias,
        *texts,
        images,
        other_core_slopes,
        *far,
        flops=pair_flops * (len(near) + 3 * len(far)),
        scalars=2,
        after=[image_grad],
    )
    crossed = swapped(crossing, "dp", 1)
    sent = call(
        functools.partial(image_sums_kernel, 0, 0),
        [shape((head_rows, lanes), bf16), shape((rows, tail_width), bf16)] * len(far),
        loss,
        far_own_slopes,
        far_other_slopes,
        *texts,
        flops=2 * pair_flops * len(far),
    )
    far_places = [(p, q) for q in image_inner for p in image_dp]
    moved_tails = [swapped(tail, "dp", p) for tail, (p, q) in zip(sent[1::2], far_places)]
    yz_heads = [swapped_both(head, p, q) for head, (p, q) in zip(sent[::2], far_places)]
    text_grad, text_x_sums, text_z_sums, text_xz_sums = call(
        functools.partial(text_sums_kernel, 2),
        (wide_block, block, wide_block, block),
        crossed,
        own_core_slopes,
        far_own_slopes,
        images,
        far_images,
        flops=pair_flops * (len(near) + len(far)),
        after=[sent[0]],
    )
    moved_text = swapped(text_xz_sums, "dp", 2)
    (moved_text,) = call(late_heads_kernel, [block], moved_text, weight=weights["text"])

    z_heads = call(late_heads_kernel, [shape(h.shape, bf16) for h in z_heads], *z_heads, weight=weights["heads"], after=[text_x_sums])
    late = call(
        functools.partial(late_kernel, len(image_inner), len(image_dp)),
        [shape((rows, tail_width), bf16)] * len(image_inner) + [shape(p.shape, bf16) for p in payloads_y],
        *tails,
        *moved_tails,
        *payloads_y,
        weight=weights["late"],
        after=z_heads,
    )
    tail_parts = [swapped(part, "inner", q) for part, q in zip(late, image_inner)]
    y_parts = [swapped(part, "dp", p) for part, p in zip(late[len(image_inner) :], image_dp)]
    yz_heads = call(
        late_heads_kernel, [shape(h.shape, bf16) for h in yz_heads], *yz_heads, weight=weights["far heads"], after=late[:1]
    )
    late_text_z, late_text_x = call(
        functools.partial(late_kernel, 1, 1),
        [block, block],
        text_z_sums,
        moved_text,
        text_x_sums,
        after=yz_heads,
    )
    text_parts = [swapped(late_text_z, "inner", 1), swapped(late_text_x, "dp", 2)]

    head_parts = [*z_heads, *yz_heads, *y_parts]
    image_gradient, image_loss = call(
        functools.partial(image_end_kernel, batch, len(head_parts)),
        (wide_block, shape((1, rows), f32)),
        scale,
        image,
        image_grad,
        own_loss,
        *head_parts,
        *tail_parts,
        scalars=1,
        weight=weights["end"],
        scratch=[pltpu.VMEM((rows, width), f32)],
    )
    text_gradient = call(text_end_kernel, wide_block, scale, text, text_grad, *text_parts, scalars=1)
    return (image_gradient, text_gradient, image_loss.reshape(rows))


def solution(mesh):
    return jax.shard_map(
        body,
        mesh=mesh,
        in_specs=(P(("dp", "inner"), None), P(("dp", "inner"), None), P(), P()),
        out_specs=(P(("dp", "inner"), None), P(("dp", "inner"), None), P(("dp", "inner"))),
        check_vma=False,
    )
```

```python
import functools

import jax
import jax.numpy as jnp
from jax import lax
from jax.experimental import pallas as pl
from jax.experimental.pallas import tpu as pltpu
from jax.sharding import PartitionSpec as P

epsilon = 1e-06
f32, bf16 = jnp.float32, jnp.bfloat16
lanes = 128
extra = 16
direct_panels = 4
weights = {"z": 10, "p1": 10, "heads": 2, "late": 0, "far heads": 2, "end": 0, "text": 4, "text end": 10}
VMEM = pl.BlockSpec(memory_space=pltpu.VMEM)
SMEM = pl.BlockSpec(memory_space=pltpu.SMEM)
ANY = pl.BlockSpec(memory_space=pl.ANY)


def swapped(value, axis, step):
    return lax.ppermute(value, axis, [(place, place ^ step) for place in range(lax.axis_size(axis))])


def swapped_both(value, dp_step, inner_step):
    dp_count, inner_count = lax.axis_size("dp"), lax.axis_size("inner")
    pairs = [
        (d * inner_count + i, (d ^ dp_step) * inner_count + (i ^ inner_step))
        for d in range(dp_count)
        for i in range(inner_count)
    ]
    return lax.ppermute(value, ("dp", "inner"), pairs)


def call(kernel, out_shape, *operands, flops=0, weight=0, scalars=0, scratch=(), after=()):
    moved = sum(o.size * o.dtype.itemsize for o in operands)
    moved += sum(o.size * o.dtype.itemsize for o in jax.tree.leaves(out_shape))
    first, last = len(operands), len(operands) + len(after)
    return pl.pallas_call(
        lambda *refs: kernel(*refs[:first], *refs[last:]),
        out_shape=out_shape,
        in_specs=[SMEM] * scalars + [VMEM] * (len(operands) - scalars) + [ANY] * len(after),
        out_specs=jax.tree.map(lambda _: VMEM, out_shape),
        scratch_shapes=scratch,
        compiler_params=pltpu.CompilerParams(vmem_limit_bytes=40 * 1024 * 1024),
        cost_estimate=pl.CostEstimate(
            flops=flops + int(weight * 1e9), bytes_accessed=moved, transcendentals=0
        ),
    )(*operands, *after)


def shape(dims, kind):
    return jax.ShapeDtypeStruct(dims, kind)


def unit_of(rows):
    wide = rows.astype(f32)
    inverse = lax.rsqrt(jnp.sum(wide * wide, axis=-1, keepdims=True) + epsilon)
    return wide * inverse, inverse


def pair_terms(scale, offset, text_refs, images_ref, slopes_ref, own):
    step = 256
    totals = []
    for left in range(0, images_ref.shape[0], step):
        images = images_ref[left : left + step, :]
        total, done = jnp.zeros((1, images.shape[0]), f32), 0
        for texts in text_refs:
            for start in range(0, texts.shape[0], step):
                chunk = texts[start : min(start + step, texts.shape[0]), :]
                logits = (
                    scale
                    * lax.dot_general(
                        chunk, images, (((1,), (1,)), ((), ())), preferred_element_type=f32
                    )
                    + offset
                )
                shrunk = jnp.exp(-jnp.abs(logits))
                raised = 1.0 + shrunk
                inverse = pl.reciprocal(raised, approx=True)
                inverse = inverse * (2.0 - raised * inverse)
                log_raised = jnp.log(raised) + (shrunk - (raised - 1.0)) * inverse
                softplus = jnp.maximum(logits, 0.0) + log_raised
                sigmoid = jnp.where(logits >= 0.0, inverse, shrunk * inverse)
                if own and done == 0 and left == 0:
                    text_ids = lax.broadcasted_iota(jnp.int32, logits.shape, 0)
                    image_ids = lax.broadcasted_iota(jnp.int32, logits.shape, 1)
                    match = ((text_ids == image_ids) & (text_ids < own)).astype(f32)
                    softplus = softplus - match * logits
                    sigmoid = sigmoid - match
                slopes_ref[done : done + chunk.shape[0], left : left + images.shape[0]] = sigmoid.astype(bf16)
                total = total + jnp.sum(softplus, axis=0, keepdims=True)
                done += chunk.shape[0]
        totals.append(total)
    return jnp.concatenate(totals, axis=1)


def own_rows_kernel(text_ref, image_ref, text_emb_ref, image_emb_ref):
    text_emb_ref[...] = unit_of(text_ref[...])[0].astype(bf16)
    image_emb_ref[...] = unit_of(image_ref[...])[0].astype(bf16)


def near_texts_kernel(above_ref, beside_ref, own_ref, texts_ref):
    rows = own_ref.shape[0]
    texts_ref[:rows, :] = own_ref[...]
    texts_ref[rows : 2 * rows, :] = unit_of(beside_ref[...])[0].astype(bf16)
    texts_ref[2 * rows :, :] = above_ref[...]


def unit_kernel(*refs):
    for raw, emb in zip(refs[: len(refs) // 2], refs[len(refs) // 2 :]):
        emb[...] = unit_of(raw[...])[0].astype(bf16)


def far_pairs_kernel(scale_ref, bias_ref, *refs):
    text_refs, near_images_ref, near_slopes_ref, refs = refs[:4], refs[4], refs[5], refs[6:]
    image_refs, (images_ref, own_slopes_ref, other_slopes_ref, loss_ref, sent_ref) = refs[:-5], refs[-5:]
    rows = image_refs[0].shape[0]
    for place, block in enumerate(image_refs):
        images_ref[place * rows : (place + 1) * rows, :] = block[...]
    loss = pair_terms(scale_ref[0], bias_ref[0], text_refs[2:], images_ref, other_slopes_ref, 0)
    sums = jnp.dot(near_slopes_ref[...], near_images_ref[...], preferred_element_type=f32)
    sums = sums + jnp.dot(other_slopes_ref[...], images_ref[...], preferred_element_type=f32)
    sent_ref[...] = sums.astype(bf16)
    loss_ref[...] = loss + pair_terms(
        scale_ref[0], bias_ref[0], text_refs[:2], images_ref, own_slopes_ref, 0
    )


def own_core_pairs_kernel(scale_ref, bias_ref, near_ref, far_ref, *refs):
    image_refs, (images_ref, slopes_ref, loss_ref) = refs[:-3], refs[-3:]
    rows = far_ref.shape[0]
    for place, block in enumerate(image_refs):
        images_ref[place * rows : (place + 1) * rows, :] = block[...]
    loss_ref[...] = pair_terms(
        scale_ref[0], bias_ref[0], (near_ref, far_ref), images_ref, slopes_ref, rows
    )


def other_core_pairs_kernel(
    scale_ref, bias_ref, near_ref, far_ref, images_ref, first_loss_ref, slopes_ref, loss_ref
):
    loss_ref[...] = first_loss_ref[...] + pair_terms(
        scale_ref[0], bias_ref[0], (near_ref, far_ref), images_ref, slopes_ref, 0
    )


def loss_rows(loss):
    high = loss.astype(bf16).astype(f32)
    which = lax.broadcasted_iota(jnp.int32, (extra, loss.shape[1]), 0)
    return jnp.where(which == 0, high, loss - high).astype(bf16)


def image_sums_kernel(own, plain, loss_ref, *refs):
    slope_refs, text_refs, refs = refs[:2], refs[2:6], refs[6:]
    own_refs, refs = refs[: 2 * own], refs[2 * own :]
    whole_refs = (*refs[:plain], *refs[plain::2])
    tail_refs = (None,) * plain + tuple(refs[plain + 1 :: 2])
    rows, width = text_refs[1].shape
    step = 3 * lanes
    for left in range(0, width, step):
        total = None
        for slopes, texts in zip(slope_refs, (text_refs[:2], text_refs[2:])):
            done = 0
            for block in texts:
                part = lax.dot_general(
                    slopes[done : done + block.shape[0], :],
                    block[:, left : left + step],
                    (((0,), (0,)), ((), ())),
                    preferred_element_type=f32,
                )
                total, done = part if total is None else total + part, done + block.shape[0]
        if own:
            own_refs[0][:, left : left + step] = total[:rows, :]
        for place, (out, tail) in enumerate(zip(whole_refs, tail_refs), own):
            first = (out.shape[0] - extra) // rows * lanes
            for at in range(left, left + step, lanes):
                piece = total[place * rows : (place + 1) * rows, at - left : at - left + lanes]
                if at < first:
                    out[at // lanes * rows : (at // lanes + 1) * rows, :] = piece.astype(bf16)
                else:
                    tail[:, at - first : at - first + lanes] = piece.astype(tail.dtype)
    if own:
        own_refs[1][...] = loss_ref[:, :rows]
    for place, out in enumerate(whole_refs, own):
        out[out.shape[0] - extra :, :] = loss_rows(loss_ref[:, place * rows : (place + 1) * rows])


def text_sums_kernel(groups, received_ref, *refs):
    slope_refs, image_refs, outs = refs[:groups], refs[groups : 2 * groups], refs[2 * groups :]
    rows = outs[0].shape[0]
    for k, out in enumerate(outs):
        cut = slice(k * rows, (k + 1) * rows)
        sums = received_ref[cut, :].astype(f32)
        for slopes, images in zip(slope_refs, image_refs):
            sums = sums + jnp.dot(slopes[cut, :], images[...], preferred_element_type=f32)
        out[...] = sums.astype(out.dtype)


def late_heads_kernel(*refs):
    for source, target in zip(refs[: len(refs) // 2], refs[len(refs) // 2 :]):
        target[...] = source[...]


def late_kernel(sums, parts, *refs):
    payloads = (len(refs) - 2 * sums - sums * parts) // 2
    own, received = refs[:sums], refs[sums : sums + sums * parts]
    passed, outs = refs[sums + sums * parts :][:payloads], refs[sums + sums * parts + payloads :]
    for k in range(sums):
        total = own[k][...]
        for part in received[k * parts : (k + 1) * parts]:
            total = total + part[...].astype(f32)
        outs[k][...] = total.astype(bf16)
    for source, target in zip(passed, outs[sums:]):
        target[...] = source[...]


def row_gradient(rows, sums, scale, out_ref):
    unit_rows, inverse = unit_of(rows)
    unit_grad = scale * sums
    out_ref[...] = (
        unit_grad - unit_rows * jnp.sum(unit_rows * unit_grad, axis=-1, keepdims=True)
    ) * inverse


def image_end_kernel(batch, heads, scale_ref, image_ref, grad_ref, loss_ref, *refs):
    out_ref, out_loss_ref, sums_ref = refs[-3:]
    head_refs, tail_refs = refs[:heads], refs[heads:-3]
    rows, width = image_ref.shape
    loss = loss_ref[...]
    for panel in range(width // lanes):
        cut = slice(panel * lanes, (panel + 1) * lanes)
        sums = grad_ref[:, cut]
        for r in head_refs:
            if (panel + 1) * rows <= r.shape[0] - extra:
                sums = sums + r[panel * rows : (panel + 1) * rows, :].astype(f32)
        for r in tail_refs:
            first = panel * lanes - (width - r.shape[1])
            if first >= 0:
                sums = sums + r[:, first : first + lanes].astype(f32)
        sums_ref[:, cut] = sums
    for r in head_refs:
        last = r[r.shape[0] - extra :, :].astype(f32)
        loss = loss + (last[0:1, :] + last[1:2, :])
    row_gradient(image_ref[...], sums_ref[...], scale_ref[0], out_ref)
    out_loss_ref[...] = loss / batch


def text_end_kernel(scale_ref, text_ref, grad_ref, *refs):
    sums = grad_ref[...]
    for r in refs[:-1]:
        sums = sums + r[...].astype(f32)
    row_gradient(text_ref[...], sums, scale_ref[0], refs[-1])


def body(image, text, logarithm_scale, bias):
    rows, width = image.shape
    dp_count, inner_count = lax.axis_size("dp"), lax.axis_size("inner")
    batch = rows * dp_count * inner_count
    scale = jnp.exp(logarithm_scale)
    block = shape((rows, width), bf16)
    wide_block = shape((rows, width), f32)

    image_dp, image_inner = range(4, dp_count, 4), range(2, inner_count, 2)

    images_y = [swapped(image, "dp", p) for p in image_dp]
    text_x = swapped(text, "dp", 2)
    images_z = [swapped(image, "inner", q) for q in image_inner]
    text_z = swapped(text, "inner", 1)
    text_emb, image_emb = call(own_rows_kernel, (block, block), text, image)

    text_z_emb, *embs_z = call(
        unit_kernel, [block] * (1 + len(images_z)), text_z, *images_z, weight=weights["z"]
    )
    near_texts = call(
        near_texts_kernel,
        shape((3 * rows, width), bf16),
        text_z_emb,
        text_x,
        text_emb,
        after=images_y,
    )
    far_text = swapped(text_z_emb, "dp", 2)
    near_swapped = swapped(near_texts, "dp", 1)
    embs_yz = [swapped(emb, "dp", p) for emb in embs_z for p in image_dp]
    far_swapped = swapped(far_text, "dp", 1)
    embs_y = call(unit_kernel, [block] * len(images_y), *images_y)

    near, far = [image_emb, *embs_y, *embs_z], embs_yz
    near_rows, far_rows, texts_half = len(near) * rows, len(far) * rows, 4 * rows
    texts = [near_texts, far_text, near_swapped, far_swapped]
    pair_flops = 2 * rows * texts_half * width
    images, own_core_slopes, loss = call(
        own_core_pairs_kernel,
        (shape((near_rows, width), bf16), shape((texts_half, near_rows), bf16), shape((1, near_rows), f32)),
        scale,
        bias,
        *texts[:2],
        *near,
        flops=pair_flops * len(near),
        weight=weights["p1"],
        scalars=2,
    )
    other_core_slopes, loss = call(
        other_core_pairs_kernel,
        (shape((texts_half, near_rows), bf16), shape((1, near_rows), f32)),
        scale,
        bias,
        *texts[2:],
        images,
        loss,
        flops=pair_flops * len(near),
        scalars=2,
    )
    head_rows = direct_panels * rows + extra
    tail_width = width - direct_panels * lanes
    image_grad, own_loss, *sent = call(
        functools.partial(image_sums_kernel, 1, len(embs_y)),
        [wide_block, shape((1, rows), f32)]
        + [shape((width // lanes * rows + extra, lanes), bf16)] * len(embs_y)
        + [shape((head_rows, lanes), bf16), shape((rows, tail_width), f32)] * len(embs_z),
        loss,
        own_core_slopes,
        other_core_slopes,
        *texts,
        flops=2 * pair_flops * len(near),
    )
    payloads_y, heads, tails = sent[: len(embs_y)], sent[len(embs_y) :: 2], sent[len(embs_y) + 1 :: 2]
    z_heads = [swapped(head, "inner", q) for head, q in zip(heads, image_inner)]

    far_images, far_own_slopes, far_other_slopes, loss, crossing = call(
        far_pairs_kernel,
        (
            shape((far_rows, width), bf16),
            shape((texts_half, far_rows), bf16),
            shape((texts_half, far_rows), bf16),
            shape((1, far_rows), f32),
            shape((texts_half, width), bf16),
        ),
        scale,
        bias,
        *texts,
        images,
        other_core_slopes,
        *far,
        flops=pair_flops * (len(near) + 3 * len(far)),
        scalars=2,
        after=[image_grad],
    )
    crossed = swapped(crossing, "dp", 1)
    sent = call(
        functools.partial(image_sums_kernel, 0, 0),
        [shape((head_rows, lanes), bf16), shape((rows, tail_width), bf16)] * len(far),
        loss,
        far_own_slopes,
        far_other_slopes,
        *texts,
        flops=2 * pair_flops * len(far),
    )
    text_grad, text_x_sums, text_z_sums, text_xz_sums = call(
        functools.partial(text_sums_kernel, 2),
        (wide_block, block, wide_block, block),
        crossed,
        own_core_slopes,
        far_own_slopes,
        images,
        far_images,
        flops=pair_flops * (len(near) + len(far)),
        after=[sent[0]],
    )
    moved_text = swapped(text_xz_sums, "dp", 2)
    sent = call(
        late_heads_kernel, [shape(part.shape, bf16) for part in sent], *sent, after=[text_x_sums]
    )
    far_places = [(p, q) for q in image_inner for p in image_dp]
    moved_tails = [swapped(tail, "dp", p) for tail, (p, q) in zip(sent[1::2], far_places)]
    yz_heads = [swapped_both(head, p, q) for head, (p, q) in zip(sent[::2], far_places)]

    z_heads = call(
        late_heads_kernel,
        [shape(h.shape, bf16) for h in z_heads],
        *z_heads,
        weight=weights["heads"],
        after=[text_x_sums],
    )
    late_text_z, late_text_x = call(
        functools.partial(late_kernel, 1, 1),
        [block, block],
        text_z_sums,
        moved_text,
        text_x_sums,
        weight=weights["text"],
        after=z_heads,
    )
    text_parts = [swapped(late_text_z, "inner", 1), swapped(late_text_x, "dp", 2)]
    late = call(
        functools.partial(late_kernel, len(image_inner), len(image_dp)),
        [shape((rows, tail_width), bf16)] * len(image_inner) + [shape(p.shape, bf16) for p in payloads_y],
        *tails,
        *moved_tails,
        *payloads_y,
        weight=weights["late"],
        after=[late_text_z],
    )
    tail_parts = [swapped(part, "inner", q) for part, q in zip(late, image_inner)]
    y_parts = [swapped(part, "dp", p) for part, p in zip(late[len(image_inner) :], image_dp)]
    yz_heads = call(
        late_heads_kernel,
        [shape(h.shape, bf16) for h in yz_heads],
        *yz_heads,
        weight=weights["far heads"],
        after=late[:1],
    )

    head_parts = [*z_heads, *yz_heads, *y_parts]
    image_gradient, image_loss = call(
        functools.partial(image_end_kernel, batch, len(head_parts)),
        (wide_block, shape((1, rows), f32)),
        scale,
        image,
        image_grad,
        own_loss,
        *head_parts,
        *tail_parts,
        scalars=1,
        weight=weights["end"],
        scratch=[pltpu.VMEM((rows, width), f32)],
    )
    text_gradient = call(text_end_kernel, wide_block, scale, text, text_grad, *text_parts, scalars=1, weight=weights["text end"])
    return (image_gradient, text_gradient, image_loss.reshape(rows))


def solution(mesh):
    return jax.shard_map(
        body,
        mesh=mesh,
        in_specs=(P(("dp", "inner"), None), P(("dp", "inner"), None), P(), P()),
        out_specs=(P(("dp", "inner"), None), P(("dp", "inner"), None), P(("dp", "inner"))),
        check_vma=False,
    )
```

```python
import functools

import jax
import jax.numpy as jnp
from jax import lax
from jax.experimental import pallas as pl
from jax.experimental.pallas import tpu as pltpu
from jax.sharding import PartitionSpec as P

epsilon = 1e-06
f32, bf16 = jnp.float32, jnp.bfloat16
lanes = 128
extra = 16
weights = {"z": 10, "late": 2, "text": 2, "end": 0, "text end": 0}
VMEM = pl.BlockSpec(memory_space=pltpu.VMEM)
SMEM = pl.BlockSpec(memory_space=pltpu.SMEM)
ANY = pl.BlockSpec(memory_space=pl.ANY)


def swapped(value, axis, step):
    return lax.ppermute(value, axis, [(place, place ^ step) for place in range(lax.axis_size(axis))])


def call(kernel, out_shape, *operands, flops=0, weight=0, scalars=0, scratch=(), after=()):
    moved = sum(o.size * o.dtype.itemsize for o in operands)
    moved += sum(o.size * o.dtype.itemsize for o in jax.tree.leaves(out_shape))
    first, last = len(operands), len(operands) + len(after)
    return pl.pallas_call(
        lambda *refs: kernel(*refs[:first], *refs[last:]),
        out_shape=out_shape,
        in_specs=[SMEM] * scalars + [VMEM] * (len(operands) - scalars) + [ANY] * len(after),
        out_specs=jax.tree.map(lambda _: VMEM, out_shape),
        scratch_shapes=scratch,
        compiler_params=pltpu.CompilerParams(vmem_limit_bytes=40 * 1024 * 1024),
        cost_estimate=pl.CostEstimate(
            flops=flops + int(weight * 1e9), bytes_accessed=moved, transcendentals=0
        ),
    )(*operands, *after)


def shape(dims, kind):
    return jax.ShapeDtypeStruct(dims, kind)


def unit_of(rows):
    wide = rows.astype(f32)
    inverse = lax.rsqrt(jnp.sum(wide * wide, axis=-1, keepdims=True) + epsilon)
    return wide * inverse, inverse


def pair_terms(scale, offset, text_refs, image_refs, slopes_ref, own=0, losses=True):
    step = 256
    totals, left = [], 0
    for image_rows in image_refs:
        for at in range(0, image_rows.shape[0], step):
            images = image_rows[at : min(at + step, image_rows.shape[0]), :]
            count = images.shape[0]
            total, done = jnp.zeros((1, count), f32), 0
            for texts in text_refs:
                for start in range(0, texts.shape[0], step):
                    chunk = texts[start : min(start + step, texts.shape[0]), :]
                    logits = (
                        scale
                        * lax.dot_general(
                            chunk, images, (((1,), (1,)), ((), ())), preferred_element_type=f32
                        )
                        + offset
                    )
                    shrunk = jnp.exp(-jnp.abs(logits))
                    raised = 1.0 + shrunk
                    inverse = pl.reciprocal(raised, approx=True)
                    inverse = inverse * (2.0 - raised * inverse)
                    sigmoid = jnp.where(logits >= 0.0, inverse, shrunk * inverse)
                    match = None
                    if own and done == 0 and left == 0:
                        text_ids = lax.broadcasted_iota(jnp.int32, logits.shape, 0)
                        image_ids = lax.broadcasted_iota(jnp.int32, logits.shape, 1)
                        match = ((text_ids == image_ids) & (text_ids < own)).astype(f32)
                        sigmoid = sigmoid - match
                    slopes_ref[done : done + chunk.shape[0], left : left + count] = sigmoid.astype(bf16)
                    if losses:
                        log_raised = jnp.log(raised) + (shrunk - (raised - 1.0)) * inverse
                        softplus = jnp.maximum(logits, 0.0) + log_raised
                        if match is not None:
                            softplus = softplus - match * logits
                        total = total + jnp.sum(softplus, axis=0, keepdims=True)
                    done += chunk.shape[0]
            totals.append(total)
            left += count
    return jnp.concatenate(totals, axis=1)


def unit_kernel(*refs):
    for raw, emb in zip(refs[: len(refs) // 2], refs[len(refs) // 2 :]):
        emb[...] = unit_of(raw[...])[0].astype(bf16)


def copies_kernel(*refs):
    for source, target in zip(refs[: len(refs) // 2], refs[len(refs) // 2 :]):
        target[...] = source[...]


def near_kernel(held, *refs):
    out_ref, rows = refs[-1], refs[0].shape[0]
    for place, block in enumerate(refs[:-1]):
        emb = block[...] if place in held else unit_of(block[...])[0].astype(bf16)
        out_ref[place * rows : (place + 1) * rows, :] = emb


def near_pairs_kernel(own, scale_ref, bias_ref, near_ref, far_ref, images_ref, *refs):
    slopes_ref, loss_ref = refs[-2:]
    rows = far_ref.shape[0]
    texts = (near_ref.at[: 3 * rows, :], far_ref)
    loss = pair_terms(
        scale_ref[0], bias_ref[0], texts, (images_ref.at[3 * rows :, :],), slopes_ref, rows if own else 0
    )
    loss_ref[...] = loss if own else loss + refs[0][...]


def loss_rows(loss):
    high = loss.astype(bf16).astype(f32)
    which = lax.broadcasted_iota(jnp.int32, (extra, loss.shape[1]), 0)
    return jnp.where(which == 0, high, loss - high).astype(bf16)


def sums_in_parts(slope_refs, text_refs, width):
    step = 3 * lanes
    for left in range(0, width, step):
        total = None
        for slopes, texts in zip(slope_refs, text_refs):
            done = 0
            for block in texts:
                part = lax.dot_general(
                    slopes[done : done + block.shape[0], :],
                    block[:, left : left + step],
                    (((0,), (0,)), ((), ())),
                    preferred_element_type=f32,
                )
                total, done = part if total is None else total + part, done + block.shape[0]
        yield left, step, total


def put_panels(out, rows, left, sums):
    for at in range(0, sums.shape[1], lanes):
        panel = (left + at) // lanes
        out[panel * rows : (panel + 1) * rows, :] = sums[:, at : at + lanes].astype(out.dtype)


def far_kernel(count, scale_ref, bias_ref, near_ref, far_ref, near_swapped_ref, far_swapped_ref, *refs):
    image_refs, (own_slopes_ref, *sent_refs), other_slopes_ref = refs[:count], refs[count:-1], refs[-1]
    rows, width = far_ref.shape
    scale, offset = scale_ref[0], bias_ref[0]
    own_texts = (near_ref.at[: 3 * rows, :], far_ref)
    other_texts = (near_swapped_ref.at[: 3 * rows, :], far_swapped_ref)
    loss = pair_terms(scale, offset, own_texts, image_refs, own_slopes_ref)
    loss = loss + pair_terms(scale, offset, other_texts, image_refs, other_slopes_ref)
    slopes = (own_slopes_ref, other_slopes_ref)
    for left, step, total in sums_in_parts(slopes, (own_texts, other_texts), width):
        for place, out in enumerate(sent_refs):
            put_panels(out, rows, left, total[place * rows : (place + 1) * rows, :])
    for place, out in enumerate(sent_refs):
        out[width // lanes * rows :, :] = loss_rows(loss[:, place * rows : (place + 1) * rows])


def near_sums_kernel(
    plain, own_slopes_ref, other_slopes_ref, near_ref, far_ref, near_swapped_ref, far_swapped_ref, loss_ref, *refs
):
    own_ref, own_loss_ref, plain_refs, rest = refs[0], refs[1], refs[2 : 2 + plain], refs[2 + plain :]
    z_refs, z_loss_refs = rest[::2], rest[1::2]
    rows, width = far_ref.shape
    own_texts = (near_ref.at[: 3 * rows, :], far_ref)
    other_texts = (near_swapped_ref.at[: 3 * rows, :], far_swapped_ref)
    slopes = (own_slopes_ref, other_slopes_ref)
    for left, step, total in sums_in_parts(slopes, (own_texts, other_texts), width):
        own_ref[:, left : left + step] = total[:rows, :]
        for place, out in enumerate((*plain_refs, *z_refs), 1):
            put_panels(out, rows, left, total[place * rows : (place + 1) * rows, :])
    own_loss_ref[...] = loss_ref[:, :rows]
    for place, out in enumerate(plain_refs, 1):
        out[width // lanes * rows :, :] = loss_rows(loss_ref[:, place * rows : (place + 1) * rows])
    for place, out in enumerate(z_loss_refs, 1 + plain):
        out[...] = loss_ref[:, place * rows : (place + 1) * rows]


def text_kernel(
    count, scale_ref, bias_ref, near_ref, far_ref, near_swapped_ref, near_slopes_ref, far_slopes_ref, *refs
):
    far_refs, far_swapped_refs, outs, slopes_ref = refs[:count], refs[count : 2 * count], refs[2 * count : -1], refs[-1]
    rows, width = far_ref.shape
    own_texts = (near_ref.at[: 3 * rows, :], far_ref)
    swapped_images = (near_swapped_ref.at[3 * rows :, :], *far_swapped_refs)
    pair_terms(scale_ref[0], bias_ref[0], own_texts, swapped_images, slopes_ref, losses=False)
    terms, left = [], near_slopes_ref.shape[1]
    for slopes, blocks in (
        (near_slopes_ref, (near_ref.at[3 * rows :, :],)),
        (far_slopes_ref, far_refs),
        (slopes_ref, swapped_images),
    ):
        left = 0
        for images in blocks:
            terms.append((slopes.at[:, left : left + images.shape[0]], images))
            left += images.shape[0]
    step = 3 * lanes
    for left in range(0, width, step):
        total = None
        for slopes, images in terms:
            part = jnp.dot(slopes[...], images[:, left : left + step], preferred_element_type=f32)
            total = part if total is None else total + part
        for k, out in enumerate(outs):
            out[:, left : left + step] = total[k * rows : (k + 1) * rows, :].astype(out.dtype)


def late_image_kernel(zs, ys, *refs):
    sums, losses, refs = refs[:zs], refs[zs : 2 * zs], refs[2 * zs :]
    parts, payloads, outs = refs[: zs * ys], refs[zs * ys : zs * ys + ys], refs[zs * ys + ys :]
    for k in range(zs):
        height = sums[k].shape[0]
        total, loss = sums[k][...], losses[k][...]
        for part in parts[k * ys : (k + 1) * ys]:
            total = total + part[:height, :].astype(f32)
            last = part[height:, :].astype(f32)
            loss = loss + (last[0:1, :] + last[1:2, :])
        outs[k][:height, :] = total.astype(bf16)
        outs[k][height:, :] = loss_rows(loss)
    for source, target in zip(payloads, outs[zs:]):
        target[...] = source[...]


def late_text_kernel(sums_ref, part_ref, passed_ref, out_ref, passed_out_ref):
    out_ref[...] = (sums_ref[...] + part_ref[...].astype(f32)).astype(bf16)
    passed_out_ref[...] = passed_ref[...]


def row_gradient(rows, sums, scale, out_ref):
    unit_rows, inverse = unit_of(rows)
    unit_grad = scale * sums
    out_ref[...] = (
        unit_grad - unit_rows * jnp.sum(unit_rows * unit_grad, axis=-1, keepdims=True)
    ) * inverse


def image_end_kernel(batch, scale_ref, image_ref, grad_ref, loss_ref, *refs):
    parts, (out_ref, out_loss_ref, sums_ref) = refs[:-3], refs[-3:]
    rows, width = image_ref.shape
    loss = loss_ref[...]
    for panel in range(width // lanes):
        cut = slice(panel * lanes, (panel + 1) * lanes)
        sums = grad_ref[:, cut]
        for part in parts:
            sums = sums + part[panel * rows : (panel + 1) * rows, :].astype(f32)
        sums_ref[:, cut] = sums
    for part in parts:
        last = part[width // lanes * rows :, :].astype(f32)
        loss = loss + (last[0:1, :] + last[1:2, :])
    row_gradient(image_ref[...], sums_ref[...], scale_ref[0], out_ref)
    out_loss_ref[...] = loss / batch


def text_end_kernel(scale_ref, text_ref, grad_ref, *refs):
    sums = grad_ref[...]
    for r in refs[:-1]:
        sums = sums + r[...].astype(f32)
    row_gradient(text_ref[...], sums, scale_ref[0], refs[-1])


def body(image, text, logarithm_scale, bias):
    rows, width = image.shape
    dp_count, inner_count = lax.axis_size("dp"), lax.axis_size("inner")
    batch = rows * dp_count * inner_count
    scale = jnp.exp(logarithm_scale)
    block = shape((rows, width), bf16)
    wide_block = shape((rows, width), f32)

    image_dp, image_inner = range(4, dp_count, 4), range(2, inner_count, 2)

    images_y = [swapped(image, "dp", p) for p in image_dp]
    text_x = swapped(text, "dp", 2)
    images_z = [swapped(image, "inner", q) for q in image_inner]
    text_z = swapped(text, "inner", 1)
    text_emb, image_emb = call(unit_kernel, [block, block], text, image)
    text_z_emb, *embs_z = call(
        unit_kernel, [block] * (1 + len(images_z)), text_z, *images_z, weight=weights["z"], after=[text_emb]
    )
    far_text = swapped(text_z_emb, "dp", 2)
    far = [swapped(emb, "dp", p) for emb in embs_z for p in image_dp]
    far_places = [(p, q) for q in image_inner for p in image_dp]
    zs, ys = len(embs_z), len(images_y)

    held = {0, 2, 3, *range(4 + ys, 4 + ys + zs)}
    near = call(
        functools.partial(near_kernel, frozenset(held)),
        shape(((4 + ys + zs) * rows, width), bf16),
        text_emb,
        text_x,
        text_z_emb,
        image_emb,
        *images_y,
        *embs_z,
    )
    near_swapped = swapped(near, "dp", 1)
    far_text_swapped = swapped(far_text, "dp", 1)

    half, near_rows, far_rows = 4 * rows, (1 + ys + zs) * rows, len(far) * rows
    own_texts, other_texts = (near, far_text), (near_swapped, far_text_swapped)
    pair_flops = 2 * rows * half * width
    near_slopes, near_loss = shape((half, near_rows), bf16), shape((1, near_rows), f32)
    payload = shape((width // lanes * rows + extra, lanes), bf16)
    own_slopes, loss = call(
        functools.partial(near_pairs_kernel, True),
        (near_slopes, near_loss),
        scale,
        bias,
        *own_texts,
        near,
        flops=pair_flops * (1 + ys + zs),
        scalars=2,
    )
    passed = call(copies_kernel, [block] * len(far), *far, after=[loss])
    far_swapped = [swapped(emb, "dp", 1) for emb in passed]
    other_slopes, loss = call(
        functools.partial(near_pairs_kernel, False),
        (near_slopes, near_loss),
        scale,
        bias,
        *other_texts,
        near,
        loss,
        flops=pair_flops * (1 + ys + zs),
        scalars=2,
    )
    far_slopes, *far_sent = call(
        functools.partial(far_kernel, len(far)),
        [shape((half, far_rows), bf16)] + [payload] * len(far),
        scale,
        bias,
        *own_texts,
        *other_texts,
        *far,
        flops=4 * pair_flops * len(far),
        scalars=2,
        scratch=[pltpu.VMEM((half, far_rows), bf16)],
        after=[loss],
    )
    moved = [swapped(part, "dp", p) for part, (p, q) in zip(far_sent, far_places)]
    text_grad, text_x_sums, text_z_sums, text_xz_sums = call(
        functools.partial(text_kernel, len(far)),
        (wide_block, block, wide_block, block),
        scale,
        bias,
        *own_texts,
        near_swapped,
        own_slopes,
        far_slopes,
        *far,
        *far_swapped,
        flops=3 * pair_flops * (1 + ys + zs + len(far)),
        scalars=2,
        scratch=[pltpu.VMEM((half, near_rows + far_rows), bf16)],
        after=far_sent[:1],
    )
    moved_text = swapped(text_xz_sums, "dp", 2)
    image_grad, own_loss, *sums = call(
        functools.partial(near_sums_kernel, ys),
        [wide_block, shape((1, rows), f32)]
        + [payload] * ys
        + [shape((width // lanes * rows, lanes), f32), shape((1, rows), f32)] * zs,
        own_slopes,
        other_slopes,
        *own_texts,
        *other_texts,
        loss,
        flops=2 * pair_flops * (1 + ys + zs),
        after=[text_x_sums],
    )

    late = call(
        functools.partial(late_image_kernel, zs, ys),
        [payload] * (zs + ys),
        *sums[ys::2],
        *sums[ys + 1 :: 2],
        *moved,
        *sums[:ys],
        weight=weights["late"],
    )
    image_parts = [swapped(part, "inner", q) for part, q in zip(late, image_inner)]
    image_parts += [swapped(part, "dp", p) for part, p in zip(late[zs:], image_dp)]
    late_text_z, late_text_x = call(
        late_text_kernel,
        [block, block],
        text_z_sums,
        moved_text,
        text_x_sums,
        weight=weights["text"],
        after=late[:1],
    )
    text_parts = [swapped(late_text_z, "inner", 1), swapped(late_text_x, "dp", 2)]

    image_gradient, image_loss = call(
        functools.partial(image_end_kernel, batch),
        (wide_block, shape((1, rows), f32)),
        scale,
        image,
        image_grad,
        own_loss,
        *image_parts,
        scalars=1,
        weight=weights["end"],
        scratch=[pltpu.VMEM((rows, width), f32)],
    )
    text_gradient = call(
        text_end_kernel, wide_block, scale, text, text_grad, *text_parts, scalars=1, weight=weights["text end"]
    )
    return (image_gradient, text_gradient, image_loss.reshape(rows))


def solution(mesh):
    return jax.shard_map(
        body,
        mesh=mesh,
        in_specs=(P(("dp", "inner"), None), P(("dp", "inner"), None), P(), P()),
        out_specs=(P(("dp", "inner"), None), P(("dp", "inner"), None), P(("dp", "inner"))),
        check_vma=False,
    )
```

```python
import functools

import jax
import jax.numpy as jnp
from jax import lax
from jax.experimental import pallas as pl
from jax.experimental.pallas import tpu as pltpu
from jax.sharding import PartitionSpec as P

epsilon = 1e-06
f32, bf16 = jnp.float32, jnp.bfloat16
lanes = 128
extra = 16
weights = {"x far": 10, "y far": 10, "x": 0, "a": 10, "b": 10, "late": 2, "text": 2, "end": 0, "text end": 0}
VMEM = pl.BlockSpec(memory_space=pltpu.VMEM)
SMEM = pl.BlockSpec(memory_space=pltpu.SMEM)
ANY = pl.BlockSpec(memory_space=pl.ANY)


def swapped(value, axis, step):
    return lax.ppermute(value, axis, [(place, place ^ step) for place in range(lax.axis_size(axis))])


def call(kernel, out_shape, *operands, flops=0, weight=0, scalars=0, scratch=(), after=()):
    moved = sum(o.size * o.dtype.itemsize for o in operands)
    moved += sum(o.size * o.dtype.itemsize for o in jax.tree.leaves(out_shape))
    first, last = len(operands), len(operands) + len(after)
    return pl.pallas_call(
        lambda *refs: kernel(*refs[:first], *refs[last:]),
        out_shape=out_shape,
        in_specs=[SMEM] * scalars + [VMEM] * (len(operands) - scalars) + [ANY] * len(after),
        out_specs=jax.tree.map(lambda _: VMEM, out_shape),
        scratch_shapes=scratch,
        compiler_params=pltpu.CompilerParams(vmem_limit_bytes=40 * 1024 * 1024),
        cost_estimate=pl.CostEstimate(
            flops=flops + int(weight * 1e9), bytes_accessed=moved, transcendentals=0
        ),
    )(*operands, *after)


def shape(dims, kind):
    return jax.ShapeDtypeStruct(dims, kind)


def unit_of(rows):
    wide = rows.astype(f32)
    inverse = lax.rsqrt(jnp.sum(wide * wide, axis=-1, keepdims=True) + epsilon)
    return wide * inverse, inverse


def pair_terms(scale, offset, text_refs, image_refs, slopes_ref, own=0, losses=True):
    step = 256
    totals, left = [], 0
    for image_rows in image_refs:
        for at in range(0, image_rows.shape[0], step):
            images = image_rows[at : min(at + step, image_rows.shape[0]), :]
            count = images.shape[0]
            total, done = jnp.zeros((1, count), f32), 0
            for texts in text_refs:
                for start in range(0, texts.shape[0], step):
                    chunk = texts[start : min(start + step, texts.shape[0]), :]
                    logits = (
                        scale
                        * lax.dot_general(
                            chunk, images, (((1,), (1,)), ((), ())), preferred_element_type=f32
                        )
                        + offset
                    )
                    shrunk = jnp.exp(-jnp.abs(logits))
                    raised = 1.0 + shrunk
                    inverse = pl.reciprocal(raised, approx=True)
                    inverse = inverse * (2.0 - raised * inverse)
                    sigmoid = jnp.where(logits >= 0.0, inverse, shrunk * inverse)
                    match = None
                    if own and done == 0 and left == 0:
                        text_ids = lax.broadcasted_iota(jnp.int32, logits.shape, 0)
                        image_ids = lax.broadcasted_iota(jnp.int32, logits.shape, 1)
                        match = ((text_ids == image_ids) & (text_ids < own)).astype(f32)
                        sigmoid = sigmoid - match
                    slopes_ref[done : done + chunk.shape[0], left : left + count] = sigmoid.astype(bf16)
                    if losses:
                        log_raised = jnp.log(raised) + (shrunk - (raised - 1.0)) * inverse
                        softplus = jnp.maximum(logits, 0.0) + log_raised
                        if match is not None:
                            softplus = softplus - match * logits
                        total = total + jnp.sum(softplus, axis=0, keepdims=True)
                    done += chunk.shape[0]
            totals.append(total)
            left += count
    return jnp.concatenate(totals, axis=1)


def unit_kernel(*refs):
    for raw, emb in zip(refs[: len(refs) // 2], refs[len(refs) // 2 :]):
        emb[...] = unit_of(raw[...])[0].astype(bf16)


def copies_kernel(*refs):
    for source, target in zip(refs[: len(refs) // 2], refs[len(refs) // 2 :]):
        target[...] = source[...]


def own_rows_kernel(scale_ref, bias_ref, text_ref, image_ref, text_emb_ref, image_emb_ref, half_ref):
    text_emb_ref[...] = unit_of(text_ref[...])[0].astype(bf16)
    emb = unit_of(image_ref[...])[0].astype(bf16)
    image_emb_ref[...] = emb
    half_ref[...] = emb[emb.shape[0] // 2 :, :]


def near_kernel(raw, *refs):
    out_ref, start = refs[-1], 0
    for place, block in enumerate(refs[:-1]):
        count = block.shape[0]
        out_ref[start : start + count, :] = unit_of(block[...])[0].astype(bf16) if place in raw else block[...]
        start += count


def join_kernel(*refs):
    count = len(refs) // 3
    for first, second, out in zip(refs[:count], refs[count : 2 * count], refs[2 * count :]):
        rows = first.shape[0]
        out[:rows, :] = first[...]
        out[rows:, :] = second[...]


def near_pairs_kernel(own, scale_ref, bias_ref, near_ref, far_ref, images_ref, *refs):
    slopes_ref, loss_ref = refs[-2:]
    rows = far_ref.shape[0]
    texts = (near_ref.at[: 3 * rows, :], far_ref)
    loss = pair_terms(
        scale_ref[0], bias_ref[0], texts, (images_ref.at[3 * rows :, :],), slopes_ref, rows if own else 0
    )
    loss_ref[...] = loss if own else loss + refs[0][...]


def loss_rows(loss):
    high = loss.astype(bf16).astype(f32)
    which = lax.broadcasted_iota(jnp.int32, (extra, loss.shape[1]), 0)
    return jnp.where(which == 0, high, loss - high).astype(bf16)


def sums_in_parts(slope_refs, text_refs, width):
    step = 3 * lanes
    for left in range(0, width, step):
        total = None
        for slopes, texts in zip(slope_refs, text_refs):
            done = 0
            for block in texts:
                part = lax.dot_general(
                    slopes[done : done + block.shape[0], :],
                    block[:, left : left + step],
                    (((0,), (0,)), ((), ())),
                    preferred_element_type=f32,
                )
                total, done = part if total is None else total + part, done + block.shape[0]
        yield left, step, total


def put_panels(out, rows, left, sums):
    for at in range(0, sums.shape[1], lanes):
        panel = (left + at) // lanes
        out[panel * rows : (panel + 1) * rows, :] = sums[:, at : at + lanes].astype(out.dtype)


def far_kernel(count, scale_ref, bias_ref, near_ref, far_ref, near_swapped_ref, far_swapped_ref, *refs):
    image_refs, (own_slopes_ref, *sent_refs), other_slopes_ref = refs[:count], refs[count:-1], refs[-1]
    rows, width = far_ref.shape
    scale, offset = scale_ref[0], bias_ref[0]
    own_texts = (near_ref.at[: 3 * rows, :], far_ref)
    other_texts = (near_swapped_ref.at[: 3 * rows, :], far_swapped_ref)
    loss = pair_terms(scale, offset, own_texts, image_refs, own_slopes_ref)
    loss = loss + pair_terms(scale, offset, other_texts, image_refs, other_slopes_ref)
    slopes = (own_slopes_ref, other_slopes_ref)
    for left, step, total in sums_in_parts(slopes, (own_texts, other_texts), width):
        for place, out in enumerate(sent_refs):
            put_panels(out, rows, left, total[place * rows : (place + 1) * rows, :])
    for place, out in enumerate(sent_refs):
        out[width // lanes * rows :, :] = loss_rows(loss[:, place * rows : (place + 1) * rows])


def near_sums_kernel(
    plain, own_slopes_ref, other_slopes_ref, near_ref, far_ref, near_swapped_ref, far_swapped_ref, loss_ref, *refs
):
    own_ref, own_loss_ref, plain_refs, rest = refs[0], refs[1], refs[2 : 2 + plain], refs[2 + plain :]
    z_refs, z_loss_refs = rest[::2], rest[1::2]
    rows, width = far_ref.shape
    own_texts = (near_ref.at[: 3 * rows, :], far_ref)
    other_texts = (near_swapped_ref.at[: 3 * rows, :], far_swapped_ref)
    slopes = (own_slopes_ref, other_slopes_ref)
    for left, step, total in sums_in_parts(slopes, (own_texts, other_texts), width):
        own_ref[:, left : left + step] = total[:rows, :]
        for place, out in enumerate((*plain_refs, *z_refs), 1):
            put_panels(out, rows, left, total[place * rows : (place + 1) * rows, :])
    own_loss_ref[...] = loss_ref[:, :rows]
    for place, out in enumerate(plain_refs, 1):
        out[width // lanes * rows :, :] = loss_rows(loss_ref[:, place * rows : (place + 1) * rows])
    for place, out in enumerate(z_loss_refs, 1 + plain):
        out[...] = loss_ref[:, place * rows : (place + 1) * rows]


def text_kernel(
    count, scale_ref, bias_ref, near_ref, far_ref, near_swapped_ref, near_slopes_ref, far_slopes_ref, *refs
):
    far_refs, far_swapped_refs, outs, slopes_ref = refs[:count], refs[count : 2 * count], refs[2 * count : -1], refs[-1]
    rows, width = far_ref.shape
    own_texts = (near_ref.at[: 3 * rows, :], far_ref)
    swapped_images = (near_swapped_ref.at[3 * rows :, :], *far_swapped_refs)
    pair_terms(scale_ref[0], bias_ref[0], own_texts, swapped_images, slopes_ref, losses=False)
    terms, left = [], near_slopes_ref.shape[1]
    for slopes, blocks in (
        (near_slopes_ref, (near_ref.at[3 * rows :, :],)),
        (far_slopes_ref, far_refs),
        (slopes_ref, swapped_images),
    ):
        left = 0
        for images in blocks:
            terms.append((slopes.at[:, left : left + images.shape[0]], images))
            left += images.shape[0]
    step = 3 * lanes
    for left in range(0, width, step):
        total = None
        for slopes, images in terms:
            part = jnp.dot(slopes[...], images[:, left : left + step], preferred_element_type=f32)
            total = part if total is None else total + part
        for k, out in enumerate(outs):
            out[:, left : left + step] = total[k * rows : (k + 1) * rows, :].astype(out.dtype)


def late_image_kernel(zs, ys, *refs):
    sums, losses, refs = refs[:zs], refs[zs : 2 * zs], refs[2 * zs :]
    parts, payloads, outs = refs[: zs * ys], refs[zs * ys : zs * ys + ys], refs[zs * ys + ys :]
    for k in range(zs):
        height = sums[k].shape[0]
        total, loss = sums[k][...], losses[k][...]
        for part in parts[k * ys : (k + 1) * ys]:
            total = total + part[:height, :].astype(f32)
            last = part[height:, :].astype(f32)
            loss = loss + (last[0:1, :] + last[1:2, :])
        outs[k][:height, :] = total.astype(bf16)
        outs[k][height:, :] = loss_rows(loss)
    for source, target in zip(payloads, outs[zs:]):
        target[...] = source[...]


def late_text_kernel(sums_ref, part_ref, passed_ref, out_ref, passed_out_ref):
    out_ref[...] = (sums_ref[...] + part_ref[...].astype(f32)).astype(bf16)
    passed_out_ref[...] = passed_ref[...]


def row_gradient(rows, sums, scale, out_ref):
    unit_rows, inverse = unit_of(rows)
    unit_grad = scale * sums
    out_ref[...] = (
        unit_grad - unit_rows * jnp.sum(unit_rows * unit_grad, axis=-1, keepdims=True)
    ) * inverse


def image_end_kernel(batch, scale_ref, image_ref, grad_ref, loss_ref, *refs):
    parts, (out_ref, out_loss_ref, sums_ref) = refs[:-3], refs[-3:]
    rows, width = image_ref.shape
    loss = loss_ref[...]
    for panel in range(width // lanes):
        cut = slice(panel * lanes, (panel + 1) * lanes)
        sums = grad_ref[:, cut]
        for part in parts:
            sums = sums + part[panel * rows : (panel + 1) * rows, :].astype(f32)
        sums_ref[:, cut] = sums
    for part in parts:
        last = part[width // lanes * rows :, :].astype(f32)
        loss = loss + (last[0:1, :] + last[1:2, :])
    row_gradient(image_ref[...], sums_ref[...], scale_ref[0], out_ref)
    out_loss_ref[...] = loss / batch


def text_end_kernel(scale_ref, text_ref, grad_ref, *refs):
    sums = grad_ref[...]
    for r in refs[:-1]:
        sums = sums + r[...].astype(f32)
    row_gradient(text_ref[...], sums, scale_ref[0], refs[-1])


def body(image, text, logarithm_scale, bias):
    rows, width = image.shape
    dp_count, inner_count = lax.axis_size("dp"), lax.axis_size("inner")
    batch = rows * dp_count * inner_count
    scale = jnp.exp(logarithm_scale)
    block = shape((rows, width), bf16)
    wide_block = shape((rows, width), f32)

    image_dp, image_inner = range(4, dp_count, 4), range(2, inner_count, 2)

    half_block = shape((rows // 2, width), bf16)
    text_z = swapped(text, "inner", 1)
    text_x = swapped(text, "dp", 2)
    first_half = image[: rows // 2]
    first_z = [swapped(first_half, "inner", q) for q in image_inner]
    images_y = [swapped(image, "dp", p) for p in image_dp]
    text_emb, image_emb, second_half = call(
        own_rows_kernel, [block, block, half_block], scale, bias, text, image, scalars=2
    )
    second_z = [swapped(second_half, "inner", q) for q in image_inner]
    zs, ys = len(first_z), len(images_y)

    (text_z_emb,) = call(unit_kernel, [block], text_z, weight=weights["x"], after=[text_x, second_half])
    (far_text,) = call(copies_kernel, [block], swapped(text_z_emb, "dp", 2), weight=weights["x far"])
    far_places = [(p, q) for q in image_inner for p in image_dp]
    first_z = call(
        unit_kernel, [half_block] * zs, *first_z, weight=weights["a"], after=[text_z_emb, *images_y]
    )
    first_far = [swapped(emb, "dp", p) for emb in first_z for p in image_dp]
    first_far = call(
        copies_kernel, [half_block] * (zs * ys), *first_far, weight=weights["y far"], after=[far_text]
    )
    second_z = call(copies_kernel, [half_block] * zs, *second_z, weight=weights["b"], after=first_z)
    second_far = [swapped(emb, "dp", p) for emb in second_z for p in image_dp]

    near = call(
        functools.partial(near_kernel, frozenset({1, *range(4, 4 + ys)})),
        shape(((4 + ys + zs) * rows, width), bf16),
        text_emb,
        text_x,
        text_z_emb,
        image_emb,
        *images_y,
        *(part for both in zip(first_z, second_z) for part in both),
    )
    near_swapped = swapped(near, "dp", 1)
    far_text_swapped = swapped(far_text, "dp", 1)

    half, near_rows, far_rows = 4 * rows, (1 + ys + zs) * rows, zs * ys * rows
    own_texts, other_texts = (near, far_text), (near_swapped, far_text_swapped)
    pair_flops = 2 * rows * half * width
    near_slopes, near_loss = shape((half, near_rows), bf16), shape((1, near_rows), f32)
    payload = shape((width // lanes * rows + extra, lanes), bf16)
    own_slopes, loss = call(
        functools.partial(near_pairs_kernel, True),
        (near_slopes, near_loss),
        scale,
        bias,
        *own_texts,
        near,
        flops=pair_flops * (1 + ys + zs),
        scalars=2,
    )
    far = call(join_kernel, [block] * (zs * ys), *first_far, *second_far, after=[loss])
    far_swapped = [swapped(emb, "dp", 1) for emb in far]
    other_slopes, loss = call(
        functools.partial(near_pairs_kernel, False),
        (near_slopes, near_loss),
        scale,
        bias,
        *other_texts,
        near,
        loss,
        flops=pair_flops * (1 + ys + zs),
        scalars=2,
    )
    far_slopes, *far_sent = call(
        functools.partial(far_kernel, len(far)),
        [shape((half, far_rows), bf16)] + [payload] * len(far),
        scale,
        bias,
        *own_texts,
        *other_texts,
        *far,
        flops=4 * pair_flops * len(far),
        scalars=2,
        scratch=[pltpu.VMEM((half, far_rows), bf16)],
        after=[loss],
    )
    moved = [swapped(part, "dp", p) for part, (p, q) in zip(far_sent, far_places)]
    text_grad, text_x_sums, text_z_sums, text_xz_sums = call(
        functools.partial(text_kernel, len(far)),
        (wide_block, block, wide_block, block),
        scale,
        bias,
        *own_texts,
        near_swapped,
        own_slopes,
        far_slopes,
        *far,
        *far_swapped,
        flops=3 * pair_flops * (1 + ys + zs + len(far)),
        scalars=2,
        scratch=[pltpu.VMEM((half, near_rows + far_rows), bf16)],
        after=far_sent[:1],
    )
    moved_text = swapped(text_xz_sums, "dp", 2)
    image_grad, own_loss, *sums = call(
        functools.partial(near_sums_kernel, ys),
        [wide_block, shape((1, rows), f32)]
        + [payload] * ys
        + [shape((width // lanes * rows, lanes), f32), shape((1, rows), f32)] * zs,
        own_slopes,
        other_slopes,
        *own_texts,
        *other_texts,
        loss,
        flops=2 * pair_flops * (1 + ys + zs),
        after=[text_x_sums],
    )

    late = call(
        functools.partial(late_image_kernel, zs, ys),
        [payload] * (zs + ys),
        *sums[ys::2],
        *sums[ys + 1 :: 2],
        *moved,
        *sums[:ys],
        weight=weights["late"],
    )
    image_parts = [swapped(part, "inner", q) for part, q in zip(late, image_inner)]
    image_parts += [swapped(part, "dp", p) for part, p in zip(late[zs:], image_dp)]
    late_text_z, late_text_x = call(
        late_text_kernel,
        [block, block],
        text_z_sums,
        moved_text,
        text_x_sums,
        weight=weights["text"],
        after=late[:1],
    )
    text_parts = [swapped(late_text_z, "inner", 1), swapped(late_text_x, "dp", 2)]

    image_gradient, image_loss = call(
        functools.partial(image_end_kernel, batch),
        (wide_block, shape((1, rows), f32)),
        scale,
        image,
        image_grad,
        own_loss,
        *image_parts,
        scalars=1,
        weight=weights["end"],
        scratch=[pltpu.VMEM((rows, width), f32)],
    )
    text_gradient = call(
        text_end_kernel, wide_block, scale, text, text_grad, *text_parts, scalars=1, weight=weights["text end"]
    )
    return (image_gradient, text_gradient, image_loss.reshape(rows))


def solution(mesh):
    return jax.shard_map(
        body,
        mesh=mesh,
        in_specs=(P(("dp", "inner"), None), P(("dp", "inner"), None), P(), P()),
        out_specs=(P(("dp", "inner"), None), P(("dp", "inner"), None), P(("dp", "inner"))),
        check_vma=False,
    )
```

```python
import functools

import jax
import jax.numpy as jnp
from jax import lax
from jax.experimental import pallas as pl
from jax.experimental.pallas import tpu as pltpu
from jax.sharding import PartitionSpec as P

epsilon = 1e-06
f32, bf16 = jnp.float32, jnp.bfloat16
lanes = 128
extra = 16
weights = {"x far": 10, "y far": 10, "x": 0, "a": 10, "b": 10, "late": 2, "text": 2, "end": 5}
VMEM = pl.BlockSpec(memory_space=pltpu.VMEM)
SMEM = pl.BlockSpec(memory_space=pltpu.SMEM)
ANY = pl.BlockSpec(memory_space=pl.ANY)


def swapped(value, axis, step):
    return lax.ppermute(value, axis, [(place, place ^ step) for place in range(lax.axis_size(axis))])


def call(kernel, out_shape, *operands, flops=0, weight=0, scalars=0, scratch=(), after=()):
    moved = sum(o.size * o.dtype.itemsize for o in operands)
    moved += sum(o.size * o.dtype.itemsize for o in jax.tree.leaves(out_shape))
    first, last = len(operands), len(operands) + len(after)
    return pl.pallas_call(
        lambda *refs: kernel(*refs[:first], *refs[last:]),
        out_shape=out_shape,
        in_specs=[SMEM] * scalars + [VMEM] * (len(operands) - scalars) + [ANY] * len(after),
        out_specs=jax.tree.map(lambda _: VMEM, out_shape),
        scratch_shapes=scratch,
        compiler_params=pltpu.CompilerParams(vmem_limit_bytes=40 * 1024 * 1024),
        cost_estimate=pl.CostEstimate(
            flops=flops + int(weight * 1e9), bytes_accessed=moved, transcendentals=0
        ),
    )(*operands, *after)


def shape(dims, kind):
    return jax.ShapeDtypeStruct(dims, kind)


def unit_of(rows):
    wide = rows.astype(f32)
    inverse = lax.rsqrt(jnp.sum(wide * wide, axis=-1, keepdims=True) + epsilon)
    return wide * inverse, inverse


def pair_terms(scale, offset, text_refs, image_refs, slopes_ref, own=0, losses=True):
    step = 256
    totals, left = [], 0
    for image_rows in image_refs:
        for at in range(0, image_rows.shape[0], step):
            images = image_rows[at : min(at + step, image_rows.shape[0]), :]
            count = images.shape[0]
            total, done = jnp.zeros((1, count), f32), 0
            for texts in text_refs:
                for start in range(0, texts.shape[0], step):
                    chunk = texts[start : min(start + step, texts.shape[0]), :]
                    logits = (
                        scale
                        * lax.dot_general(
                            chunk, images, (((1,), (1,)), ((), ())), preferred_element_type=f32
                        )
                        + offset
                    )
                    shrunk = jnp.exp(-jnp.abs(logits))
                    raised = 1.0 + shrunk
                    inverse = pl.reciprocal(raised, approx=True)
                    inverse = inverse * (2.0 - raised * inverse)
                    sigmoid = jnp.where(logits >= 0.0, inverse, shrunk * inverse)
                    match = None
                    if own and done == 0 and left == 0:
                        text_ids = lax.broadcasted_iota(jnp.int32, logits.shape, 0)
                        image_ids = lax.broadcasted_iota(jnp.int32, logits.shape, 1)
                        match = ((text_ids == image_ids) & (text_ids < own)).astype(f32)
                        sigmoid = sigmoid - match
                    slopes_ref[done : done + chunk.shape[0], left : left + count] = sigmoid.astype(bf16)
                    if losses:
                        log_raised = jnp.log(raised) + (shrunk - (raised - 1.0)) * inverse
                        softplus = jnp.maximum(logits, 0.0) + log_raised
                        if match is not None:
                            softplus = softplus - match * logits
                        total = total + jnp.sum(softplus, axis=0, keepdims=True)
                    done += chunk.shape[0]
            totals.append(total)
            left += count
    return jnp.concatenate(totals, axis=1)


def unit_kernel(*refs):
    for raw, emb in zip(refs[: len(refs) // 2], refs[len(refs) // 2 :]):
        emb[...] = unit_of(raw[...])[0].astype(bf16)


def copies_kernel(*refs):
    for source, target in zip(refs[: len(refs) // 2], refs[len(refs) // 2 :]):
        target[...] = source[...]


def own_rows_kernel(scale_ref, bias_ref, text_ref, image_ref, text_emb_ref, image_emb_ref, half_ref):
    text_emb_ref[...] = unit_of(text_ref[...])[0].astype(bf16)
    emb = unit_of(image_ref[...])[0].astype(bf16)
    image_emb_ref[...] = emb
    half_ref[...] = emb[emb.shape[0] // 2 :, :]


def near_kernel(raw, *refs):
    out_ref, start = refs[-1], 0
    for place, block in enumerate(refs[:-1]):
        count = block.shape[0]
        out_ref[start : start + count, :] = unit_of(block[...])[0].astype(bf16) if place in raw else block[...]
        start += count


def join_kernel(*refs):
    count = len(refs) // 3
    for first, second, out in zip(refs[:count], refs[count : 2 * count], refs[2 * count :]):
        rows = first.shape[0]
        out[:rows, :] = first[...]
        out[rows:, :] = second[...]


def near_pairs_kernel(own, scale_ref, bias_ref, near_ref, far_ref, images_ref, *refs):
    slopes_ref, loss_ref = refs[-2:]
    rows = far_ref.shape[0]
    texts = (near_ref.at[: 3 * rows, :], far_ref)
    loss = pair_terms(
        scale_ref[0], bias_ref[0], texts, (images_ref.at[3 * rows :, :],), slopes_ref, rows if own else 0
    )
    loss_ref[...] = loss if own else loss + refs[0][...]


def loss_rows(loss):
    high = loss.astype(bf16).astype(f32)
    which = lax.broadcasted_iota(jnp.int32, (extra, loss.shape[1]), 0)
    return jnp.where(which == 0, high, loss - high).astype(bf16)


def sums_in_parts(slope_refs, text_refs, width):
    step = 3 * lanes
    for left in range(0, width, step):
        total = None
        for slopes, texts in zip(slope_refs, text_refs):
            done = 0
            for block in texts:
                part = lax.dot_general(
                    slopes[done : done + block.shape[0], :],
                    block[:, left : left + step],
                    (((0,), (0,)), ((), ())),
                    preferred_element_type=f32,
                )
                total, done = part if total is None else total + part, done + block.shape[0]
        yield left, step, total


def put_panels(out, rows, left, sums):
    for at in range(0, sums.shape[1], lanes):
        panel = (left + at) // lanes
        out[panel * rows : (panel + 1) * rows, :] = sums[:, at : at + lanes].astype(out.dtype)


def far_kernel(count, scale_ref, bias_ref, near_ref, far_ref, near_swapped_ref, far_swapped_ref, *refs):
    image_refs, (own_slopes_ref, *sent_refs), other_slopes_ref = refs[:count], refs[count:-1], refs[-1]
    rows, width = far_ref.shape
    scale, offset = scale_ref[0], bias_ref[0]
    own_texts = (near_ref.at[: 3 * rows, :], far_ref)
    other_texts = (near_swapped_ref.at[: 3 * rows, :], far_swapped_ref)
    loss = pair_terms(scale, offset, own_texts, image_refs, own_slopes_ref)
    loss = loss + pair_terms(scale, offset, other_texts, image_refs, other_slopes_ref)
    slopes = (own_slopes_ref, other_slopes_ref)
    for left, step, total in sums_in_parts(slopes, (own_texts, other_texts), width):
        for place, out in enumerate(sent_refs):
            put_panels(out, rows, left, total[place * rows : (place + 1) * rows, :])
    for place, out in enumerate(sent_refs):
        out[width // lanes * rows :, :] = loss_rows(loss[:, place * rows : (place + 1) * rows])


def near_sums_kernel(
    plain, own_slopes_ref, other_slopes_ref, near_ref, far_ref, near_swapped_ref, far_swapped_ref, loss_ref, *refs
):
    own_ref, own_loss_ref, plain_refs, rest = refs[0], refs[1], refs[2 : 2 + plain], refs[2 + plain :]
    z_refs, z_loss_refs = rest[::2], rest[1::2]
    rows, width = far_ref.shape
    own_texts = (near_ref.at[: 3 * rows, :], far_ref)
    other_texts = (near_swapped_ref.at[: 3 * rows, :], far_swapped_ref)
    slopes = (own_slopes_ref, other_slopes_ref)
    for left, step, total in sums_in_parts(slopes, (own_texts, other_texts), width):
        own_ref[:, left : left + step] = total[:rows, :]
        for place, out in enumerate((*plain_refs, *z_refs), 1):
            put_panels(out, rows, left, total[place * rows : (place + 1) * rows, :])
    own_loss_ref[...] = loss_ref[:, :rows]
    for place, out in enumerate(plain_refs, 1):
        out[width // lanes * rows :, :] = loss_rows(loss_ref[:, place * rows : (place + 1) * rows])
    for place, out in enumerate(z_loss_refs, 1 + plain):
        out[...] = loss_ref[:, place * rows : (place + 1) * rows]


def swapped_pairs_kernel(scale_ref, bias_ref, near_ref, far_ref, near_swapped_ref, slopes_ref):
    rows = far_ref.shape[0]
    own_texts = (near_ref.at[: 3 * rows, :], far_ref)
    images = (near_swapped_ref.at[3 * rows :, :],)
    pair_terms(scale_ref[0], bias_ref[0], own_texts, images, slopes_ref, losses=False)


def text_kernel(
    count, scale_ref, bias_ref, near_ref, far_ref, near_swapped_ref, near_slopes_ref, far_slopes_ref, other_slopes_ref, *refs
):
    far_refs, far_swapped_refs, outs, slopes_ref = refs[:count], refs[count : 2 * count], refs[2 * count : -1], refs[-1]
    rows, width = far_ref.shape
    own_texts = (near_ref.at[: 3 * rows, :], far_ref)
    pair_terms(scale_ref[0], bias_ref[0], own_texts, far_swapped_refs, slopes_ref, losses=False)
    terms = []
    for slopes, blocks in (
        (near_slopes_ref, (near_ref.at[3 * rows :, :],)),
        (other_slopes_ref, (near_swapped_ref.at[3 * rows :, :],)),
        (far_slopes_ref, far_refs),
        (slopes_ref, far_swapped_refs),
    ):
        left = 0
        for images in blocks:
            terms.append((slopes.at[:, left : left + images.shape[0]], images))
            left += images.shape[0]
    step = 3 * lanes
    for left in range(0, width, step):
        total = None
        for slopes, images in terms:
            part = jnp.dot(slopes[...], images[:, left : left + step], preferred_element_type=f32)
            total = part if total is None else total + part
        for k, out in enumerate(outs):
            out[:, left : left + step] = total[k * rows : (k + 1) * rows, :].astype(out.dtype)


def late_image_kernel(zs, ys, *refs):
    sums, losses, parts, outs = refs[:zs], refs[zs : 2 * zs], refs[2 * zs : -zs], refs[-zs:]
    for k in range(zs):
        height = sums[k].shape[0]
        total, loss = sums[k][...], losses[k][...]
        for part in parts[k * ys : (k + 1) * ys]:
            total = total + part[:height, :].astype(f32)
            last = part[height:, :].astype(f32)
            loss = loss + (last[0:1, :] + last[1:2, :])
        outs[k][:height, :] = total.astype(bf16)
        outs[k][height:, :] = loss_rows(loss)


def late_text_kernel(sums_ref, part_ref, *refs):
    count = len(refs) // 2
    refs[count][...] = (sums_ref[...] + part_ref[...].astype(f32)).astype(bf16)
    for source, target in zip(refs[:count], refs[count + 1 :]):
        target[...] = source[...]


def row_gradient(rows, sums, scale, out_ref):
    unit_rows, inverse = unit_of(rows)
    unit_grad = scale * sums
    out_ref[...] = (
        unit_grad - unit_rows * jnp.sum(unit_rows * unit_grad, axis=-1, keepdims=True)
    ) * inverse


def part_sums_kernel(grad_ref, loss_ref, *refs):
    parts, (sums_ref, out_loss_ref) = refs[:-2], refs[-2:]
    rows, width = grad_ref.shape
    loss = loss_ref[...]
    for panel in range(width // lanes):
        cut = slice(panel * lanes, (panel + 1) * lanes)
        sums = grad_ref[:, cut]
        for part in parts:
            sums = sums + part[panel * rows : (panel + 1) * rows, :].astype(f32)
        sums_ref[:, cut] = sums
    for part in parts:
        last = part[width // lanes * rows :, :].astype(f32)
        loss = loss + (last[0:1, :] + last[1:2, :])
    out_loss_ref[...] = loss


def image_end_kernel(batch, scale_ref, image_ref, grad_ref, loss_ref, *refs):
    parts, (out_ref, out_loss_ref, sums_ref) = refs[:-3], refs[-3:]
    part_sums_kernel(grad_ref, loss_ref, *parts, sums_ref, out_loss_ref)
    row_gradient(image_ref[...], sums_ref[...], scale_ref[0], out_ref)
    out_loss_ref[...] = out_loss_ref[...] / batch


def text_end_kernel(scale_ref, text_ref, grad_ref, *refs):
    sums = grad_ref[...]
    for r in refs[:-1]:
        sums = sums + r[...].astype(f32)
    row_gradient(text_ref[...], sums, scale_ref[0], refs[-1])


def body(image, text, logarithm_scale, bias):
    rows, width = image.shape
    dp_count, inner_count = lax.axis_size("dp"), lax.axis_size("inner")
    batch = rows * dp_count * inner_count
    scale = jnp.exp(logarithm_scale)
    block = shape((rows, width), bf16)
    wide_block = shape((rows, width), f32)

    image_dp, image_inner = range(4, dp_count, 4), range(2, inner_count, 2)

    half_block = shape((rows // 2, width), bf16)
    text_z = swapped(text, "inner", 1)
    text_x = swapped(text, "dp", 2)
    first_half = image[: rows // 2]
    first_z = [swapped(first_half, "inner", q) for q in image_inner]
    images_y = [swapped(image, "dp", p) for p in image_dp]
    text_emb, image_emb, second_half = call(
        own_rows_kernel, [block, block, half_block], scale, bias, text, image, scalars=2
    )
    second_z = [swapped(second_half, "inner", q) for q in image_inner]
    zs, ys = len(first_z), len(images_y)

    (text_z_emb,) = call(unit_kernel, [block], text_z, weight=weights["x"], after=[text_x, second_half])
    (far_text,) = call(copies_kernel, [block], swapped(text_z_emb, "dp", 2), weight=weights["x far"])
    far_places = [(p, q) for q in image_inner for p in image_dp]
    first_z = call(
        unit_kernel, [half_block] * zs, *first_z, weight=weights["a"], after=[text_z_emb, *images_y]
    )
    first_far = [swapped(emb, "dp", p) for emb in first_z for p in image_dp]
    first_far = call(
        copies_kernel, [half_block] * (zs * ys), *first_far, weight=weights["y far"], after=[far_text]
    )
    second_z = call(copies_kernel, [half_block] * zs, *second_z, weight=weights["b"], after=first_z)
    second_far = [swapped(emb, "dp", p) for emb in second_z for p in image_dp]

    near = call(
        functools.partial(near_kernel, frozenset({1, *range(4, 4 + ys)})),
        shape(((4 + ys + zs) * rows, width), bf16),
        text_emb,
        text_x,
        text_z_emb,
        image_emb,
        *images_y,
        *(part for both in zip(first_z, second_z) for part in both),
    )
    near_swapped = swapped(near, "dp", 1)
    far_text_swapped = swapped(far_text, "dp", 1)

    half, near_rows, far_rows = 4 * rows, (1 + ys + zs) * rows, zs * ys * rows
    own_texts, other_texts = (near, far_text), (near_swapped, far_text_swapped)
    pair_flops = 2 * rows * half * width
    near_slopes, near_loss = shape((half, near_rows), bf16), shape((1, near_rows), f32)
    payload = shape((width // lanes * rows + extra, lanes), bf16)
    own_slopes, loss = call(
        functools.partial(near_pairs_kernel, True),
        (near_slopes, near_loss),
        scale,
        bias,
        *own_texts,
        near,
        flops=pair_flops * (1 + ys + zs),
        scalars=2,
    )
    swapped_slopes = call(
        swapped_pairs_kernel,
        near_slopes,
        scale,
        bias,
        *own_texts,
        near_swapped,
        flops=pair_flops * (1 + ys + zs),
        scalars=2,
        after=[own_slopes],
    )
    far = call(join_kernel, [block] * (zs * ys), *first_far, *second_far, after=[swapped_slopes])
    far_swapped = [swapped(emb, "dp", 1) for emb in far]
    other_slopes, loss = call(
        functools.partial(near_pairs_kernel, False),
        (near_slopes, near_loss),
        scale,
        bias,
        *other_texts,
        near,
        loss,
        flops=pair_flops * (1 + ys + zs),
        scalars=2,
        after=[swapped_slopes],
    )
    far_slopes, *far_sent = call(
        functools.partial(far_kernel, len(far)),
        [shape((half, far_rows), bf16)] + [payload] * len(far),
        scale,
        bias,
        *own_texts,
        *other_texts,
        *far,
        flops=4 * pair_flops * len(far),
        scalars=2,
        scratch=[pltpu.VMEM((half, far_rows), bf16)],
        after=[loss],
    )
    moved = [swapped(part, "dp", p) for part, (p, q) in zip(far_sent, far_places)]
    text_grad, text_x_sums, text_z_sums, text_xz_sums = call(
        functools.partial(text_kernel, len(far)),
        (wide_block, block, wide_block, block),
        scale,
        bias,
        *own_texts,
        near_swapped,
        own_slopes,
        far_slopes,
        swapped_slopes,
        *far,
        *far_swapped,
        flops=3 * pair_flops * (1 + ys + zs + len(far)),
        scalars=2,
        scratch=[pltpu.VMEM((half, far_rows), bf16)],
        after=far_sent[:1],
    )
    moved_text = swapped(text_xz_sums, "dp", 2)
    image_grad, own_loss, *sums = call(
        functools.partial(near_sums_kernel, ys),
        [wide_block, shape((1, rows), f32)]
        + [payload] * ys
        + [shape((width // lanes * rows, lanes), f32), shape((1, rows), f32)] * zs,
        own_slopes,
        other_slopes,
        *own_texts,
        *other_texts,
        loss,
        flops=2 * pair_flops * (1 + ys + zs),
        after=[text_x_sums],
    )

    late = call(
        functools.partial(late_image_kernel, zs, ys),
        [payload] * zs,
        *sums[ys::2],
        *sums[ys + 1 :: 2],
        *moved,
        weight=weights["late"],
    )
    z_parts = [swapped(part, "inner", q) for part, q in zip(late, image_inner)]
    image_grad, own_loss = call(
        part_sums_kernel, (wide_block, shape((1, rows), f32)), image_grad, own_loss, *z_parts, weight=weights["end"]
    )
    late_text_z, late_text_x, *late_y = call(
        late_text_kernel,
        [block, block] + [payload] * ys,
        text_z_sums,
        moved_text,
        text_x_sums,
        *sums[:ys],
        weight=weights["text"],
        after=late[:1],
    )
    image_parts = [swapped(part, "dp", p) for part, p in zip(late_y, image_dp)]
    text_parts = [swapped(late_text_z, "inner", 1), swapped(late_text_x, "dp", 2)]

    image_gradient, image_loss = call(
        functools.partial(image_end_kernel, batch),
        (wide_block, shape((1, rows), f32)),
        scale,
        image,
        image_grad,
        own_loss,
        *image_parts,
        scalars=1,
        scratch=[pltpu.VMEM((rows, width), f32)],
    )
    text_gradient = call(
        text_end_kernel, wide_block, scale, text, text_grad, *text_parts, scalars=1, after=[image_gradient]
    )
    return (image_gradient, text_gradient, image_loss.reshape(rows))


def solution(mesh):
    return jax.shard_map(
        body,
        mesh=mesh,
        in_specs=(P(("dp", "inner"), None), P(("dp", "inner"), None), P(), P()),
        out_specs=(P(("dp", "inner"), None), P(("dp", "inner"), None), P(("dp", "inner"))),
        check_vma=False,
    )
```

```python
import functools

import jax
import jax.numpy as jnp
from jax import lax
from jax.experimental import pallas as pl
from jax.experimental.pallas import tpu as pltpu
from jax.sharding import PartitionSpec as P

epsilon = 1e-06
f32, bf16 = jnp.float32, jnp.bfloat16
lanes = 128
extra = 16
weights = {"x far": 10, "y far": 10, "x": 0, "a": 10, "b": 10, "late": 2, "text": 2, "end": 5}
VMEM = pl.BlockSpec(memory_space=pltpu.VMEM)
SMEM = pl.BlockSpec(memory_space=pltpu.SMEM)
ANY = pl.BlockSpec(memory_space=pl.ANY)


def swapped(value, axis, step):
    return lax.ppermute(value, axis, [(place, place ^ step) for place in range(lax.axis_size(axis))])


def call(kernel, out_shape, *operands, flops=0, weight=0, scalars=0, scratch=(), after=()):
    moved = sum(o.size * o.dtype.itemsize for o in operands)
    moved += sum(o.size * o.dtype.itemsize for o in jax.tree.leaves(out_shape))
    first, last = len(operands), len(operands) + len(after)
    return pl.pallas_call(
        lambda *refs: kernel(*refs[:first], *refs[last:]),
        out_shape=out_shape,
        in_specs=[SMEM] * scalars + [VMEM] * (len(operands) - scalars) + [ANY] * len(after),
        out_specs=jax.tree.map(lambda _: VMEM, out_shape),
        scratch_shapes=scratch,
        compiler_params=pltpu.CompilerParams(vmem_limit_bytes=40 * 1024 * 1024),
        cost_estimate=pl.CostEstimate(
            flops=flops + int(weight * 1e9), bytes_accessed=moved, transcendentals=0
        ),
    )(*operands, *after)


def shape(dims, kind):
    return jax.ShapeDtypeStruct(dims, kind)


def unit_of(rows):
    wide = rows.astype(f32)
    inverse = lax.rsqrt(jnp.sum(wide * wide, axis=-1, keepdims=True) + epsilon)
    return wide * inverse, inverse


def pair_terms(scale, offset, text_refs, image_refs, slopes_ref, own=0, losses=True):
    step = 256
    totals, left = [], 0
    for image_rows in image_refs:
        for at in range(0, image_rows.shape[0], step):
            images = image_rows[at : min(at + step, image_rows.shape[0]), :]
            count = images.shape[0]
            total, done = jnp.zeros((1, count), f32), 0
            for texts in text_refs:
                for start in range(0, texts.shape[0], step):
                    chunk = texts[start : min(start + step, texts.shape[0]), :]
                    logits = (
                        scale
                        * lax.dot_general(
                            chunk, images, (((1,), (1,)), ((), ())), preferred_element_type=f32
                        )
                        + offset
                    )
                    shrunk = jnp.exp(-jnp.abs(logits))
                    raised = 1.0 + shrunk
                    inverse = pl.reciprocal(raised, approx=True)
                    inverse = inverse * (2.0 - raised * inverse)
                    sigmoid = jnp.where(logits >= 0.0, inverse, shrunk * inverse)
                    match = None
                    if own and done == 0 and left == 0:
                        text_ids = lax.broadcasted_iota(jnp.int32, logits.shape, 0)
                        image_ids = lax.broadcasted_iota(jnp.int32, logits.shape, 1)
                        match = ((text_ids == image_ids) & (text_ids < own)).astype(f32)
                        sigmoid = sigmoid - match
                    slopes_ref[done : done + chunk.shape[0], left : left + count] = sigmoid.astype(bf16)
                    if losses:
                        log_raised = jnp.log(raised) + (shrunk - (raised - 1.0)) * inverse
                        softplus = jnp.maximum(logits, 0.0) + log_raised
                        if match is not None:
                            softplus = softplus - match * logits
                        total = total + jnp.sum(softplus, axis=0, keepdims=True)
                    done += chunk.shape[0]
            totals.append(total)
            left += count
    return jnp.concatenate(totals, axis=1)


def unit_kernel(*refs):
    for raw, emb in zip(refs[: len(refs) // 2], refs[len(refs) // 2 :]):
        emb[...] = unit_of(raw[...])[0].astype(bf16)


def copies_kernel(*refs):
    for source, target in zip(refs[: len(refs) // 2], refs[len(refs) // 2 :]):
        target[...] = source[...]


def own_rows_kernel(
    scale_ref, bias_ref, text_ref, image_ref, text_emb_ref, image_emb_ref, half_ref, text_out_ref, image_out_ref
):
    text_out_ref[...] = text_ref[...]
    image_out_ref[...] = image_ref[...]
    text_emb_ref[...] = unit_of(text_ref[...])[0].astype(bf16)
    emb = unit_of(image_ref[...])[0].astype(bf16)
    image_emb_ref[...] = emb
    half_ref[...] = emb[emb.shape[0] // 2 :, :]


def near_kernel(raw, *refs):
    out_ref, start = refs[-1], 0
    for place, block in enumerate(refs[:-1]):
        count = block.shape[0]
        out_ref[start : start + count, :] = unit_of(block[...])[0].astype(bf16) if place in raw else block[...]
        start += count


def join_kernel(*refs):
    count = len(refs) // 3
    for first, second, out in zip(refs[:count], refs[count : 2 * count], refs[2 * count :]):
        rows = first.shape[0]
        out[:rows, :] = first[...]
        out[rows:, :] = second[...]


def near_pairs_kernel(own, scale_ref, bias_ref, near_ref, far_ref, images_ref, *refs):
    slopes_ref, loss_ref = refs[-2:]
    rows = far_ref.shape[0]
    texts = (near_ref, far_ref)
    loss = pair_terms(
        scale_ref[0], bias_ref[0], texts, (images_ref,), slopes_ref, rows if own else 0
    )
    loss_ref[...] = loss if own else loss + refs[0][...]


def loss_rows(loss):
    high = loss.astype(bf16).astype(f32)
    which = lax.broadcasted_iota(jnp.int32, (extra, loss.shape[1]), 0)
    return jnp.where(which == 0, high, loss - high).astype(bf16)


def sums_in_parts(slope_refs, text_refs, width):
    step = 3 * lanes
    for left in range(0, width, step):
        total = None
        for slopes, texts in zip(slope_refs, text_refs):
            done = 0
            for block in texts:
                part = lax.dot_general(
                    slopes[done : done + block.shape[0], :],
                    block[:, left : left + step],
                    (((0,), (0,)), ((), ())),
                    preferred_element_type=f32,
                )
                total, done = part if total is None else total + part, done + block.shape[0]
        yield left, step, total


def put_panels(out, rows, left, sums):
    for at in range(0, sums.shape[1], lanes):
        panel = (left + at) // lanes
        out[panel * rows : (panel + 1) * rows, :] = sums[:, at : at + lanes].astype(out.dtype)


def far_kernel(count, scale_ref, bias_ref, near_ref, far_ref, near_swapped_ref, far_swapped_ref, *refs):
    image_refs, (own_slopes_ref, *sent_refs), other_slopes_ref = refs[:count], refs[count:-1], refs[-1]
    rows, width = far_ref.shape
    scale, offset = scale_ref[0], bias_ref[0]
    own_texts = (near_ref, far_ref)
    other_texts = (near_swapped_ref, far_swapped_ref)
    loss = pair_terms(scale, offset, own_texts, image_refs, own_slopes_ref)
    loss = loss + pair_terms(scale, offset, other_texts, image_refs, other_slopes_ref)
    slopes = (own_slopes_ref, other_slopes_ref)
    for left, step, total in sums_in_parts(slopes, (own_texts, other_texts), width):
        for place, out in enumerate(sent_refs):
            put_panels(out, rows, left, total[place * rows : (place + 1) * rows, :])
    for place, out in enumerate(sent_refs):
        out[width // lanes * rows :, :] = loss_rows(loss[:, place * rows : (place + 1) * rows])


def near_sums_kernel(
    plain, own_slopes_ref, other_slopes_ref, near_ref, far_ref, near_swapped_ref, far_swapped_ref, loss_ref, *refs
):
    own_ref, own_loss_ref, plain_refs, rest = refs[0], refs[1], refs[2 : 2 + plain], refs[2 + plain :]
    z_refs, z_loss_refs = rest[::2], rest[1::2]
    rows, width = far_ref.shape
    own_texts = (near_ref, far_ref)
    other_texts = (near_swapped_ref, far_swapped_ref)
    slopes = (own_slopes_ref, other_slopes_ref)
    for left, step, total in sums_in_parts(slopes, (own_texts, other_texts), width):
        own_ref[:, left : left + step] = total[:rows, :]
        for place, out in enumerate((*plain_refs, *z_refs), 1):
            put_panels(out, rows, left, total[place * rows : (place + 1) * rows, :])
    own_loss_ref[...] = loss_ref[:, :rows]
    for place, out in enumerate(plain_refs, 1):
        out[width // lanes * rows :, :] = loss_rows(loss_ref[:, place * rows : (place + 1) * rows])
    for place, out in enumerate(z_loss_refs, 1 + plain):
        out[...] = loss_ref[:, place * rows : (place + 1) * rows]


def swapped_pairs_kernel(scale_ref, bias_ref, near_ref, far_ref, images_ref, slopes_ref):
    pair_terms(scale_ref[0], bias_ref[0], (near_ref, far_ref), (images_ref,), slopes_ref, losses=False)


def text_kernel(
    count,
    scale_ref,
    bias_ref,
    near_ref,
    far_ref,
    images_ref,
    images_swapped_ref,
    near_slopes_ref,
    far_slopes_ref,
    other_slopes_ref,
    *refs,
):
    far_refs, far_swapped_refs, outs, slopes_ref = refs[:count], refs[count : 2 * count], refs[2 * count : -1], refs[-1]
    rows, width = far_ref.shape
    own_texts = (near_ref, far_ref)
    pair_terms(scale_ref[0], bias_ref[0], own_texts, far_swapped_refs, slopes_ref, losses=False)
    terms = []
    for slopes, blocks in (
        (near_slopes_ref, (images_ref,)),
        (other_slopes_ref, (images_swapped_ref,)),
        (far_slopes_ref, far_refs),
        (slopes_ref, far_swapped_refs),
    ):
        left = 0
        for images in blocks:
            terms.append((slopes.at[:, left : left + images.shape[0]], images))
            left += images.shape[0]
    step = 3 * lanes
    for left in range(0, width, step):
        total = None
        for slopes, images in terms:
            part = jnp.dot(slopes[...], images[:, left : left + step], preferred_element_type=f32)
            total = part if total is None else total + part
        for k, out in enumerate(outs):
            out[:, left : left + step] = total[k * rows : (k + 1) * rows, :].astype(out.dtype)


def late_image_kernel(zs, ys, *refs):
    sums, losses, parts, outs = refs[:zs], refs[zs : 2 * zs], refs[2 * zs : -zs], refs[-zs:]
    for k in range(zs):
        height = sums[k].shape[0]
        total, loss = sums[k][...], losses[k][...]
        for part in parts[k * ys : (k + 1) * ys]:
            total = total + part[:height, :].astype(f32)
            last = part[height:, :].astype(f32)
            loss = loss + (last[0:1, :] + last[1:2, :])
        outs[k][:height, :] = total.astype(bf16)
        outs[k][height:, :] = loss_rows(loss)


def late_text_kernel(sums_ref, part_ref, *refs):
    count = len(refs) // 2
    refs[count][...] = (sums_ref[...] + part_ref[...].astype(f32)).astype(bf16)
    for source, target in zip(refs[:count], refs[count + 1 :]):
        target[...] = source[...]


def row_gradient(rows, sums, scale, out_ref):
    unit_rows, inverse = unit_of(rows)
    unit_grad = scale * sums
    out_ref[...] = (
        unit_grad - unit_rows * jnp.sum(unit_rows * unit_grad, axis=-1, keepdims=True)
    ) * inverse


def part_sums_kernel(grad_ref, loss_ref, *refs):
    parts, (sums_ref, out_loss_ref) = refs[:-2], refs[-2:]
    rows, width = grad_ref.shape
    loss = loss_ref[...]
    for panel in range(width // lanes):
        cut = slice(panel * lanes, (panel + 1) * lanes)
        sums = grad_ref[:, cut]
        for part in parts:
            sums = sums + part[panel * rows : (panel + 1) * rows, :].astype(f32)
        sums_ref[:, cut] = sums
    for part in parts:
        last = part[width // lanes * rows :, :].astype(f32)
        loss = loss + (last[0:1, :] + last[1:2, :])
    out_loss_ref[...] = loss


def image_end_kernel(batch, scale_ref, image_ref, grad_ref, loss_ref, *refs):
    parts, (out_ref, out_loss_ref, sums_ref) = refs[:-3], refs[-3:]
    part_sums_kernel(grad_ref, loss_ref, *parts, sums_ref, out_loss_ref)
    row_gradient(image_ref[...], sums_ref[...], scale_ref[0], out_ref)
    out_loss_ref[...] = out_loss_ref[...] / batch


def text_end_kernel(scale_ref, text_ref, grad_ref, *refs):
    sums = grad_ref[...]
    for r in refs[:-1]:
        sums = sums + r[...].astype(f32)
    row_gradient(text_ref[...], sums, scale_ref[0], refs[-1])


def body(image, text, logarithm_scale, bias):
    rows, width = image.shape
    dp_count, inner_count = lax.axis_size("dp"), lax.axis_size("inner")
    batch = rows * dp_count * inner_count
    scale = jnp.exp(logarithm_scale)
    block = shape((rows, width), bf16)
    wide_block = shape((rows, width), f32)

    image_dp, image_inner = range(4, dp_count, 4), range(2, inner_count, 2)

    half_block = shape((rows // 2, width), bf16)
    text_z = swapped(text, "inner", 1)
    text_x = swapped(text, "dp", 2)
    first_half = image[: rows // 2]
    first_z = [swapped(first_half, "inner", q) for q in image_inner]
    images_y = [swapped(image, "dp", p) for p in image_dp]
    text_emb, image_emb, second_half, text_rows, image_rows = call(
        own_rows_kernel, [block, block, half_block, block, block], scale, bias, text, image, scalars=2
    )
    second_z = [swapped(second_half, "inner", q) for q in image_inner]
    zs, ys = len(first_z), len(images_y)

    (text_z_emb,) = call(unit_kernel, [block], text_z, weight=weights["x"], after=[text_x, second_half])
    near_texts = call(
        functools.partial(near_kernel, frozenset({1})),
        shape((3 * rows, width), bf16),
        text_emb,
        text_x,
        text_z_emb,
    )
    texts_swapped = swapped(near_texts, "dp", 1)
    far_places = [(p, q) for q in image_inner for p in image_dp]
    first_z = call(
        unit_kernel, [half_block] * zs, *first_z, weight=weights["a"], after=[text_z_emb, *images_y]
    )
    first_far = [swapped(emb, "dp", p) for emb in first_z for p in image_dp]
    second_z = call(copies_kernel, [half_block] * zs, *second_z, weight=weights["b"], after=[*first_z, texts_swapped])
    (far_text,) = call(copies_kernel, [block], swapped(text_z_emb, "dp", 2), weight=weights["x far"], after=second_z)
    first_far = call(
        copies_kernel, [half_block] * (zs * ys), *first_far, weight=weights["y far"], after=[far_text]
    )
    second_far = [swapped(emb, "dp", p) for emb in second_z for p in image_dp]

    near_images = call(
        functools.partial(near_kernel, frozenset(range(1, 1 + ys))),
        shape(((1 + ys + zs) * rows, width), bf16),
        image_emb,
        *images_y,
        *(part for both in zip(first_z, second_z) for part in both),
    )
    images_swapped = swapped(near_images, "dp", 1)
    far_text_swapped = swapped(far_text, "dp", 1)

    half, near_rows, far_rows = 4 * rows, (1 + ys + zs) * rows, zs * ys * rows
    own_texts, other_texts = (near_texts, far_text), (texts_swapped, far_text_swapped)
    pair_flops = 2 * rows * half * width
    near_slopes, near_loss = shape((half, near_rows), bf16), shape((1, near_rows), f32)
    payload = shape((width // lanes * rows + extra, lanes), bf16)
    own_slopes, loss = call(
        functools.partial(near_pairs_kernel, True),
        (near_slopes, near_loss),
        scale,
        bias,
        *own_texts,
        near_images,
        flops=pair_flops * (1 + ys + zs),
        scalars=2,
    )
    swapped_slopes = call(
        swapped_pairs_kernel,
        near_slopes,
        scale,
        bias,
        *own_texts,
        images_swapped,
        flops=pair_flops * (1 + ys + zs),
        scalars=2,
        after=[own_slopes],
    )
    far = call(join_kernel, [block] * (zs * ys), *first_far, *second_far, after=[swapped_slopes])
    far_swapped = [swapped(emb, "dp", 1) for emb in far]
    far_slopes, *far_sent = call(
        functools.partial(far_kernel, len(far)),
        [shape((half, far_rows), bf16)] + [payload] * len(far),
        scale,
        bias,
        *own_texts,
        *other_texts,
        *far,
        flops=4 * pair_flops * len(far),
        scalars=2,
        scratch=[pltpu.VMEM((half, far_rows), bf16)],
        after=[swapped_slopes],
    )
    moved = [swapped(part, "dp", p) for part, (p, q) in zip(far_sent, far_places)]
    text_grad, text_x_sums, text_z_sums, text_xz_sums = call(
        functools.partial(text_kernel, len(far)),
        (wide_block, block, wide_block, block),
        scale,
        bias,
        *own_texts,
        near_images,
        images_swapped,
        own_slopes,
        far_slopes,
        swapped_slopes,
        *far,
        *far_swapped,
        flops=3 * pair_flops * (1 + ys + zs + len(far)),
        scalars=2,
        scratch=[pltpu.VMEM((half, far_rows), bf16)],
        after=far_sent[:1],
    )
    moved_text = swapped(text_xz_sums, "dp", 2)
    other_slopes, loss = call(
        functools.partial(near_pairs_kernel, False),
        (near_slopes, near_loss),
        scale,
        bias,
        *other_texts,
        near_images,
        loss,
        flops=pair_flops * (1 + ys + zs),
        scalars=2,
        after=[text_x_sums],
    )
    image_grad, own_loss, *sums = call(
        functools.partial(near_sums_kernel, ys),
        [wide_block, shape((1, rows), f32)]
        + [payload] * ys
        + [shape((width // lanes * rows, lanes), f32), shape((1, rows), f32)] * zs,
        own_slopes,
        other_slopes,
        *own_texts,
        *other_texts,
        loss,
        flops=2 * pair_flops * (1 + ys + zs),
        after=[text_x_sums],
    )

    late = call(
        functools.partial(late_image_kernel, zs, ys),
        [payload] * zs,
        *sums[ys::2],
        *sums[ys + 1 :: 2],
        *moved,
        weight=weights["late"],
    )
    z_parts = [swapped(part, "inner", q) for part, q in zip(late, image_inner)]
    image_grad, own_loss = call(
        part_sums_kernel, (wide_block, shape((1, rows), f32)), image_grad, own_loss, *z_parts, weight=weights["end"]
    )
    late_text_z, late_text_x, *late_y = call(
        late_text_kernel,
        [block, block] + [payload] * ys,
        text_z_sums,
        moved_text,
        text_x_sums,
        *sums[:ys],
        weight=weights["text"],
        after=late[:1],
    )
    image_parts = [swapped(part, "dp", p) for part, p in zip(late_y, image_dp)]
    text_parts = [swapped(late_text_z, "inner", 1), swapped(late_text_x, "dp", 2)]

    image_gradient, image_loss = call(
        functools.partial(image_end_kernel, batch),
        (wide_block, shape((1, rows), f32)),
        scale,
        image_rows,
        image_grad,
        own_loss,
        *image_parts,
        scalars=1,
        scratch=[pltpu.VMEM((rows, width), f32)],
    )
    text_gradient = call(
        text_end_kernel, wide_block, scale, text_rows, text_grad, *text_parts, scalars=1, after=[image_gradient]
    )
    return (image_gradient, text_gradient, image_loss.reshape(rows))


def solution(mesh):
    return jax.shard_map(
        body,
        mesh=mesh,
        in_specs=(P(("dp", "inner"), None), P(("dp", "inner"), None), P(), P()),
        out_specs=(P(("dp", "inner"), None), P(("dp", "inner"), None), P(("dp", "inner"))),
        check_vma=False,
    )
```

```python
import functools

import jax
import jax.numpy as jnp
from jax import lax
from jax.experimental import pallas as pl
from jax.experimental.pallas import tpu as pltpu
from jax.sharding import PartitionSpec as P

epsilon = 1e-06
f32, bf16 = jnp.float32, jnp.bfloat16
lanes = 128
extra = 16
weights = {"x far": 10, "y far": 10, "x": 0, "a": 10, "b": 10, "late": 2, "gate": 2, "end": 2}
VMEM = pl.BlockSpec(memory_space=pltpu.VMEM)
SMEM = pl.BlockSpec(memory_space=pltpu.SMEM)
ANY = pl.BlockSpec(memory_space=pl.ANY)


def swapped(value, axis, step):
    return lax.ppermute(value, axis, [(place, place ^ step) for place in range(lax.axis_size(axis))])


def swapped_both(value, dp_step, inner_step):
    dp_count, inner_count = lax.axis_size("dp"), lax.axis_size("inner")
    pairs = [
        (d * inner_count + i, (d ^ dp_step) * inner_count + (i ^ inner_step))
        for d in range(dp_count)
        for i in range(inner_count)
    ]
    return lax.ppermute(value, ("dp", "inner"), pairs)


def call(kernel, out_shape, *operands, flops=0, weight=0, scalars=0, scratch=(), after=()):
    moved = sum(o.size * o.dtype.itemsize for o in operands)
    moved += sum(o.size * o.dtype.itemsize for o in jax.tree.leaves(out_shape))
    first, last = len(operands), len(operands) + len(after)
    return pl.pallas_call(
        lambda *refs: kernel(*refs[:first], *refs[last:]),
        out_shape=out_shape,
        in_specs=[SMEM] * scalars + [VMEM] * (len(operands) - scalars) + [ANY] * len(after),
        out_specs=jax.tree.map(lambda _: VMEM, out_shape),
        scratch_shapes=scratch,
        compiler_params=pltpu.CompilerParams(vmem_limit_bytes=40 * 1024 * 1024),
        cost_estimate=pl.CostEstimate(
            flops=flops + int(weight * 1e9), bytes_accessed=moved, transcendentals=0
        ),
    )(*operands, *after)


def shape(dims, kind):
    return jax.ShapeDtypeStruct(dims, kind)


def unit_of(rows):
    wide = rows.astype(f32)
    inverse = lax.rsqrt(jnp.sum(wide * wide, axis=-1, keepdims=True) + epsilon)
    return wide * inverse, inverse


def pair_terms(scale, offset, text_refs, image_refs, slopes_ref, own=0, losses=True):
    step = 256
    totals, left = [], 0
    for image_rows in image_refs:
        for at in range(0, image_rows.shape[0], step):
            images = image_rows[at : min(at + step, image_rows.shape[0]), :]
            count = images.shape[0]
            total, done = jnp.zeros((1, count), f32), 0
            for texts in text_refs:
                for start in range(0, texts.shape[0], step):
                    chunk = texts[start : min(start + step, texts.shape[0]), :]
                    logits = (
                        scale
                        * lax.dot_general(
                            chunk, images, (((1,), (1,)), ((), ())), preferred_element_type=f32
                        )
                        + offset
                    )
                    shrunk = jnp.exp(-jnp.abs(logits))
                    raised = 1.0 + shrunk
                    inverse = pl.reciprocal(raised, approx=True)
                    inverse = inverse * (2.0 - raised * inverse)
                    sigmoid = jnp.where(logits >= 0.0, inverse, shrunk * inverse)
                    match = None
                    if own and done == 0 and left == 0:
                        text_ids = lax.broadcasted_iota(jnp.int32, logits.shape, 0)
                        image_ids = lax.broadcasted_iota(jnp.int32, logits.shape, 1)
                        match = ((text_ids == image_ids) & (text_ids < own)).astype(f32)
                        sigmoid = sigmoid - match
                    slopes_ref[done : done + chunk.shape[0], left : left + count] = sigmoid.astype(bf16)
                    if losses:
                        log_raised = jnp.log(raised) + (shrunk - (raised - 1.0)) * inverse
                        softplus = jnp.maximum(logits, 0.0) + log_raised
                        if match is not None:
                            softplus = softplus - match * logits
                        total = total + jnp.sum(softplus, axis=0, keepdims=True)
                    done += chunk.shape[0]
            totals.append(total)
            left += count
    return jnp.concatenate(totals, axis=1)


def unit_kernel(*refs):
    for raw, emb in zip(refs[: len(refs) // 2], refs[len(refs) // 2 :]):
        emb[...] = unit_of(raw[...])[0].astype(bf16)


def copies_kernel(*refs):
    for source, target in zip(refs[: len(refs) // 2], refs[len(refs) // 2 :]):
        target[...] = source[...]


def own_rows_kernel(
    scale_ref, bias_ref, text_ref, image_ref, text_emb_ref, image_emb_ref, half_ref, text_out_ref, image_out_ref
):
    text_out_ref[...] = text_ref[...]
    image_out_ref[...] = image_ref[...]
    text_emb_ref[...] = unit_of(text_ref[...])[0].astype(bf16)
    emb = unit_of(image_ref[...])[0].astype(bf16)
    image_emb_ref[...] = emb
    half_ref[...] = emb[emb.shape[0] // 2 :, :]


def near_kernel(raw, *refs):
    out_ref, start = refs[-1], 0
    for place, block in enumerate(refs[:-1]):
        count = block.shape[0]
        out_ref[start : start + count, :] = unit_of(block[...])[0].astype(bf16) if place in raw else block[...]
        start += count


def join_kernel(*refs):
    count = len(refs) // 3
    for first, second, out in zip(refs[:count], refs[count : 2 * count], refs[2 * count :]):
        rows = first.shape[0]
        out[:rows, :] = first[...]
        out[rows:, :] = second[...]


def near_pairs_kernel(own, scale_ref, bias_ref, near_ref, far_ref, images_ref, *refs):
    slopes_ref, loss_ref = refs[-2:]
    rows = far_ref.shape[0]
    texts = (near_ref, far_ref)
    loss = pair_terms(
        scale_ref[0], bias_ref[0], texts, (images_ref,), slopes_ref, rows if own else 0
    )
    loss_ref[...] = loss if own else loss + refs[0][...]


def loss_rows(loss):
    high = loss.astype(bf16).astype(f32)
    which = lax.broadcasted_iota(jnp.int32, (extra, loss.shape[1]), 0)
    return jnp.where(which == 0, high, loss - high).astype(bf16)


def sums_in_parts(slope_refs, text_refs, width):
    step = 3 * lanes
    for left in range(0, width, step):
        total = None
        for slopes, texts in zip(slope_refs, text_refs):
            done = 0
            for block in texts:
                part = lax.dot_general(
                    slopes[done : done + block.shape[0], :],
                    block[:, left : left + step],
                    (((0,), (0,)), ((), ())),
                    preferred_element_type=f32,
                )
                total, done = part if total is None else total + part, done + block.shape[0]
        yield left, step, total


def put_panels(out, rows, left, sums):
    for at in range(0, sums.shape[1], lanes):
        panel = (left + at) // lanes
        out[panel * rows : (panel + 1) * rows, :] = sums[:, at : at + lanes].astype(out.dtype)


def far_kernel(count, scale_ref, bias_ref, near_ref, far_ref, near_swapped_ref, far_swapped_ref, *refs):
    image_refs, (own_slopes_ref, *sent_refs), other_slopes_ref = refs[:count], refs[count:-1], refs[-1]
    rows, width = far_ref.shape
    scale, offset = scale_ref[0], bias_ref[0]
    own_texts = (near_ref, far_ref)
    other_texts = (near_swapped_ref, far_swapped_ref)
    loss = pair_terms(scale, offset, own_texts, image_refs, own_slopes_ref)
    loss = loss + pair_terms(scale, offset, other_texts, image_refs, other_slopes_ref)
    slopes = (own_slopes_ref, other_slopes_ref)
    for left, step, total in sums_in_parts(slopes, (own_texts, other_texts), width):
        for place, out in enumerate(sent_refs):
            put_panels(out, rows, left, total[place * rows : (place + 1) * rows, :])
    for place, out in enumerate(sent_refs):
        out[width // lanes * rows :, :] = loss_rows(loss[:, place * rows : (place + 1) * rows])


def near_sums_kernel(
    plain, own_slopes_ref, other_slopes_ref, near_ref, far_ref, near_swapped_ref, far_swapped_ref, loss_ref, *refs
):
    own_ref, own_loss_ref, plain_refs, rest = refs[0], refs[1], refs[2 : 2 + plain], refs[2 + plain :]
    z_refs, z_loss_refs = rest[::2], rest[1::2]
    rows, width = far_ref.shape
    own_texts = (near_ref, far_ref)
    other_texts = (near_swapped_ref, far_swapped_ref)
    slopes = (own_slopes_ref, other_slopes_ref)
    for left, step, total in sums_in_parts(slopes, (own_texts, other_texts), width):
        own_ref[:, left : left + step] = total[:rows, :]
        for place, out in enumerate((*plain_refs, *z_refs), 1):
            put_panels(out, rows, left, total[place * rows : (place + 1) * rows, :])
    own_loss_ref[...] = loss_ref[:, :rows]
    for place, out in enumerate(plain_refs, 1):
        out[width // lanes * rows :, :] = loss_rows(loss_ref[:, place * rows : (place + 1) * rows])
    for place, out in enumerate(z_loss_refs, 1 + plain):
        out[...] = loss_ref[:, place * rows : (place + 1) * rows]


def swapped_pairs_kernel(scale_ref, bias_ref, near_ref, far_ref, images_ref, slopes_ref):
    pair_terms(scale_ref[0], bias_ref[0], (near_ref, far_ref), (images_ref,), slopes_ref, losses=False)


def text_kernel(
    count,
    scale_ref,
    bias_ref,
    near_ref,
    far_ref,
    images_ref,
    images_swapped_ref,
    near_slopes_ref,
    far_slopes_ref,
    other_slopes_ref,
    *refs,
):
    far_refs, far_swapped_refs, outs, slopes_ref = refs[:count], refs[count : 2 * count], refs[2 * count : -1], refs[-1]
    rows, width = far_ref.shape
    own_texts = (near_ref, far_ref)
    pair_terms(scale_ref[0], bias_ref[0], own_texts, far_swapped_refs, slopes_ref, losses=False)
    terms = []
    for slopes, blocks in (
        (near_slopes_ref, (images_ref,)),
        (other_slopes_ref, (images_swapped_ref,)),
        (far_slopes_ref, far_refs),
        (slopes_ref, far_swapped_refs),
    ):
        left = 0
        for images in blocks:
            terms.append((slopes.at[:, left : left + images.shape[0]], images))
            left += images.shape[0]
    step = 3 * lanes
    for left in range(0, width, step):
        total = None
        for slopes, images in terms:
            part = jnp.dot(slopes[...], images[:, left : left + step], preferred_element_type=f32)
            total = part if total is None else total + part
        for k, out in enumerate(outs):
            out[:, left : left + step] = total[k * rows : (k + 1) * rows, :].astype(out.dtype)


def late_image_kernel(zs, ys, *refs):
    sums, losses, parts, outs = refs[:zs], refs[zs : 2 * zs], refs[2 * zs : -zs], refs[-zs:]
    for k in range(zs):
        height = sums[k].shape[0]
        total, loss = sums[k][...], losses[k][...]
        for part in parts[k * ys : (k + 1) * ys]:
            total = total + part[:height, :].astype(f32)
            last = part[height:, :].astype(f32)
            loss = loss + (last[0:1, :] + last[1:2, :])
        outs[k][:height, :] = total.astype(bf16)
        outs[k][height:, :] = loss_rows(loss)


def gate_kernel(out_ref):
    out_ref[...] = jnp.zeros_like(out_ref)


def row_gradient(rows, sums, scale, out_ref):
    unit_rows, inverse = unit_of(rows)
    unit_grad = scale * sums
    out_ref[...] = (
        unit_grad - unit_rows * jnp.sum(unit_rows * unit_grad, axis=-1, keepdims=True)
    ) * inverse


def part_sums_kernel(grad_ref, loss_ref, *refs):
    parts, (sums_ref, out_loss_ref) = refs[:-2], refs[-2:]
    rows, width = grad_ref.shape
    loss = loss_ref[...]
    for panel in range(width // lanes):
        cut = slice(panel * lanes, (panel + 1) * lanes)
        sums = grad_ref[:, cut]
        for part in parts:
            sums = sums + part[panel * rows : (panel + 1) * rows, :].astype(f32)
        sums_ref[:, cut] = sums
    for part in parts:
        last = part[width // lanes * rows :, :].astype(f32)
        loss = loss + (last[0:1, :] + last[1:2, :])
    out_loss_ref[...] = loss


def image_end_kernel(batch, scale_ref, image_ref, grad_ref, loss_ref, *refs):
    parts, (out_ref, out_loss_ref, sums_ref) = refs[:-3], refs[-3:]
    part_sums_kernel(grad_ref, loss_ref, *parts, sums_ref, out_loss_ref)
    row_gradient(image_ref[...], sums_ref[...], scale_ref[0], out_ref)
    out_loss_ref[...] = out_loss_ref[...] / batch


def text_end_kernel(scale_ref, text_ref, grad_ref, *refs):
    sums = grad_ref[...]
    for r in refs[:-1]:
        sums = sums + r[...].astype(f32)
    row_gradient(text_ref[...], sums, scale_ref[0], refs[-1])


def body(image, text, logarithm_scale, bias):
    rows, width = image.shape
    dp_count, inner_count = lax.axis_size("dp"), lax.axis_size("inner")
    batch = rows * dp_count * inner_count
    scale = jnp.exp(logarithm_scale)
    block = shape((rows, width), bf16)
    wide_block = shape((rows, width), f32)

    image_dp, image_inner = range(4, dp_count, 4), range(2, inner_count, 2)

    half_block = shape((rows // 2, width), bf16)
    text_z = swapped(text, "inner", 1)
    text_x = swapped(text, "dp", 2)
    first_half = image[: rows // 2]
    first_z = [swapped(first_half, "inner", q) for q in image_inner]
    images_y = [swapped(image, "dp", p) for p in image_dp]
    text_emb, image_emb, second_half, text_rows, image_rows = call(
        own_rows_kernel, [block, block, half_block, block, block], scale, bias, text, image, scalars=2
    )
    second_z = [swapped(second_half, "inner", q) for q in image_inner]
    zs, ys = len(first_z), len(images_y)

    (text_z_emb,) = call(unit_kernel, [block], text_z, weight=weights["x"], after=[text_x, second_half])
    near_texts = call(
        functools.partial(near_kernel, frozenset({1})),
        shape((3 * rows, width), bf16),
        text_emb,
        text_x,
        text_z_emb,
    )
    texts_swapped = swapped(near_texts, "dp", 1)
    far_places = [(p, q) for q in image_inner for p in image_dp]
    first_z = call(
        unit_kernel, [half_block] * zs, *first_z, weight=weights["a"], after=[text_z_emb, *images_y]
    )
    first_far = [swapped(emb, "dp", p) for emb in first_z for p in image_dp]
    second_z = call(copies_kernel, [half_block] * zs, *second_z, weight=weights["b"], after=[*first_z, texts_swapped])
    (far_text,) = call(copies_kernel, [block], swapped(text_z_emb, "dp", 2), weight=weights["x far"], after=second_z)
    first_far = call(
        copies_kernel, [half_block] * (zs * ys), *first_far, weight=weights["y far"], after=[far_text]
    )
    second_far = [swapped(emb, "dp", p) for emb in second_z for p in image_dp]

    near_images = call(
        functools.partial(near_kernel, frozenset(range(1, 1 + ys))),
        shape(((1 + ys + zs) * rows, width), bf16),
        image_emb,
        *images_y,
        *(part for both in zip(first_z, second_z) for part in both),
    )
    images_swapped = swapped(near_images, "dp", 1)
    far_text_swapped = swapped(far_text, "dp", 1)

    half, near_rows, far_rows = 4 * rows, (1 + ys + zs) * rows, zs * ys * rows
    own_texts, other_texts = (near_texts, far_text), (texts_swapped, far_text_swapped)
    pair_flops = 2 * rows * half * width
    near_slopes, near_loss = shape((half, near_rows), bf16), shape((1, near_rows), f32)
    payload = shape((width // lanes * rows + extra, lanes), bf16)
    own_slopes, loss = call(
        functools.partial(near_pairs_kernel, True),
        (near_slopes, near_loss),
        scale,
        bias,
        *own_texts,
        near_images,
        flops=pair_flops * (1 + ys + zs),
        scalars=2,
    )
    swapped_slopes = call(
        swapped_pairs_kernel,
        near_slopes,
        scale,
        bias,
        *own_texts,
        images_swapped,
        flops=pair_flops * (1 + ys + zs),
        scalars=2,
        after=[own_slopes],
    )
    far = call(join_kernel, [block] * (zs * ys), *first_far, *second_far, after=[swapped_slopes])
    far_swapped = [swapped(emb, "dp", 1) for emb in far]
    far_slopes, *far_sent = call(
        functools.partial(far_kernel, len(far)),
        [shape((half, far_rows), bf16)] + [payload] * len(far),
        scale,
        bias,
        *own_texts,
        *other_texts,
        *far,
        flops=4 * pair_flops * len(far),
        scalars=2,
        scratch=[pltpu.VMEM((half, far_rows), bf16)],
        after=[swapped_slopes],
    )
    moved = [swapped(part, "dp", p) for part, (p, q) in zip(far_sent, far_places)]
    text_grad, text_x_sums, text_z_sums, text_xz_sums = call(
        functools.partial(text_kernel, len(far)),
        (wide_block, block, block, block),
        scale,
        bias,
        *own_texts,
        near_images,
        images_swapped,
        own_slopes,
        far_slopes,
        swapped_slopes,
        *far,
        *far_swapped,
        flops=3 * pair_flops * (1 + ys + zs + len(far)),
        scalars=2,
        scratch=[pltpu.VMEM((half, far_rows), bf16)],
        after=far_sent[:1],
    )
    text_parts = [
        swapped_both(text_xz_sums, 2, 1),
        swapped(text_z_sums, "inner", 1),
        swapped(text_x_sums, "dp", 2),
    ]
    other_slopes, loss = call(
        functools.partial(near_pairs_kernel, False),
        (near_slopes, near_loss),
        scale,
        bias,
        *other_texts,
        near_images,
        loss,
        flops=pair_flops * (1 + ys + zs),
        scalars=2,
        after=[text_x_sums],
    )
    image_grad, own_loss, *sums = call(
        functools.partial(near_sums_kernel, ys),
        [wide_block, shape((1, rows), f32)]
        + [payload] * ys
        + [shape((width // lanes * rows, lanes), f32), shape((1, rows), f32)] * zs,
        own_slopes,
        other_slopes,
        *own_texts,
        *other_texts,
        loss,
        flops=2 * pair_flops * (1 + ys + zs),
        after=[text_x_sums],
    )

    late = call(
        functools.partial(late_image_kernel, zs, ys),
        [payload] * zs,
        *sums[ys::2],
        *sums[ys + 1 :: 2],
        *moved,
        weight=weights["late"],
    )
    z_parts = [swapped(part, "inner", q) for part, q in zip(late, image_inner)]
    gate = call(gate_kernel, shape((8, lanes), f32), weight=weights["gate"], after=text_parts[:2])
    image_grad, own_loss = call(
        part_sums_kernel, (wide_block, shape((1, rows), f32)), image_grad, own_loss, *z_parts, weight=weights["end"], after=[gate]
    )
    image_parts = [swapped(part, "dp", p) for part, p in zip(sums[:ys], image_dp)]

    image_gradient, image_loss = call(
        functools.partial(image_end_kernel, batch),
        (wide_block, shape((1, rows), f32)),
        scale,
        image_rows,
        image_grad,
        own_loss,
        *image_parts,
        scalars=1,
        scratch=[pltpu.VMEM((rows, width), f32)],
    )
    text_gradient = call(
        text_end_kernel, wide_block, scale, text_rows, text_grad, *text_parts, scalars=1, after=[image_gradient]
    )
    return (image_gradient, text_gradient, image_loss.reshape(rows))


def solution(mesh):
    return jax.shard_map(
        body,
        mesh=mesh,
        in_specs=(P(("dp", "inner"), None), P(("dp", "inner"), None), P(), P()),
        out_specs=(P(("dp", "inner"), None), P(("dp", "inner"), None), P(("dp", "inner"))),
        check_vma=False,
    )
```

```python
import functools

import jax
import jax.numpy as jnp
from jax import lax
from jax.experimental import pallas as pl
from jax.experimental.pallas import tpu as pltpu
from jax.sharding import PartitionSpec as P

epsilon = 1e-06
f32, bf16 = jnp.float32, jnp.bfloat16
lanes = 128
extra = 16
weights = {"x far": 10, "y far": 10, "x": 0, "a": 10, "b": 10, "late": 2, "gate": 2}
VMEM = pl.BlockSpec(memory_space=pltpu.VMEM)
SMEM = pl.BlockSpec(memory_space=pltpu.SMEM)
ANY = pl.BlockSpec(memory_space=pl.ANY)


def swapped(value, axis, step):
    return lax.ppermute(value, axis, [(place, place ^ step) for place in range(lax.axis_size(axis))])


def swapped_both(value, dp_step, inner_step):
    dp_count, inner_count = lax.axis_size("dp"), lax.axis_size("inner")
    pairs = [
        (d * inner_count + i, (d ^ dp_step) * inner_count + (i ^ inner_step))
        for d in range(dp_count)
        for i in range(inner_count)
    ]
    return lax.ppermute(value, ("dp", "inner"), pairs)


def call(kernel, out_shape, *operands, flops=0, weight=0, scalars=0, scratch=(), after=()):
    moved = sum(o.size * o.dtype.itemsize for o in operands)
    moved += sum(o.size * o.dtype.itemsize for o in jax.tree.leaves(out_shape))
    first, last = len(operands), len(operands) + len(after)
    return pl.pallas_call(
        lambda *refs: kernel(*refs[:first], *refs[last:]),
        out_shape=out_shape,
        in_specs=[SMEM] * scalars + [VMEM] * (len(operands) - scalars) + [ANY] * len(after),
        out_specs=jax.tree.map(lambda _: VMEM, out_shape),
        scratch_shapes=scratch,
        compiler_params=pltpu.CompilerParams(vmem_limit_bytes=40 * 1024 * 1024),
        cost_estimate=pl.CostEstimate(
            flops=flops + int(weight * 1e9), bytes_accessed=moved, transcendentals=0
        ),
    )(*operands, *after)


def shape(dims, kind):
    return jax.ShapeDtypeStruct(dims, kind)


def unit_of(rows):
    wide = rows.astype(f32)
    inverse = lax.rsqrt(jnp.sum(wide * wide, axis=-1, keepdims=True) + epsilon)
    return wide * inverse, inverse


def pair_terms(scale, offset, text_refs, image_refs, slopes_ref, own=0, losses=True):
    step = 256
    totals, left = [], 0
    for image_rows in image_refs:
        for at in range(0, image_rows.shape[0], step):
            images = image_rows[at : min(at + step, image_rows.shape[0]), :]
            count = images.shape[0]
            total, done = jnp.zeros((1, count), f32), 0
            for texts in text_refs:
                for start in range(0, texts.shape[0], step):
                    chunk = texts[start : min(start + step, texts.shape[0]), :]
                    logits = (
                        scale
                        * lax.dot_general(
                            chunk, images, (((1,), (1,)), ((), ())), preferred_element_type=f32
                        )
                        + offset
                    )
                    shrunk = jnp.exp(-jnp.abs(logits))
                    raised = 1.0 + shrunk
                    inverse = pl.reciprocal(raised, approx=True)
                    inverse = inverse * (2.0 - raised * inverse)
                    sigmoid = jnp.where(logits >= 0.0, inverse, shrunk * inverse)
                    match = None
                    if own and done == 0 and left == 0:
                        text_ids = lax.broadcasted_iota(jnp.int32, logits.shape, 0)
                        image_ids = lax.broadcasted_iota(jnp.int32, logits.shape, 1)
                        match = ((text_ids == image_ids) & (text_ids < own)).astype(f32)
                        sigmoid = sigmoid - match
                    slopes_ref[done : done + chunk.shape[0], left : left + count] = sigmoid.astype(bf16)
                    if losses:
                        log_raised = jnp.log(raised) + (shrunk - (raised - 1.0)) * inverse
                        softplus = jnp.maximum(logits, 0.0) + log_raised
                        if match is not None:
                            softplus = softplus - match * logits
                        total = total + jnp.sum(softplus, axis=0, keepdims=True)
                    done += chunk.shape[0]
            totals.append(total)
            left += count
    return jnp.concatenate(totals, axis=1)


def unit_kernel(*refs):
    for raw, emb in zip(refs[: len(refs) // 2], refs[len(refs) // 2 :]):
        emb[...] = unit_of(raw[...])[0].astype(bf16)


def copies_kernel(*refs):
    for source, target in zip(refs[: len(refs) // 2], refs[len(refs) // 2 :]):
        target[...] = source[...]


def own_rows_kernel(
    scale_ref, bias_ref, text_ref, image_ref, text_emb_ref, image_emb_ref, half_ref, text_out_ref, image_out_ref
):
    text_out_ref[...] = text_ref[...]
    image_out_ref[...] = image_ref[...]
    text_emb_ref[...] = unit_of(text_ref[...])[0].astype(bf16)
    emb = unit_of(image_ref[...])[0].astype(bf16)
    image_emb_ref[...] = emb
    half_ref[...] = emb[emb.shape[0] // 2 :, :]


def near_kernel(raw, *refs):
    out_ref, start = refs[-1], 0
    for place, block in enumerate(refs[:-1]):
        count = block.shape[0]
        out_ref[start : start + count, :] = unit_of(block[...])[0].astype(bf16) if place in raw else block[...]
        start += count


def join_kernel(*refs):
    count = len(refs) // 3
    for first, second, out in zip(refs[:count], refs[count : 2 * count], refs[2 * count :]):
        rows = first.shape[0]
        out[:rows, :] = first[...]
        out[rows:, :] = second[...]


def near_pairs_kernel(own, scale_ref, bias_ref, near_ref, far_ref, images_ref, *refs):
    slopes_ref, loss_ref = refs[-2:]
    rows = far_ref.shape[0]
    texts = (near_ref, far_ref)
    loss = pair_terms(
        scale_ref[0], bias_ref[0], texts, (images_ref,), slopes_ref, rows if own else 0
    )
    loss_ref[...] = loss if own else loss + refs[0][...]


def loss_rows(loss):
    high = loss.astype(bf16).astype(f32)
    which = lax.broadcasted_iota(jnp.int32, (extra, loss.shape[1]), 0)
    return jnp.where(which == 0, high, loss - high).astype(bf16)


def sums_in_parts(slope_refs, text_refs, width):
    step = 3 * lanes
    for left in range(0, width, step):
        total = None
        for slopes, texts in zip(slope_refs, text_refs):
            done = 0
            for block in texts:
                part = lax.dot_general(
                    slopes[done : done + block.shape[0], :],
                    block[:, left : left + step],
                    (((0,), (0,)), ((), ())),
                    preferred_element_type=f32,
                )
                total, done = part if total is None else total + part, done + block.shape[0]
        yield left, step, total


def put_panels(out, rows, left, sums):
    for at in range(0, sums.shape[1], lanes):
        panel = (left + at) // lanes
        out[panel * rows : (panel + 1) * rows, :] = sums[:, at : at + lanes].astype(out.dtype)


def far_kernel(count, scale_ref, bias_ref, near_ref, far_ref, near_swapped_ref, far_swapped_ref, *refs):
    image_refs, (own_slopes_ref, *sent_refs), other_slopes_ref = refs[:count], refs[count:-1], refs[-1]
    rows, width = far_ref.shape
    scale, offset = scale_ref[0], bias_ref[0]
    own_texts = (near_ref, far_ref)
    other_texts = (near_swapped_ref, far_swapped_ref)
    loss = pair_terms(scale, offset, own_texts, image_refs, own_slopes_ref)
    loss = loss + pair_terms(scale, offset, other_texts, image_refs, other_slopes_ref)
    slopes = (own_slopes_ref, other_slopes_ref)
    for left, step, total in sums_in_parts(slopes, (own_texts, other_texts), width):
        for place, out in enumerate(sent_refs):
            put_panels(out, rows, left, total[place * rows : (place + 1) * rows, :])
    for place, out in enumerate(sent_refs):
        out[width // lanes * rows :, :] = loss_rows(loss[:, place * rows : (place + 1) * rows])


def near_sums_kernel(
    plain, own_slopes_ref, other_slopes_ref, near_ref, far_ref, near_swapped_ref, far_swapped_ref, loss_ref, *refs
):
    own_ref, own_loss_ref, plain_refs, rest = refs[0], refs[1], refs[2 : 2 + plain], refs[2 + plain :]
    z_refs, z_loss_refs = rest[::2], rest[1::2]
    rows, width = far_ref.shape
    own_texts = (near_ref, far_ref)
    other_texts = (near_swapped_ref, far_swapped_ref)
    slopes = (own_slopes_ref, other_slopes_ref)
    for left, step, total in sums_in_parts(slopes, (own_texts, other_texts), width):
        own_ref[:, left : left + step] = total[:rows, :]
        for place, out in enumerate((*plain_refs, *z_refs), 1):
            put_panels(out, rows, left, total[place * rows : (place + 1) * rows, :])
    own_loss_ref[...] = loss_ref[:, :rows]
    for place, out in enumerate(plain_refs, 1):
        out[width // lanes * rows :, :] = loss_rows(loss_ref[:, place * rows : (place + 1) * rows])
    for place, out in enumerate(z_loss_refs, 1 + plain):
        out[...] = loss_ref[:, place * rows : (place + 1) * rows]


def swapped_pairs_kernel(scale_ref, bias_ref, near_ref, far_ref, images_ref, slopes_ref):
    pair_terms(scale_ref[0], bias_ref[0], (near_ref, far_ref), (images_ref,), slopes_ref, losses=False)


def text_kernel(
    count,
    scale_ref,
    bias_ref,
    near_ref,
    far_ref,
    images_ref,
    images_swapped_ref,
    near_slopes_ref,
    far_slopes_ref,
    other_slopes_ref,
    *refs,
):
    far_refs, far_swapped_refs, outs, slopes_ref = refs[:count], refs[count : 2 * count], refs[2 * count : -1], refs[-1]
    rows, width = far_ref.shape
    own_texts = (near_ref, far_ref)
    pair_terms(scale_ref[0], bias_ref[0], own_texts, far_swapped_refs, slopes_ref, losses=False)
    terms = []
    for slopes, blocks in (
        (near_slopes_ref, (images_ref,)),
        (other_slopes_ref, (images_swapped_ref,)),
        (far_slopes_ref, far_refs),
        (slopes_ref, far_swapped_refs),
    ):
        left = 0
        for images in blocks:
            terms.append((slopes.at[:, left : left + images.shape[0]], images))
            left += images.shape[0]
    step = 3 * lanes
    for left in range(0, width, step):
        total = None
        for slopes, images in terms:
            part = jnp.dot(slopes[...], images[:, left : left + step], preferred_element_type=f32)
            total = part if total is None else total + part
        for k, out in enumerate(outs):
            out[:, left : left + step] = total[k * rows : (k + 1) * rows, :].astype(out.dtype)


def late_image_kernel(zs, ys, *refs):
    sums, losses, refs = refs[:zs], refs[zs : 2 * zs], refs[2 * zs :]
    parts, payloads, outs = refs[: zs * ys], refs[zs * ys : zs * ys + ys], refs[zs * ys + ys :]
    for k in range(zs):
        height = sums[k].shape[0]
        total, loss = sums[k][...], losses[k][...]
        for part in parts[k * ys : (k + 1) * ys]:
            total = total + part[:height, :].astype(f32)
            last = part[height:, :].astype(f32)
            loss = loss + (last[0:1, :] + last[1:2, :])
        outs[k][:height, :] = total.astype(bf16)
        outs[k][height:, :] = loss_rows(loss)
    for source, target in zip(payloads, outs[zs:]):
        target[...] = source[...]


def gate_kernel(out_ref):
    out_ref[...] = jnp.zeros_like(out_ref)


def row_gradient(rows, sums, scale, out_ref):
    unit_rows, inverse = unit_of(rows)
    unit_grad = scale * sums
    out_ref[...] = (
        unit_grad - unit_rows * jnp.sum(unit_rows * unit_grad, axis=-1, keepdims=True)
    ) * inverse


def end_kernel(batch, images, scale_ref, image_ref, text_ref, grad_ref, loss_ref, text_grad_ref, *refs):
    parts, text_parts, (out_ref, text_out_ref, out_loss_ref, sums_ref) = refs[:images], refs[images:-4], refs[-4:]
    rows, width = image_ref.shape
    loss = loss_ref[...]
    for part in parts:
        last = part[width // lanes * rows :, :].astype(f32)
        loss = loss + (last[0:1, :] + last[1:2, :])
    out_loss_ref[...] = loss / batch
    for panel in range(width // lanes):
        cut = slice(panel * lanes, (panel + 1) * lanes)
        sums = grad_ref[:, cut]
        for part in parts:
            sums = sums + part[panel * rows : (panel + 1) * rows, :].astype(f32)
        sums_ref[:, cut] = sums
    row_gradient(image_ref[...], sums_ref[...], scale_ref[0], out_ref)
    sums = text_grad_ref[...]
    for part in text_parts:
        sums = sums + part[...].astype(f32)
    row_gradient(text_ref[...], sums, scale_ref[0], text_out_ref)


def body(image, text, logarithm_scale, bias):
    rows, width = image.shape
    dp_count, inner_count = lax.axis_size("dp"), lax.axis_size("inner")
    batch = rows * dp_count * inner_count
    scale = jnp.exp(logarithm_scale)
    block = shape((rows, width), bf16)
    wide_block = shape((rows, width), f32)

    image_dp, image_inner = range(4, dp_count, 4), range(2, inner_count, 2)

    half_block = shape((rows // 2, width), bf16)
    text_z = swapped(text, "inner", 1)
    text_x = swapped(text, "dp", 2)
    first_half = image[: rows // 2]
    first_z = [swapped(first_half, "inner", q) for q in image_inner]
    images_y = [swapped(image, "dp", p) for p in image_dp]
    text_emb, image_emb, second_half, text_rows, image_rows = call(
        own_rows_kernel, [block, block, half_block, block, block], scale, bias, text, image, scalars=2
    )
    second_z = [swapped(second_half, "inner", q) for q in image_inner]
    zs, ys = len(first_z), len(images_y)

    (text_z_emb,) = call(unit_kernel, [block], text_z, weight=weights["x"], after=[text_x, second_half])
    near_texts = call(
        functools.partial(near_kernel, frozenset({1})),
        shape((3 * rows, width), bf16),
        text_emb,
        text_x,
        text_z_emb,
    )
    texts_swapped = swapped(near_texts, "dp", 1)
    far_places = [(p, q) for q in image_inner for p in image_dp]
    first_z = call(
        unit_kernel, [half_block] * zs, *first_z, weight=weights["a"], after=[text_z_emb, *images_y]
    )
    first_far = [swapped(emb, "dp", p) for emb in first_z for p in image_dp]
    second_z = call(copies_kernel, [half_block] * zs, *second_z, weight=weights["b"], after=[*first_z, texts_swapped])
    (far_text,) = call(copies_kernel, [block], swapped(text_z_emb, "dp", 2), weight=weights["x far"], after=second_z)
    first_far = call(
        copies_kernel, [half_block] * (zs * ys), *first_far, weight=weights["y far"], after=[far_text]
    )
    second_far = [swapped(emb, "dp", p) for emb in second_z for p in image_dp]

    near_images = call(
        functools.partial(near_kernel, frozenset(range(1, 1 + ys))),
        shape(((1 + ys + zs) * rows, width), bf16),
        image_emb,
        *images_y,
        *(part for both in zip(first_z, second_z) for part in both),
    )
    images_swapped = swapped(near_images, "dp", 1)
    far_text_swapped = swapped(far_text, "dp", 1)

    half, near_rows, far_rows = 4 * rows, (1 + ys + zs) * rows, zs * ys * rows
    own_texts, other_texts = (near_texts, far_text), (texts_swapped, far_text_swapped)
    pair_flops = 2 * rows * half * width
    near_slopes, near_loss = shape((half, near_rows), bf16), shape((1, near_rows), f32)
    payload = shape((width // lanes * rows + extra, lanes), bf16)
    own_slopes, loss = call(
        functools.partial(near_pairs_kernel, True),
        (near_slopes, near_loss),
        scale,
        bias,
        *own_texts,
        near_images,
        flops=pair_flops * (1 + ys + zs),
        scalars=2,
    )
    swapped_slopes = call(
        swapped_pairs_kernel,
        near_slopes,
        scale,
        bias,
        *own_texts,
        images_swapped,
        flops=pair_flops * (1 + ys + zs),
        scalars=2,
        after=[own_slopes],
    )
    far = call(join_kernel, [block] * (zs * ys), *first_far, *second_far, after=[swapped_slopes])
    far_swapped = [swapped(emb, "dp", 1) for emb in far]
    far_slopes, *far_sent = call(
        functools.partial(far_kernel, len(far)),
        [shape((half, far_rows), bf16)] + [payload] * len(far),
        scale,
        bias,
        *own_texts,
        *other_texts,
        *far,
        flops=4 * pair_flops * len(far),
        scalars=2,
        scratch=[pltpu.VMEM((half, far_rows), bf16)],
        after=[swapped_slopes],
    )
    moved = [swapped(part, "dp", p) for part, (p, q) in zip(far_sent, far_places)]
    text_grad, text_x_sums, text_z_sums, text_xz_sums = call(
        functools.partial(text_kernel, len(far)),
        (wide_block, block, block, block),
        scale,
        bias,
        *own_texts,
        near_images,
        images_swapped,
        own_slopes,
        far_slopes,
        swapped_slopes,
        *far,
        *far_swapped,
        flops=3 * pair_flops * (1 + ys + zs + len(far)),
        scalars=2,
        scratch=[pltpu.VMEM((half, far_rows), bf16)],
        after=far_sent[:1],
    )
    text_parts = [
        swapped_both(text_xz_sums, 2, 1),
        swapped(text_z_sums, "inner", 1),
        swapped(text_x_sums, "dp", 2),
    ]
    other_slopes, loss = call(
        functools.partial(near_pairs_kernel, False),
        (near_slopes, near_loss),
        scale,
        bias,
        *other_texts,
        near_images,
        loss,
        flops=pair_flops * (1 + ys + zs),
        scalars=2,
        after=[text_x_sums],
    )
    image_grad, own_loss, *sums = call(
        functools.partial(near_sums_kernel, ys),
        [wide_block, shape((1, rows), f32)]
        + [payload] * ys
        + [shape((width // lanes * rows, lanes), f32), shape((1, rows), f32)] * zs,
        own_slopes,
        other_slopes,
        *own_texts,
        *other_texts,
        loss,
        flops=2 * pair_flops * (1 + ys + zs),
        after=[text_x_sums],
    )

    late = call(
        functools.partial(late_image_kernel, zs, ys),
        [payload] * (zs + ys),
        *sums[ys::2],
        *sums[ys + 1 :: 2],
        *moved,
        *sums[:ys],
        weight=weights["late"],
    )
    z_parts = [swapped(part, "inner", q) for part, q in zip(late, image_inner)]
    gate = call(gate_kernel, shape((8, lanes), f32), weight=weights["gate"], after=text_parts[:2])
    image_parts = [*z_parts, *(swapped(part, "dp", p) for part, p in zip(late[zs:], image_dp))]
    image_gradient, text_gradient, image_loss = call(
        functools.partial(end_kernel, batch, len(image_parts)),
        (wide_block, wide_block, shape((1, rows), f32)),
        scale,
        image_rows,
        text_rows,
        image_grad,
        own_loss,
        text_grad,
        *image_parts,
        *text_parts,
        scalars=1,
        scratch=[pltpu.VMEM((rows, width), f32)],
        after=[gate],
    )
    return (image_gradient, text_gradient, image_loss.reshape(rows))


def solution(mesh):
    return jax.shard_map(
        body,
        mesh=mesh,
        in_specs=(P(("dp", "inner"), None), P(("dp", "inner"), None), P(), P()),
        out_specs=(P(("dp", "inner"), None), P(("dp", "inner"), None), P(("dp", "inner"))),
        check_vma=False,
    )
```

```python
import functools

import jax
import jax.numpy as jnp
from jax import lax
from jax.experimental import pallas as pl
from jax.experimental.pallas import tpu as pltpu
from jax.sharding import PartitionSpec as P

epsilon = 1e-06
f32, bf16 = jnp.float32, jnp.bfloat16
lanes = 128
extra = 16
weights = {"x far": 10, "y far": 10, "x": 0, "a": 10, "b": 10, "late": 2, "gate": 2}
VMEM = pl.BlockSpec(memory_space=pltpu.VMEM)
SMEM = pl.BlockSpec(memory_space=pltpu.SMEM)
ANY = pl.BlockSpec(memory_space=pl.ANY)


def swapped(value, axis, step):
    return lax.ppermute(value, axis, [(place, place ^ step) for place in range(lax.axis_size(axis))])


def swapped_both(value, dp_step, inner_step):
    dp_count, inner_count = lax.axis_size("dp"), lax.axis_size("inner")
    pairs = [
        (d * inner_count + i, (d ^ dp_step) * inner_count + (i ^ inner_step))
        for d in range(dp_count)
        for i in range(inner_count)
    ]
    return lax.ppermute(value, ("dp", "inner"), pairs)


def call(kernel, out_shape, *operands, flops=0, weight=0, scalars=0, scratch=(), after=()):
    moved = sum(o.size * o.dtype.itemsize for o in operands)
    moved += sum(o.size * o.dtype.itemsize for o in jax.tree.leaves(out_shape))
    first, last = len(operands), len(operands) + len(after)
    return pl.pallas_call(
        lambda *refs: kernel(*refs[:first], *refs[last:]),
        out_shape=out_shape,
        in_specs=[SMEM] * scalars + [VMEM] * (len(operands) - scalars) + [ANY] * len(after),
        out_specs=jax.tree.map(lambda _: VMEM, out_shape),
        scratch_shapes=scratch,
        compiler_params=pltpu.CompilerParams(vmem_limit_bytes=40 * 1024 * 1024),
        cost_estimate=pl.CostEstimate(
            flops=flops + int(weight * 1e9), bytes_accessed=moved, transcendentals=0
        ),
    )(*operands, *after)


def shape(dims, kind):
    return jax.ShapeDtypeStruct(dims, kind)


def unit_of(rows):
    wide = rows.astype(f32)
    inverse = lax.rsqrt(jnp.sum(wide * wide, axis=-1, keepdims=True) + epsilon)
    return wide * inverse, inverse


def joined(refs):
    return refs[0][...] if len(refs) == 1 else jnp.concatenate([ref[...] for ref in refs], axis=0)


def pair_terms(scale, offset, text_refs, image_refs, slopes_ref, own=0, losses=True):
    texts, all_images = joined(text_refs), joined(image_refs)
    totals = []
    for left in range(0, all_images.shape[0], 256):
        images = all_images[left : min(left + 256, all_images.shape[0]), :]
        total = jnp.zeros((1, images.shape[0]), f32)
        for start in range(0, texts.shape[0], 256):
            logits = (
                scale
                * lax.dot_general(
                    texts[start : start + 256, :],
                    images,
                    (((1,), (1,)), ((), ())),
                    preferred_element_type=f32,
                )
                + offset
            )
            shrunk = jnp.exp(-jnp.abs(logits))
            raised = 1.0 + shrunk
            inverse = pl.reciprocal(raised, approx=True)
            inverse = inverse * (2.0 - raised * inverse)
            sigmoid = jnp.where(logits >= 0.0, inverse, shrunk * inverse)
            match = None
            if own and left == 0 and start < own:
                text_ids = start + lax.broadcasted_iota(jnp.int32, logits.shape, 0)
                image_ids = lax.broadcasted_iota(jnp.int32, logits.shape, 1)
                match = ((text_ids == image_ids) & (text_ids < own)).astype(f32)
                sigmoid = sigmoid - match
            slopes_ref[start : start + 256, left : left + images.shape[0]] = sigmoid.astype(bf16)
            if losses:
                log_raised = jnp.log(raised) + (shrunk - (raised - 1.0)) * inverse
                softplus = jnp.maximum(logits, 0.0) + log_raised
                if match is not None:
                    softplus = softplus - match * logits
                total = total + jnp.sum(softplus, axis=0, keepdims=True)
        totals.append(total)
    return jnp.concatenate(totals, axis=1) if losses else None


def unit_kernel(*refs):
    for raw, emb in zip(refs[: len(refs) // 2], refs[len(refs) // 2 :]):
        emb[...] = unit_of(raw[...])[0].astype(bf16)


def copies_kernel(*refs):
    for source, target in zip(refs[: len(refs) // 2], refs[len(refs) // 2 :]):
        target[...] = source[...]


def own_rows_kernel(
    scale_ref, bias_ref, text_ref, image_ref, text_emb_ref, image_emb_ref, half_ref, text_out_ref, image_out_ref
):
    text_out_ref[...] = text_ref[...]
    image_out_ref[...] = image_ref[...]
    text_emb_ref[...] = unit_of(text_ref[...])[0].astype(bf16)
    emb = unit_of(image_ref[...])[0].astype(bf16)
    image_emb_ref[...] = emb
    half_ref[...] = emb[emb.shape[0] // 2 :, :]


def near_kernel(raw, *refs):
    out_ref, start = refs[-1], 0
    for place, block in enumerate(refs[:-1]):
        count = block.shape[0]
        out_ref[start : start + count, :] = unit_of(block[...])[0].astype(bf16) if place in raw else block[...]
        start += count


def join_kernel(*refs):
    count = len(refs) // 3
    for first, second, out in zip(refs[:count], refs[count : 2 * count], refs[2 * count :]):
        rows = first.shape[0]
        out[:rows, :] = first[...]
        out[rows:, :] = second[...]


def near_pairs_kernel(own, scale_ref, bias_ref, near_ref, far_ref, images_ref, *refs):
    slopes_ref, loss_ref = refs[-2:]
    rows = far_ref.shape[0]
    texts = (near_ref, far_ref)
    loss = pair_terms(
        scale_ref[0], bias_ref[0], texts, (images_ref,), slopes_ref, rows if own else 0
    )
    loss_ref[...] = loss if own else loss + refs[0][...]


def loss_rows(loss):
    high = loss.astype(bf16).astype(f32)
    which = lax.broadcasted_iota(jnp.int32, (extra, loss.shape[1]), 0)
    return jnp.where(which == 0, high, loss - high).astype(bf16)


def column_cuts(width):
    step = 4 * lanes
    return [(left, min(step, width - left)) for left in range(0, width, step)]


def sums_in_parts(slope_refs, text_refs, width):
    for left, step in column_cuts(width):
        total = None
        for slopes, texts in zip(slope_refs, text_refs):
            part = lax.dot_general(
                slopes[...],
                joined([block.at[:, left : left + step] for block in texts]),
                (((0,), (0,)), ((), ())),
                preferred_element_type=f32,
            )
            total = part if total is None else total + part
        yield left, step, total


def put_panels(out, rows, left, sums):
    for at in range(0, sums.shape[1], lanes):
        panel = (left + at) // lanes
        out[panel * rows : (panel + 1) * rows, :] = sums[:, at : at + lanes].astype(out.dtype)


def far_kernel(count, scale_ref, bias_ref, near_ref, far_ref, near_swapped_ref, far_swapped_ref, *refs):
    image_refs, (own_slopes_ref, *sent_refs), other_slopes_ref = refs[:count], refs[count:-1], refs[-1]
    rows, width = far_ref.shape
    scale, offset = scale_ref[0], bias_ref[0]
    own_texts = (near_ref, far_ref)
    other_texts = (near_swapped_ref, far_swapped_ref)
    loss = pair_terms(scale, offset, own_texts, image_refs, own_slopes_ref)
    loss = loss + pair_terms(scale, offset, other_texts, image_refs, other_slopes_ref)
    slopes = (own_slopes_ref, other_slopes_ref)
    for left, step, total in sums_in_parts(slopes, (own_texts, other_texts), width):
        for place, out in enumerate(sent_refs):
            put_panels(out, rows, left, total[place * rows : (place + 1) * rows, :])
    for place, out in enumerate(sent_refs):
        out[width // lanes * rows :, :] = loss_rows(loss[:, place * rows : (place + 1) * rows])


def near_sums_kernel(
    plain, own_slopes_ref, other_slopes_ref, near_ref, far_ref, near_swapped_ref, far_swapped_ref, loss_ref, *refs
):
    own_ref, own_loss_ref, plain_refs, rest = refs[0], refs[1], refs[2 : 2 + plain], refs[2 + plain :]
    z_refs, z_loss_refs = rest[::2], rest[1::2]
    rows, width = far_ref.shape
    own_texts = (near_ref, far_ref)
    other_texts = (near_swapped_ref, far_swapped_ref)
    slopes = (own_slopes_ref, other_slopes_ref)
    for left, step, total in sums_in_parts(slopes, (own_texts, other_texts), width):
        own_ref[:, left : left + step] = total[:rows, :]
        for place, out in enumerate((*plain_refs, *z_refs), 1):
            put_panels(out, rows, left, total[place * rows : (place + 1) * rows, :])
    own_loss_ref[...] = loss_ref[:, :rows]
    for place, out in enumerate(plain_refs, 1):
        out[width // lanes * rows :, :] = loss_rows(loss_ref[:, place * rows : (place + 1) * rows])
    for place, out in enumerate(z_loss_refs, 1 + plain):
        out[...] = loss_ref[:, place * rows : (place + 1) * rows]


def swapped_pairs_kernel(scale_ref, bias_ref, near_ref, far_ref, images_ref, slopes_ref):
    pair_terms(scale_ref[0], bias_ref[0], (near_ref, far_ref), (images_ref,), slopes_ref, losses=False)


def text_kernel(
    count,
    scale_ref,
    bias_ref,
    near_ref,
    far_ref,
    images_ref,
    images_swapped_ref,
    near_slopes_ref,
    far_slopes_ref,
    other_slopes_ref,
    *refs,
):
    far_refs, far_swapped_refs, outs, slopes_ref = refs[:count], refs[count : 2 * count], refs[2 * count : -1], refs[-1]
    rows, width = far_ref.shape
    own_texts = (near_ref, far_ref)
    pair_terms(scale_ref[0], bias_ref[0], own_texts, far_swapped_refs, slopes_ref, losses=False)
    own_slopes = jnp.concatenate([near_slopes_ref[...], far_slopes_ref[...]], axis=1)
    other_slopes = jnp.concatenate([other_slopes_ref[...], slopes_ref[...]], axis=1)
    for left, step in column_cuts(width):
        cut = slice(left, left + step)
        total = jnp.dot(
            own_slopes,
            joined([ref.at[:, cut] for ref in (images_ref, *far_refs)]),
            preferred_element_type=f32,
        ) + jnp.dot(
            other_slopes,
            joined([ref.at[:, cut] for ref in (images_swapped_ref, *far_swapped_refs)]),
            preferred_element_type=f32,
        )
        for k, out in enumerate(outs):
            out[:, cut] = total[k * rows : (k + 1) * rows, :].astype(out.dtype)


def late_image_kernel(zs, ys, *refs):
    sums, losses, refs = refs[:zs], refs[zs : 2 * zs], refs[2 * zs :]
    parts, payloads, outs = refs[: zs * ys], refs[zs * ys : zs * ys + ys], refs[zs * ys + ys :]
    for k in range(zs):
        height = sums[k].shape[0]
        total, loss = sums[k][...], losses[k][...]
        for part in parts[k * ys : (k + 1) * ys]:
            total = total + part[:height, :].astype(f32)
            last = part[height:, :].astype(f32)
            loss = loss + (last[0:1, :] + last[1:2, :])
        outs[k][:height, :] = total.astype(bf16)
        outs[k][height:, :] = loss_rows(loss)
    for source, target in zip(payloads, outs[zs:]):
        target[...] = source[...]


def gate_kernel(out_ref):
    out_ref[...] = jnp.zeros_like(out_ref)


def row_gradient(rows, sums, scale, out_ref):
    unit_rows, inverse = unit_of(rows)
    unit_grad = scale * sums
    out_ref[...] = (
        unit_grad - unit_rows * jnp.sum(unit_rows * unit_grad, axis=-1, keepdims=True)
    ) * inverse


def end_kernel(batch, images, scale_ref, image_ref, text_ref, grad_ref, loss_ref, text_grad_ref, *refs):
    parts, text_parts, (out_ref, text_out_ref, out_loss_ref, sums_ref) = refs[:images], refs[images:-4], refs[-4:]
    rows, width = image_ref.shape
    loss = loss_ref[...]
    for part in parts:
        last = part[width // lanes * rows :, :].astype(f32)
        loss = loss + (last[0:1, :] + last[1:2, :])
    out_loss_ref[...] = loss / batch
    for panel in range(width // lanes):
        cut = slice(panel * lanes, (panel + 1) * lanes)
        sums = grad_ref[:, cut]
        for part in parts:
            sums = sums + part[panel * rows : (panel + 1) * rows, :].astype(f32)
        sums_ref[:, cut] = sums
    row_gradient(image_ref[...], sums_ref[...], scale_ref[0], out_ref)
    sums = text_grad_ref[...]
    for part in text_parts:
        sums = sums + part[...].astype(f32)
    row_gradient(text_ref[...], sums, scale_ref[0], text_out_ref)


def body(image, text, logarithm_scale, bias):
    rows, width = image.shape
    dp_count, inner_count = lax.axis_size("dp"), lax.axis_size("inner")
    batch = rows * dp_count * inner_count
    scale = jnp.exp(logarithm_scale)
    block = shape((rows, width), bf16)
    wide_block = shape((rows, width), f32)

    image_dp, image_inner = range(4, dp_count, 4), range(2, inner_count, 2)

    half_block = shape((rows // 2, width), bf16)
    text_z = swapped(text, "inner", 1)
    text_x = swapped(text, "dp", 2)
    first_half = image[: rows // 2]
    first_z = [swapped(first_half, "inner", q) for q in image_inner]
    images_y = [swapped(image, "dp", p) for p in image_dp]
    text_emb, image_emb, second_half, text_rows, image_rows = call(
        own_rows_kernel, [block, block, half_block, block, block], scale, bias, text, image, scalars=2
    )
    second_z = [swapped(second_half, "inner", q) for q in image_inner]
    zs, ys = len(first_z), len(images_y)

    (text_z_emb,) = call(unit_kernel, [block], text_z, weight=weights["x"], after=[text_x, second_half])
    near_texts = call(
        functools.partial(near_kernel, frozenset({1})),
        shape((3 * rows, width), bf16),
        text_emb,
        text_x,
        text_z_emb,
    )
    texts_swapped = swapped(near_texts, "dp", 1)
    far_places = [(p, q) for q in image_inner for p in image_dp]
    first_z = call(
        unit_kernel, [half_block] * zs, *first_z, weight=weights["a"], after=[text_z_emb, *images_y]
    )
    first_far = [swapped(emb, "dp", p) for emb in first_z for p in image_dp]
    second_z = call(copies_kernel, [half_block] * zs, *second_z, weight=weights["b"], after=[*first_z, texts_swapped])
    (far_text,) = call(copies_kernel, [block], swapped(text_z_emb, "dp", 2), weight=weights["x far"], after=second_z)
    first_far = call(
        copies_kernel, [half_block] * (zs * ys), *first_far, weight=weights["y far"], after=[far_text]
    )
    second_far = [swapped(emb, "dp", p) for emb in second_z for p in image_dp]

    near_images = call(
        functools.partial(near_kernel, frozenset(range(1, 1 + ys))),
        shape(((1 + ys + zs) * rows, width), bf16),
        image_emb,
        *images_y,
        *(part for both in zip(first_z, second_z) for part in both),
    )
    images_swapped = swapped(near_images, "dp", 1)
    far_text_swapped = swapped(far_text, "dp", 1)

    half, near_rows, far_rows = 4 * rows, (1 + ys + zs) * rows, zs * ys * rows
    own_texts, other_texts = (near_texts, far_text), (texts_swapped, far_text_swapped)
    pair_flops = 2 * rows * half * width
    near_slopes, near_loss = shape((half, near_rows), bf16), shape((1, near_rows), f32)
    payload = shape((width // lanes * rows + extra, lanes), bf16)
    own_slopes, loss = call(
        functools.partial(near_pairs_kernel, True),
        (near_slopes, near_loss),
        scale,
        bias,
        *own_texts,
        near_images,
        flops=pair_flops * (1 + ys + zs),
        scalars=2,
    )
    swapped_slopes = call(
        swapped_pairs_kernel,
        near_slopes,
        scale,
        bias,
        *own_texts,
        images_swapped,
        flops=pair_flops * (1 + ys + zs),
        scalars=2,
        after=[own_slopes],
    )
    far = call(join_kernel, [block] * (zs * ys), *first_far, *second_far, after=[swapped_slopes])
    far_swapped = [swapped(emb, "dp", 1) for emb in far]
    far_slopes, *far_sent = call(
        functools.partial(far_kernel, len(far)),
        [shape((half, far_rows), bf16)] + [payload] * len(far),
        scale,
        bias,
        *own_texts,
        *other_texts,
        *far,
        flops=4 * pair_flops * len(far),
        scalars=2,
        scratch=[pltpu.VMEM((half, far_rows), bf16)],
        after=[swapped_slopes],
    )
    moved = [swapped(part, "dp", p) for part, (p, q) in zip(far_sent, far_places)]
    text_grad, text_x_sums, text_z_sums, text_xz_sums = call(
        functools.partial(text_kernel, len(far)),
        (wide_block, block, block, block),
        scale,
        bias,
        *own_texts,
        near_images,
        images_swapped,
        own_slopes,
        far_slopes,
        swapped_slopes,
        *far,
        *far_swapped,
        flops=3 * pair_flops * (1 + ys + zs + len(far)),
        scalars=2,
        scratch=[pltpu.VMEM((half, far_rows), bf16)],
        after=far_sent[:1],
    )
    text_parts = [
        swapped_both(text_xz_sums, 2, 1),
        swapped(text_z_sums, "inner", 1),
        swapped(text_x_sums, "dp", 2),
    ]
    other_slopes, loss = call(
        functools.partial(near_pairs_kernel, False),
        (near_slopes, near_loss),
        scale,
        bias,
        *other_texts,
        near_images,
        loss,
        flops=pair_flops * (1 + ys + zs),
        scalars=2,
        after=[text_x_sums],
    )
    image_grad, own_loss, *sums = call(
        functools.partial(near_sums_kernel, ys),
        [wide_block, shape((1, rows), f32)]
        + [payload] * ys
        + [shape((width // lanes * rows, lanes), f32), shape((1, rows), f32)] * zs,
        own_slopes,
        other_slopes,
        *own_texts,
        *other_texts,
        loss,
        flops=2 * pair_flops * (1 + ys + zs),
        after=[text_x_sums],
    )

    late = call(
        functools.partial(late_image_kernel, zs, ys),
        [payload] * (zs + ys),
        *sums[ys::2],
        *sums[ys + 1 :: 2],
        *moved,
        *sums[:ys],
        weight=weights["late"],
    )
    z_parts = [swapped(part, "inner", q) for part, q in zip(late, image_inner)]
    gate = call(gate_kernel, shape((8, lanes), f32), weight=weights["gate"], after=text_parts[:2])
    image_parts = [*z_parts, *(swapped(part, "dp", p) for part, p in zip(late[zs:], image_dp))]
    image_gradient, text_gradient, image_loss = call(
        functools.partial(end_kernel, batch, len(image_parts)),
        (wide_block, wide_block, shape((1, rows), f32)),
        scale,
        image_rows,
        text_rows,
        image_grad,
        own_loss,
        text_grad,
        *image_parts,
        *text_parts,
        scalars=1,
        scratch=[pltpu.VMEM((rows, width), f32)],
        after=[gate],
    )
    return (image_gradient, text_gradient, image_loss.reshape(rows))


def solution(mesh):
    return jax.shard_map(
        body,
        mesh=mesh,
        in_specs=(P(("dp", "inner"), None), P(("dp", "inner"), None), P(), P()),
        out_specs=(P(("dp", "inner"), None), P(("dp", "inner"), None), P(("dp", "inner"))),
        check_vma=False,
    )
```

```python
import functools

import jax
import jax.numpy as jnp
from jax import lax
from jax.experimental import pallas as pl
from jax.experimental.pallas import tpu as pltpu
from jax.sharding import PartitionSpec as P

epsilon = 1e-06
f32, bf16 = jnp.float32, jnp.bfloat16
lanes = 128
extra = 16
weights = {"x far": 10, "y far": 10, "x": 0, "a": 10, "b": 10, "late": 2, "gate": 2}
VMEM = pl.BlockSpec(memory_space=pltpu.VMEM)
SMEM = pl.BlockSpec(memory_space=pltpu.SMEM)
ANY = pl.BlockSpec(memory_space=pl.ANY)


def swapped(value, axis, step):
    return lax.ppermute(value, axis, [(place, place ^ step) for place in range(lax.axis_size(axis))])


def swapped_both(value, dp_step, inner_step):
    dp_count, inner_count = lax.axis_size("dp"), lax.axis_size("inner")
    pairs = [
        (d * inner_count + i, (d ^ dp_step) * inner_count + (i ^ inner_step))
        for d in range(dp_count)
        for i in range(inner_count)
    ]
    return lax.ppermute(value, ("dp", "inner"), pairs)


def call(kernel, out_shape, *operands, flops=0, weight=0, scalars=0, scratch=(), after=()):
    moved = sum(o.size * o.dtype.itemsize for o in operands)
    moved += sum(o.size * o.dtype.itemsize for o in jax.tree.leaves(out_shape))
    first, last = len(operands), len(operands) + len(after)
    return pl.pallas_call(
        lambda *refs: kernel(*refs[:first], *refs[last:]),
        out_shape=out_shape,
        in_specs=[SMEM] * scalars + [VMEM] * (len(operands) - scalars) + [ANY] * len(after),
        out_specs=jax.tree.map(lambda _: VMEM, out_shape),
        scratch_shapes=scratch,
        compiler_params=pltpu.CompilerParams(vmem_limit_bytes=40 * 1024 * 1024),
        cost_estimate=pl.CostEstimate(
            flops=flops + int(weight * 1e9), bytes_accessed=moved, transcendentals=0
        ),
    )(*operands, *after)


def shape(dims, kind):
    return jax.ShapeDtypeStruct(dims, kind)


def unit_of(rows):
    wide = rows.astype(f32)
    inverse = lax.rsqrt(jnp.sum(wide * wide, axis=-1, keepdims=True) + epsilon)
    return wide * inverse, inverse


def joined(refs):
    return refs[0][...] if len(refs) == 1 else jnp.concatenate([ref[...] for ref in refs], axis=0)


def pair_terms(scale, offset, text_refs, image_refs, slopes_ref, own=0, losses=True):
    texts, all_images = joined(text_refs), joined(image_refs)
    totals = []
    for left in range(0, all_images.shape[0], 256):
        images = all_images[left : min(left + 256, all_images.shape[0]), :]
        total = jnp.zeros((1, images.shape[0]), f32)
        for start in range(0, texts.shape[0], 256):
            logits = (
                scale
                * lax.dot_general(
                    texts[start : start + 256, :],
                    images,
                    (((1,), (1,)), ((), ())),
                    preferred_element_type=f32,
                )
                + offset
            )
            shrunk = jnp.exp(-jnp.abs(logits))
            raised = 1.0 + shrunk
            inverse = pl.reciprocal(raised, approx=True)
            inverse = inverse * (2.0 - raised * inverse)
            sigmoid = jnp.where(logits >= 0.0, inverse, shrunk * inverse)
            match = None
            if own and left == 0 and start < own:
                text_ids = start + lax.broadcasted_iota(jnp.int32, logits.shape, 0)
                image_ids = lax.broadcasted_iota(jnp.int32, logits.shape, 1)
                match = ((text_ids == image_ids) & (text_ids < own)).astype(f32)
                sigmoid = sigmoid - match
            slopes_ref[start : start + 256, left : left + images.shape[0]] = sigmoid.astype(bf16)
            if losses:
                log_raised = jnp.log(raised) + (shrunk - (raised - 1.0)) * inverse
                softplus = jnp.maximum(logits, 0.0) + log_raised
                if match is not None:
                    softplus = softplus - match * logits
                total = total + jnp.sum(softplus, axis=0, keepdims=True)
        totals.append(total)
    return jnp.concatenate(totals, axis=1) if losses else None


def unit_kernel(*refs):
    for raw, emb in zip(refs[: len(refs) // 2], refs[len(refs) // 2 :]):
        emb[...] = unit_of(raw[...])[0].astype(bf16)


def copies_kernel(*refs):
    for source, target in zip(refs[: len(refs) // 2], refs[len(refs) // 2 :]):
        target[...] = source[...]


def own_rows_kernel(
    scale_ref, bias_ref, text_ref, image_ref, text_emb_ref, image_emb_ref, half_ref, text_out_ref, image_out_ref
):
    text_out_ref[...] = text_ref[...]
    image_out_ref[...] = image_ref[...]
    text_emb_ref[...] = unit_of(text_ref[...])[0].astype(bf16)
    emb = unit_of(image_ref[...])[0].astype(bf16)
    image_emb_ref[...] = emb
    half_ref[...] = emb[emb.shape[0] // 2 :, :]


def near_kernel(raw, *refs):
    out_ref, start = refs[-1], 0
    for place, block in enumerate(refs[:-1]):
        count = block.shape[0]
        out_ref[start : start + count, :] = unit_of(block[...])[0].astype(bf16) if place in raw else block[...]
        start += count


def join_kernel(*refs):
    count = len(refs) // 3
    for first, second, out in zip(refs[:count], refs[count : 2 * count], refs[2 * count :]):
        rows = first.shape[0]
        out[:rows, :] = first[...]
        out[rows:, :] = second[...]


def near_pairs_kernel(own, scale_ref, bias_ref, near_ref, far_ref, images_ref, *refs):
    slopes_ref, loss_ref = refs[-2:]
    rows = far_ref.shape[0]
    texts = (near_ref, far_ref)
    loss = pair_terms(
        scale_ref[0], bias_ref[0], texts, (images_ref,), slopes_ref, rows if own else 0
    )
    loss_ref[...] = loss if own else loss + refs[0][...]


def loss_rows(loss):
    high = loss.astype(bf16).astype(f32)
    which = lax.broadcasted_iota(jnp.int32, (extra, loss.shape[1]), 0)
    return jnp.where(which == 0, high, loss - high).astype(bf16)


def column_cuts(width):
    step = 4 * lanes
    return [(left, min(step, width - left)) for left in range(0, width, step)]


def sums_in_parts(slope_refs, text_refs, width):
    for left, step in column_cuts(width):
        total = None
        for slopes, texts in zip(slope_refs, text_refs):
            part = lax.dot_general(
                slopes[...],
                joined([block.at[:, left : left + step] for block in texts]),
                (((0,), (0,)), ((), ())),
                preferred_element_type=f32,
            )
            total = part if total is None else total + part
        yield left, step, total


def put_panels(out, rows, left, sums):
    for at in range(0, sums.shape[1], lanes):
        panel = (left + at) // lanes
        out[panel * rows : (panel + 1) * rows, :] = sums[:, at : at + lanes].astype(out.dtype)


def far_kernel(count, scale_ref, bias_ref, near_ref, far_ref, near_swapped_ref, far_swapped_ref, *refs):
    image_refs, (own_slopes_ref, *sent_refs), other_slopes_ref = refs[:count], refs[count:-1], refs[-1]
    rows, width = far_ref.shape
    scale, offset = scale_ref[0], bias_ref[0]
    own_texts = (near_ref, far_ref)
    other_texts = (near_swapped_ref, far_swapped_ref)
    loss = pair_terms(scale, offset, own_texts, image_refs, own_slopes_ref)
    loss = loss + pair_terms(scale, offset, other_texts, image_refs, other_slopes_ref)
    slopes = (own_slopes_ref, other_slopes_ref)
    for left, step, total in sums_in_parts(slopes, (own_texts, other_texts), width):
        for place, out in enumerate(sent_refs):
            put_panels(out, rows, left, total[place * rows : (place + 1) * rows, :])
    for place, out in enumerate(sent_refs):
        out[width // lanes * rows :, :] = loss_rows(loss[:, place * rows : (place + 1) * rows])


def near_sums_kernel(
    plain, own_slopes_ref, other_slopes_ref, near_ref, far_ref, near_swapped_ref, far_swapped_ref, loss_ref, *refs
):
    own_ref, own_loss_ref, plain_refs, rest = refs[0], refs[1], refs[2 : 2 + plain], refs[2 + plain :]
    z_refs, z_loss_refs = rest[::2], rest[1::2]
    rows, width = far_ref.shape
    own_texts = (near_ref, far_ref)
    other_texts = (near_swapped_ref, far_swapped_ref)
    slopes = (own_slopes_ref, other_slopes_ref)
    for left, step, total in sums_in_parts(slopes, (own_texts, other_texts), width):
        own_ref[:, left : left + step] = total[:rows, :]
        for place, out in enumerate((*plain_refs, *z_refs), 1):
            put_panels(out, rows, left, total[place * rows : (place + 1) * rows, :])
    own_loss_ref[...] = loss_ref[:, :rows]
    for place, out in enumerate(plain_refs, 1):
        out[width // lanes * rows :, :] = loss_rows(loss_ref[:, place * rows : (place + 1) * rows])
    for place, out in enumerate(z_loss_refs, 1 + plain):
        out[...] = loss_ref[:, place * rows : (place + 1) * rows]


def swapped_pairs_kernel(scale_ref, bias_ref, near_ref, far_ref, images_ref, slopes_ref):
    pair_terms(scale_ref[0], bias_ref[0], (near_ref, far_ref), (images_ref,), slopes_ref, losses=False)


def text_kernel(
    count,
    scale_ref,
    bias_ref,
    near_ref,
    far_ref,
    images_ref,
    images_swapped_ref,
    near_slopes_ref,
    far_slopes_ref,
    other_slopes_ref,
    *refs,
):
    far_refs, far_swapped_refs, outs, slopes_ref = refs[:count], refs[count : 2 * count], refs[2 * count : -1], refs[-1]
    rows, width = far_ref.shape
    own_texts = (near_ref, far_ref)
    pair_terms(scale_ref[0], bias_ref[0], own_texts, far_swapped_refs, slopes_ref, losses=False)
    own_slopes = jnp.concatenate([near_slopes_ref[...], far_slopes_ref[...]], axis=1)
    other_slopes = jnp.concatenate([other_slopes_ref[...], slopes_ref[...]], axis=1)
    for left, step in column_cuts(width):
        cut = slice(left, left + step)
        total = jnp.dot(
            own_slopes,
            joined([ref.at[:, cut] for ref in (images_ref, *far_refs)]),
            preferred_element_type=f32,
        ) + jnp.dot(
            other_slopes,
            joined([ref.at[:, cut] for ref in (images_swapped_ref, *far_swapped_refs)]),
            preferred_element_type=f32,
        )
        for k, out in enumerate(outs):
            out[:, cut] = total[k * rows : (k + 1) * rows, :].astype(out.dtype)


def late_image_kernel(zs, ys, *refs):
    sums, losses, refs = refs[:zs], refs[zs : 2 * zs], refs[2 * zs :]
    parts, payloads, outs = refs[: zs * ys], refs[zs * ys : zs * ys + ys], refs[zs * ys + ys :]
    for k in range(zs):
        height = sums[k].shape[0]
        total, loss = sums[k][...], losses[k][...]
        for part in parts[k * ys : (k + 1) * ys]:
            total = total + part[:height, :].astype(f32)
            last = part[height:, :].astype(f32)
            loss = loss + (last[0:1, :] + last[1:2, :])
        outs[k][:height, :] = total.astype(bf16)
        outs[k][height:, :] = loss_rows(loss)
    for source, target in zip(payloads, outs[zs:]):
        target[...] = source[...]


def gate_kernel(out_ref):
    out_ref[...] = jnp.zeros_like(out_ref)


def row_gradient(rows, sums, scale, out_ref):
    unit_rows, inverse = unit_of(rows)
    unit_grad = scale * sums
    out_ref[...] = (
        unit_grad - unit_rows * jnp.sum(unit_rows * unit_grad, axis=-1, keepdims=True)
    ) * inverse


def end_kernel(batch, images, scale_ref, image_ref, text_ref, grad_ref, loss_ref, text_grad_ref, *refs):
    parts, text_parts, (out_ref, text_out_ref, out_loss_ref, sums_ref) = refs[:images], refs[images:-4], refs[-4:]
    rows, width = image_ref.shape
    loss = loss_ref[...]
    for part in parts:
        last = part[width // lanes * rows :, :].astype(f32)
        loss = loss + (last[0:1, :] + last[1:2, :])
    out_loss_ref[...] = loss / batch
    for panel in range(width // lanes):
        cut = slice(panel * lanes, (panel + 1) * lanes)
        sums = grad_ref[:, cut]
        for part in parts:
            sums = sums + part[panel * rows : (panel + 1) * rows, :].astype(f32)
        sums_ref[:, cut] = sums
    row_gradient(image_ref[...], sums_ref[...], scale_ref[0], out_ref)
    sums = text_grad_ref[...]
    for part in text_parts:
        sums = sums + part[...].astype(f32)
    row_gradient(text_ref[...], sums, scale_ref[0], text_out_ref)


def body(image, text, logarithm_scale, bias):
    rows, width = image.shape
    dp_count, inner_count = lax.axis_size("dp"), lax.axis_size("inner")
    batch = rows * dp_count * inner_count
    scale = jnp.exp(logarithm_scale)
    block = shape((rows, width), bf16)
    wide_block = shape((rows, width), f32)

    image_dp, image_inner = range(4, dp_count, 4), range(2, inner_count, 2)

    half_block = shape((rows // 2, width), bf16)
    text_z = swapped(text, "inner", 1)
    text_x = swapped(text, "dp", 2)
    first_half = image[: rows // 2]
    first_z = [swapped(first_half, "inner", q) for q in image_inner]
    images_y = [swapped(image, "dp", p) for p in image_dp]
    text_emb, image_emb, second_half, text_rows, image_rows = call(
        own_rows_kernel, [block, block, half_block, block, block], scale, bias, text, image, scalars=2
    )
    second_z = [swapped(second_half, "inner", q) for q in image_inner]
    zs, ys = len(first_z), len(images_y)

    first_z = call(
        unit_kernel, [half_block] * zs, *first_z, weight=weights["a"]
    )
    (text_z_emb,) = call(unit_kernel, [block], text_z, weight=weights["x"], after=[text_x, second_half, *images_y, *first_z])
    near_texts = call(
        functools.partial(near_kernel, frozenset({1})),
        shape((3 * rows, width), bf16),
        text_emb,
        text_x,
        text_z_emb,
    )
    texts_swapped = swapped(near_texts, "dp", 1)
    far_places = [(p, q) for q in image_inner for p in image_dp]
    first_far = [swapped(emb, "dp", p) for emb in first_z for p in image_dp]
    second_z = call(copies_kernel, [half_block] * zs, *second_z, weight=weights["b"], after=first_z)
    (far_text,) = call(copies_kernel, [block], swapped(text_z_emb, "dp", 2), weight=weights["x far"], after=[*second_z, texts_swapped])
    first_far = call(
        copies_kernel, [half_block] * (zs * ys), *first_far, weight=weights["y far"], after=[far_text]
    )
    second_far = [swapped(emb, "dp", p) for emb in second_z for p in image_dp]

    near_images = call(
        functools.partial(near_kernel, frozenset(range(1, 1 + ys))),
        shape(((1 + ys + zs) * rows, width), bf16),
        image_emb,
        *images_y,
        *(part for both in zip(first_z, second_z) for part in both),
    )
    images_swapped = swapped(near_images, "dp", 1)
    far_text_swapped = swapped(far_text, "dp", 1)

    half, near_rows, far_rows = 4 * rows, (1 + ys + zs) * rows, zs * ys * rows
    own_texts, other_texts = (near_texts, far_text), (texts_swapped, far_text_swapped)
    pair_flops = 2 * rows * half * width
    near_slopes, near_loss = shape((half, near_rows), bf16), shape((1, near_rows), f32)
    payload = shape((width // lanes * rows + extra, lanes), bf16)
    own_slopes, loss = call(
        functools.partial(near_pairs_kernel, True),
        (near_slopes, near_loss),
        scale,
        bias,
        *own_texts,
        near_images,
        flops=pair_flops * (1 + ys + zs),
        scalars=2,
    )
    swapped_slopes = call(
        swapped_pairs_kernel,
        near_slopes,
        scale,
        bias,
        *own_texts,
        images_swapped,
        flops=pair_flops * (1 + ys + zs),
        scalars=2,
        after=[own_slopes],
    )
    far = call(join_kernel, [block] * (zs * ys), *first_far, *second_far, after=[swapped_slopes])
    far_swapped = [swapped(emb, "dp", 1) for emb in far]
    far_slopes, *far_sent = call(
        functools.partial(far_kernel, len(far)),
        [shape((half, far_rows), bf16)] + [payload] * len(far),
        scale,
        bias,
        *own_texts,
        *other_texts,
        *far,
        flops=4 * pair_flops * len(far),
        scalars=2,
        scratch=[pltpu.VMEM((half, far_rows), bf16)],
        after=[swapped_slopes],
    )
    moved = [swapped(part, "dp", p) for part, (p, q) in zip(far_sent, far_places)]
    text_grad, text_x_sums, text_z_sums, text_xz_sums = call(
        functools.partial(text_kernel, len(far)),
        (wide_block, block, block, block),
        scale,
        bias,
        *own_texts,
        near_images,
        images_swapped,
        own_slopes,
        far_slopes,
        swapped_slopes,
        *far,
        *far_swapped,
        flops=3 * pair_flops * (1 + ys + zs + len(far)),
        scalars=2,
        scratch=[pltpu.VMEM((half, far_rows), bf16)],
        after=far_sent[:1],
    )
    text_parts = [
        swapped_both(text_xz_sums, 2, 1),
        swapped(text_z_sums, "inner", 1),
        swapped(text_x_sums, "dp", 2),
    ]
    other_slopes, loss = call(
        functools.partial(near_pairs_kernel, False),
        (near_slopes, near_loss),
        scale,
        bias,
        *other_texts,
        near_images,
        loss,
        flops=pair_flops * (1 + ys + zs),
        scalars=2,
        after=[text_x_sums],
    )
    image_grad, own_loss, *sums = call(
        functools.partial(near_sums_kernel, ys),
        [wide_block, shape((1, rows), f32)]
        + [payload] * ys
        + [shape((width // lanes * rows, lanes), f32), shape((1, rows), f32)] * zs,
        own_slopes,
        other_slopes,
        *own_texts,
        *other_texts,
        loss,
        flops=2 * pair_flops * (1 + ys + zs),
        after=[text_x_sums],
    )

    late = call(
        functools.partial(late_image_kernel, zs, ys),
        [payload] * (zs + ys),
        *sums[ys::2],
        *sums[ys + 1 :: 2],
        *moved,
        *sums[:ys],
        weight=weights["late"],
    )
    z_parts = [swapped(part, "inner", q) for part, q in zip(late, image_inner)]
    gate = call(gate_kernel, shape((8, lanes), f32), weight=weights["gate"], after=text_parts[:2])
    image_parts = [*z_parts, *(swapped(part, "dp", p) for part, p in zip(late[zs:], image_dp))]
    image_gradient, text_gradient, image_loss = call(
        functools.partial(end_kernel, batch, len(image_parts)),
        (wide_block, wide_block, shape((1, rows), f32)),
        scale,
        image_rows,
        text_rows,
        image_grad,
        own_loss,
        text_grad,
        *image_parts,
        *text_parts,
        scalars=1,
        scratch=[pltpu.VMEM((rows, width), f32)],
        after=[gate],
    )
    return (image_gradient, text_gradient, image_loss.reshape(rows))


def solution(mesh):
    return jax.shard_map(
        body,
        mesh=mesh,
        in_specs=(P(("dp", "inner"), None), P(("dp", "inner"), None), P(), P()),
        out_specs=(P(("dp", "inner"), None), P(("dp", "inner"), None), P(("dp", "inner"))),
        check_vma=False,
    )
```

```python
import functools

import jax
import jax.numpy as jnp
from jax import lax
from jax.experimental import pallas as pl
from jax.experimental.pallas import tpu as pltpu
from jax.sharding import PartitionSpec as P

epsilon = 1e-06
f32, bf16 = jnp.float32, jnp.bfloat16
lanes = 128
extra = 16
weights = {"x far": 10, "y far": 10, "x": 0, "a": 10, "b": 10, "late": 2, "gate": 2}
VMEM = pl.BlockSpec(memory_space=pltpu.VMEM)
SMEM = pl.BlockSpec(memory_space=pltpu.SMEM)
ANY = pl.BlockSpec(memory_space=pl.ANY)


def swapped(value, axis, step):
    return lax.ppermute(value, axis, [(place, place ^ step) for place in range(lax.axis_size(axis))])


def swapped_both(value, dp_step, inner_step):
    dp_count, inner_count = lax.axis_size("dp"), lax.axis_size("inner")
    pairs = [
        (d * inner_count + i, (d ^ dp_step) * inner_count + (i ^ inner_step))
        for d in range(dp_count)
        for i in range(inner_count)
    ]
    return lax.ppermute(value, ("dp", "inner"), pairs)


def call(kernel, out_shape, *operands, flops=0, weight=0, scalars=0, scratch=(), after=()):
    moved = sum(o.size * o.dtype.itemsize for o in operands)
    moved += sum(o.size * o.dtype.itemsize for o in jax.tree.leaves(out_shape))
    first, last = len(operands), len(operands) + len(after)
    return pl.pallas_call(
        lambda *refs: kernel(*refs[:first], *refs[last:]),
        out_shape=out_shape,
        in_specs=[SMEM] * scalars + [VMEM] * (len(operands) - scalars) + [ANY] * len(after),
        out_specs=jax.tree.map(lambda _: VMEM, out_shape),
        scratch_shapes=scratch,
        compiler_params=pltpu.CompilerParams(vmem_limit_bytes=40 * 1024 * 1024),
        cost_estimate=pl.CostEstimate(
            flops=flops + int(weight * 1e9), bytes_accessed=moved, transcendentals=0
        ),
    )(*operands, *after)


def shape(dims, kind):
    return jax.ShapeDtypeStruct(dims, kind)


def unit_of(rows):
    wide = rows.astype(f32)
    inverse = lax.rsqrt(jnp.sum(wide * wide, axis=-1, keepdims=True) + epsilon)
    return wide * inverse, inverse


def joined(refs):
    return refs[0][...] if len(refs) == 1 else jnp.concatenate([ref[...] for ref in refs], axis=0)


def pair_terms(scale, offset, text_refs, image_refs, slopes_ref, own=0, losses=True):
    texts, all_images = joined(text_refs), joined(image_refs)
    totals = []
    for left in range(0, all_images.shape[0], 256):
        images = all_images[left : min(left + 256, all_images.shape[0]), :]
        total = jnp.zeros((1, images.shape[0]), f32)
        for start in range(0, texts.shape[0], 256):
            logits = (
                scale
                * lax.dot_general(
                    texts[start : start + 256, :],
                    images,
                    (((1,), (1,)), ((), ())),
                    preferred_element_type=f32,
                )
                + offset
            )
            shrunk = jnp.exp(-jnp.abs(logits))
            raised = 1.0 + shrunk
            inverse = pl.reciprocal(raised, approx=True)
            inverse = inverse * (2.0 - raised * inverse)
            sigmoid = jnp.where(logits >= 0.0, inverse, shrunk * inverse)
            match = None
            if own and left == 0 and start < own:
                text_ids = start + lax.broadcasted_iota(jnp.int32, logits.shape, 0)
                image_ids = lax.broadcasted_iota(jnp.int32, logits.shape, 1)
                match = ((text_ids == image_ids) & (text_ids < own)).astype(f32)
                sigmoid = sigmoid - match
            slopes_ref[start : start + 256, left : left + images.shape[0]] = sigmoid.astype(bf16)
            if losses:
                log_raised = jnp.log(raised) + (shrunk - (raised - 1.0)) * inverse
                softplus = jnp.maximum(logits, 0.0) + log_raised
                if match is not None:
                    softplus = softplus - match * logits
                total = total + jnp.sum(softplus, axis=0, keepdims=True)
        totals.append(total)
    return jnp.concatenate(totals, axis=1) if losses else None


def unit_kernel(*refs):
    for raw, emb in zip(refs[: len(refs) // 2], refs[len(refs) // 2 :]):
        emb[...] = unit_of(raw[...])[0].astype(bf16)


def copies_kernel(*refs):
    for source, target in zip(refs[: len(refs) // 2], refs[len(refs) // 2 :]):
        target[...] = source[...]


def own_rows_kernel(
    scale_ref, bias_ref, text_ref, image_ref, text_emb_ref, image_emb_ref, half_ref, text_out_ref, image_out_ref
):
    text_out_ref[...] = text_ref[...]
    image_out_ref[...] = image_ref[...]
    text_emb_ref[...] = unit_of(text_ref[...])[0].astype(bf16)
    emb = unit_of(image_ref[...])[0].astype(bf16)
    image_emb_ref[...] = emb
    half_ref[...] = emb[emb.shape[0] // 2 :, :]


def near_kernel(raw, *refs):
    out_ref, start = refs[-1], 0
    for place, block in enumerate(refs[:-1]):
        count = block.shape[0]
        out_ref[start : start + count, :] = unit_of(block[...])[0].astype(bf16) if place in raw else block[...]
        start += count


def join_kernel(*refs):
    count = len(refs) // 3
    for first, second, out in zip(refs[:count], refs[count : 2 * count], refs[2 * count :]):
        rows = first.shape[0]
        out[:rows, :] = first[...]
        out[rows:, :] = second[...]


def near_pairs_kernel(own, scale_ref, bias_ref, near_ref, far_ref, images_ref, *refs):
    slopes_ref, loss_ref = refs[-2:]
    rows = far_ref.shape[0]
    texts = (near_ref, far_ref)
    loss = pair_terms(
        scale_ref[0], bias_ref[0], texts, (images_ref,), slopes_ref, rows if own else 0
    )
    loss_ref[...] = loss if own else loss + refs[0][...]


def loss_rows(loss):
    high = loss.astype(bf16).astype(f32)
    which = lax.broadcasted_iota(jnp.int32, (extra, loss.shape[1]), 0)
    return jnp.where(which == 0, high, loss - high).astype(bf16)


def column_cuts(width):
    step = 4 * lanes
    return [(left, min(step, width - left)) for left in range(0, width, step)]


def sums_in_parts(slope_refs, text_refs, width):
    for left, step in column_cuts(width):
        total = None
        for slopes, texts in zip(slope_refs, text_refs):
            part = lax.dot_general(
                slopes[...],
                joined([block.at[:, left : left + step] for block in texts]),
                (((0,), (0,)), ((), ())),
                preferred_element_type=f32,
            )
            total = part if total is None else total + part
        yield left, step, total


def put_panels(out, rows, left, sums):
    for at in range(0, sums.shape[1], lanes):
        panel = (left + at) // lanes
        out[panel * rows : (panel + 1) * rows, :] = sums[:, at : at + lanes].astype(out.dtype)


def far_kernel(count, scale_ref, bias_ref, near_ref, far_ref, near_swapped_ref, far_swapped_ref, *refs):
    image_refs, (own_slopes_ref, *sent_refs), other_slopes_ref = refs[:count], refs[count:-1], refs[-1]
    rows, width = far_ref.shape
    scale, offset = scale_ref[0], bias_ref[0]
    own_texts = (near_ref, far_ref)
    other_texts = (near_swapped_ref, far_swapped_ref)
    loss = pair_terms(scale, offset, own_texts, image_refs, own_slopes_ref)
    loss = loss + pair_terms(scale, offset, other_texts, image_refs, other_slopes_ref)
    slopes = (own_slopes_ref, other_slopes_ref)
    for left, step, total in sums_in_parts(slopes, (own_texts, other_texts), width):
        for place, out in enumerate(sent_refs):
            put_panels(out, rows, left, total[place * rows : (place + 1) * rows, :])
    for place, out in enumerate(sent_refs):
        out[width // lanes * rows :, :] = loss_rows(loss[:, place * rows : (place + 1) * rows])


def near_sums_kernel(
    plain, own_slopes_ref, other_slopes_ref, near_ref, far_ref, near_swapped_ref, far_swapped_ref, loss_ref, *refs
):
    own_ref, own_loss_ref, plain_refs, rest = refs[0], refs[1], refs[2 : 2 + plain], refs[2 + plain :]
    z_refs, z_loss_refs = rest[::2], rest[1::2]
    rows, width = far_ref.shape
    own_texts = (near_ref, far_ref)
    other_texts = (near_swapped_ref, far_swapped_ref)
    slopes = (own_slopes_ref, other_slopes_ref)
    for left, step, total in sums_in_parts(slopes, (own_texts, other_texts), width):
        own_ref[:, left : left + step] = total[:rows, :]
        for place, out in enumerate((*plain_refs, *z_refs), 1):
            put_panels(out, rows, left, total[place * rows : (place + 1) * rows, :])
    own_loss_ref[...] = loss_ref[:, :rows]
    for place, out in enumerate(plain_refs, 1):
        out[width // lanes * rows :, :] = loss_rows(loss_ref[:, place * rows : (place + 1) * rows])
    for place, out in enumerate(z_loss_refs, 1 + plain):
        out[...] = loss_ref[:, place * rows : (place + 1) * rows]


def swapped_pairs_kernel(scale_ref, bias_ref, near_ref, far_ref, images_ref, slopes_ref):
    pair_terms(scale_ref[0], bias_ref[0], (near_ref, far_ref), (images_ref,), slopes_ref, losses=False)


def text_kernel(
    count,
    scale_ref,
    bias_ref,
    near_ref,
    far_ref,
    images_ref,
    images_swapped_ref,
    near_slopes_ref,
    far_slopes_ref,
    other_slopes_ref,
    *refs,
):
    far_refs, far_swapped_refs, outs, slopes_ref = refs[:count], refs[count : 2 * count], refs[2 * count : -1], refs[-1]
    rows, width = far_ref.shape
    own_texts = (near_ref, far_ref)
    pair_terms(scale_ref[0], bias_ref[0], own_texts, far_swapped_refs, slopes_ref, losses=False)
    own_slopes = jnp.concatenate([near_slopes_ref[...], far_slopes_ref[...]], axis=1)
    other_slopes = jnp.concatenate([other_slopes_ref[...], slopes_ref[...]], axis=1)
    for left, step in column_cuts(width):
        cut = slice(left, left + step)
        total = jnp.dot(
            own_slopes,
            joined([ref.at[:, cut] for ref in (images_ref, *far_refs)]),
            preferred_element_type=f32,
        ) + jnp.dot(
            other_slopes,
            joined([ref.at[:, cut] for ref in (images_swapped_ref, *far_swapped_refs)]),
            preferred_element_type=f32,
        )
        for k, out in enumerate(outs):
            out[:, cut] = total[k * rows : (k + 1) * rows, :].astype(out.dtype)


def late_image_kernel(zs, ys, *refs):
    sums, losses, refs = refs[:zs], refs[zs : 2 * zs], refs[2 * zs :]
    parts, payloads, outs = refs[: zs * ys], refs[zs * ys : zs * ys + ys], refs[zs * ys + ys :]
    for k in range(zs):
        height = sums[k].shape[0]
        total, loss = sums[k][...], losses[k][...]
        for part in parts[k * ys : (k + 1) * ys]:
            total = total + part[:height, :].astype(f32)
            last = part[height:, :].astype(f32)
            loss = loss + (last[0:1, :] + last[1:2, :])
        outs[k][:height, :] = total.astype(bf16)
        outs[k][height:, :] = loss_rows(loss)
    for source, target in zip(payloads, outs[zs:]):
        target[...] = source[...]


def gate_kernel(out_ref):
    out_ref[...] = jnp.zeros_like(out_ref)


def row_gradient(rows, sums, scale, out_ref):
    unit_rows, inverse = unit_of(rows)
    unit_grad = scale * sums
    out_ref[...] = (
        unit_grad - unit_rows * jnp.sum(unit_rows * unit_grad, axis=-1, keepdims=True)
    ) * inverse


def end_kernel(batch, images, scale_ref, image_ref, text_ref, grad_ref, loss_ref, text_grad_ref, *refs):
    parts, text_parts, (out_ref, text_out_ref, out_loss_ref, sums_ref) = refs[:images], refs[images:-4], refs[-4:]
    rows, width = image_ref.shape
    loss = loss_ref[...]
    for part in parts:
        last = part[width // lanes * rows :, :].astype(f32)
        loss = loss + (last[0:1, :] + last[1:2, :])
    out_loss_ref[...] = loss / batch
    for panel in range(width // lanes):
        cut = slice(panel * lanes, (panel + 1) * lanes)
        sums = grad_ref[:, cut]
        for part in parts:
            sums = sums + part[panel * rows : (panel + 1) * rows, :].astype(f32)
        sums_ref[:, cut] = sums
    row_gradient(image_ref[...], sums_ref[...], scale_ref[0], out_ref)
    sums = text_grad_ref[...]
    for part in text_parts:
        sums = sums + part[...].astype(f32)
    row_gradient(text_ref[...], sums, scale_ref[0], text_out_ref)


def body(image, text, logarithm_scale, bias):
    rows, width = image.shape
    dp_count, inner_count = lax.axis_size("dp"), lax.axis_size("inner")
    batch = rows * dp_count * inner_count
    scale = jnp.exp(logarithm_scale)
    block = shape((rows, width), bf16)
    wide_block = shape((rows, width), f32)

    image_dp, image_inner = range(4, dp_count, 4), range(2, inner_count, 2)

    half_block = shape((rows // 2, width), bf16)
    text_z = swapped(text, "inner", 1)
    text_x = swapped(text, "dp", 2)
    first_half = image[: rows // 2]
    first_z = [swapped(first_half, "inner", q) for q in image_inner]
    images_y = [swapped(image, "dp", p) for p in image_dp]
    text_emb, image_emb, second_half, text_rows, image_rows = call(
        own_rows_kernel, [block, block, half_block, block, block], scale, bias, text, image, scalars=2
    )
    second_z = [swapped(second_half, "inner", q) for q in image_inner]
    zs, ys = len(first_z), len(images_y)

    (text_z_emb,) = call(unit_kernel, [block], text_z, weight=weights["x"], after=[second_half])
    near_texts = call(
        functools.partial(near_kernel, frozenset({1})),
        shape((3 * rows, width), bf16),
        text_emb,
        text_x,
        text_z_emb,
    )
    texts_swapped = swapped(near_texts, "dp", 1)
    far_places = [(p, q) for q in image_inner for p in image_dp]
    first_z = call(
        unit_kernel, [half_block] * zs, *first_z, weight=weights["a"], after=[text_z_emb]
    )
    first_far = [swapped(emb, "dp", p) for emb in first_z for p in image_dp]
    second_z = call(copies_kernel, [half_block] * zs, *second_z, weight=weights["b"], after=[*first_z, texts_swapped, *images_y])
    (far_text,) = call(copies_kernel, [block], swapped(text_z_emb, "dp", 2), weight=weights["x far"], after=second_z)
    first_far = call(
        copies_kernel, [half_block] * (zs * ys), *first_far, weight=weights["y far"], after=[far_text]
    )
    second_far = [swapped(emb, "dp", p) for emb in second_z for p in image_dp]

    near_images = call(
        functools.partial(near_kernel, frozenset(range(1, 1 + ys))),
        shape(((1 + ys + zs) * rows, width), bf16),
        image_emb,
        *images_y,
        *(part for both in zip(first_z, second_z) for part in both),
    )
    images_swapped = swapped(near_images, "dp", 1)
    far_text_swapped = swapped(far_text, "dp", 1)

    half, near_rows, far_rows = 4 * rows, (1 + ys + zs) * rows, zs * ys * rows
    own_texts, other_texts = (near_texts, far_text), (texts_swapped, far_text_swapped)
    pair_flops = 2 * rows * half * width
    near_slopes, near_loss = shape((half, near_rows), bf16), shape((1, near_rows), f32)
    payload = shape((width // lanes * rows + extra, lanes), bf16)
    own_slopes, loss = call(
        functools.partial(near_pairs_kernel, True),
        (near_slopes, near_loss),
        scale,
        bias,
        *own_texts,
        near_images,
        flops=pair_flops * (1 + ys + zs),
        scalars=2,
    )
    swapped_slopes = call(
        swapped_pairs_kernel,
        near_slopes,
        scale,
        bias,
        *own_texts,
        images_swapped,
        flops=pair_flops * (1 + ys + zs),
        scalars=2,
        after=[own_slopes],
    )
    far = call(join_kernel, [block] * (zs * ys), *first_far, *second_far, after=[swapped_slopes])
    far_swapped = [swapped(emb, "dp", 1) for emb in far]
    far_slopes, *far_sent = call(
        functools.partial(far_kernel, len(far)),
        [shape((half, far_rows), bf16)] + [payload] * len(far),
        scale,
        bias,
        *own_texts,
        *other_texts,
        *far,
        flops=4 * pair_flops * len(far),
        scalars=2,
        scratch=[pltpu.VMEM((half, far_rows), bf16)],
        after=[swapped_slopes],
    )
    moved = [swapped(part, "dp", p) for part, (p, q) in zip(far_sent, far_places)]
    text_grad, text_x_sums, text_z_sums, text_xz_sums = call(
        functools.partial(text_kernel, len(far)),
        (wide_block, block, block, block),
        scale,
        bias,
        *own_texts,
        near_images,
        images_swapped,
        own_slopes,
        far_slopes,
        swapped_slopes,
        *far,
        *far_swapped,
        flops=3 * pair_flops * (1 + ys + zs + len(far)),
        scalars=2,
        scratch=[pltpu.VMEM((half, far_rows), bf16)],
        after=far_sent[:1],
    )
    text_parts = [
        swapped_both(text_xz_sums, 2, 1),
        swapped(text_z_sums, "inner", 1),
        swapped(text_x_sums, "dp", 2),
    ]
    other_slopes, loss = call(
        functools.partial(near_pairs_kernel, False),
        (near_slopes, near_loss),
        scale,
        bias,
        *other_texts,
        near_images,
        loss,
        flops=pair_flops * (1 + ys + zs),
        scalars=2,
        after=[text_x_sums],
    )
    image_grad, own_loss, *sums = call(
        functools.partial(near_sums_kernel, ys),
        [wide_block, shape((1, rows), f32)]
        + [payload] * ys
        + [shape((width // lanes * rows, lanes), f32), shape((1, rows), f32)] * zs,
        own_slopes,
        other_slopes,
        *own_texts,
        *other_texts,
        loss,
        flops=2 * pair_flops * (1 + ys + zs),
        after=[text_x_sums],
    )

    late = call(
        functools.partial(late_image_kernel, zs, ys),
        [payload] * (zs + ys),
        *sums[ys::2],
        *sums[ys + 1 :: 2],
        *moved,
        *sums[:ys],
        weight=weights["late"],
    )
    z_parts = [swapped(part, "inner", q) for part, q in zip(late, image_inner)]
    gate = call(gate_kernel, shape((8, lanes), f32), weight=weights["gate"], after=text_parts[:2])
    image_parts = [*z_parts, *(swapped(part, "dp", p) for part, p in zip(late[zs:], image_dp))]
    image_gradient, text_gradient, image_loss = call(
        functools.partial(end_kernel, batch, len(image_parts)),
        (wide_block, wide_block, shape((1, rows), f32)),
        scale,
        image_rows,
        text_rows,
        image_grad,
        own_loss,
        text_grad,
        *image_parts,
        *text_parts,
        scalars=1,
        scratch=[pltpu.VMEM((rows, width), f32)],
        after=[gate],
    )
    return (image_gradient, text_gradient, image_loss.reshape(rows))


def solution(mesh):
    return jax.shard_map(
        body,
        mesh=mesh,
        in_specs=(P(("dp", "inner"), None), P(("dp", "inner"), None), P(), P()),
        out_specs=(P(("dp", "inner"), None), P(("dp", "inner"), None), P(("dp", "inner"))),
        check_vma=False,
    )
```

```python
import functools

import jax
import jax.numpy as jnp
from jax import lax
from jax.experimental import pallas as pl
from jax.experimental.pallas import tpu as pltpu
from jax.sharding import PartitionSpec as P

epsilon = 1e-06
f32, bf16 = jnp.float32, jnp.bfloat16
lanes = 128
extra = 16
weights = {"x far": 10, "y far": 10, "x": 0, "a": 10, "b": 10, "late": 2, "gate": 2}
VMEM = pl.BlockSpec(memory_space=pltpu.VMEM)
SMEM = pl.BlockSpec(memory_space=pltpu.SMEM)
ANY = pl.BlockSpec(memory_space=pl.ANY)


def swapped(value, axis, step):
    return lax.ppermute(value, axis, [(place, place ^ step) for place in range(lax.axis_size(axis))])


def swapped_both(value, dp_step, inner_step):
    dp_count, inner_count = lax.axis_size("dp"), lax.axis_size("inner")
    pairs = [
        (d * inner_count + i, (d ^ dp_step) * inner_count + (i ^ inner_step))
        for d in range(dp_count)
        for i in range(inner_count)
    ]
    return lax.ppermute(value, ("dp", "inner"), pairs)


def call(kernel, out_shape, *operands, flops=0, weight=0, scalars=0, scratch=(), after=()):
    moved = sum(o.size * o.dtype.itemsize for o in operands)
    moved += sum(o.size * o.dtype.itemsize for o in jax.tree.leaves(out_shape))
    first, last = len(operands), len(operands) + len(after)
    return pl.pallas_call(
        lambda *refs: kernel(*refs[:first], *refs[last:]),
        out_shape=out_shape,
        in_specs=[SMEM] * scalars + [VMEM] * (len(operands) - scalars) + [ANY] * len(after),
        out_specs=jax.tree.map(lambda _: VMEM, out_shape),
        scratch_shapes=scratch,
        compiler_params=pltpu.CompilerParams(vmem_limit_bytes=40 * 1024 * 1024),
        cost_estimate=pl.CostEstimate(
            flops=flops + int(weight * 1e9), bytes_accessed=moved, transcendentals=0
        ),
    )(*operands, *after)


def shape(dims, kind):
    return jax.ShapeDtypeStruct(dims, kind)


def unit_of(rows):
    wide = rows.astype(f32)
    inverse = lax.rsqrt(jnp.sum(wide * wide, axis=-1, keepdims=True) + epsilon)
    return wide * inverse, inverse


def joined(refs):
    return refs[0][...] if len(refs) == 1 else jnp.concatenate([ref[...] for ref in refs], axis=0)


def pair_terms(scale, offset, text_refs, image_refs, slopes_ref, own=0, losses=True):
    texts, all_images = joined(text_refs), joined(image_refs)
    totals = []
    for left in range(0, all_images.shape[0], 256):
        images = all_images[left : min(left + 256, all_images.shape[0]), :]
        total = jnp.zeros((1, images.shape[0]), f32)
        for start in range(0, texts.shape[0], 256):
            logits = (
                scale
                * lax.dot_general(
                    texts[start : start + 256, :],
                    images,
                    (((1,), (1,)), ((), ())),
                    preferred_element_type=f32,
                )
                + offset
            )
            shrunk = jnp.exp(-jnp.abs(logits))
            raised = 1.0 + shrunk
            inverse = pl.reciprocal(raised, approx=True)
            inverse = inverse * (2.0 - raised * inverse)
            sigmoid = jnp.where(logits >= 0.0, inverse, shrunk * inverse)
            match = None
            if own and left == 0 and start < own:
                text_ids = start + lax.broadcasted_iota(jnp.int32, logits.shape, 0)
                image_ids = lax.broadcasted_iota(jnp.int32, logits.shape, 1)
                match = ((text_ids == image_ids) & (text_ids < own)).astype(f32)
                sigmoid = sigmoid - match
            slopes_ref[start : start + 256, left : left + images.shape[0]] = sigmoid.astype(bf16)
            if losses:
                log_raised = jnp.log(raised) + (shrunk - (raised - 1.0)) * inverse
                softplus = jnp.maximum(logits, 0.0) + log_raised
                if match is not None:
                    softplus = softplus - match * logits
                total = total + jnp.sum(softplus, axis=0, keepdims=True)
        totals.append(total)
    return jnp.concatenate(totals, axis=1) if losses else None


def unit_kernel(*refs):
    for raw, emb in zip(refs[: len(refs) // 2], refs[len(refs) // 2 :]):
        emb[...] = unit_of(raw[...])[0].astype(bf16)


def copies_kernel(*refs):
    for source, target in zip(refs[: len(refs) // 2], refs[len(refs) // 2 :]):
        target[...] = source[...]


def own_rows_kernel(
    scale_ref, bias_ref, text_ref, image_ref, text_emb_ref, image_emb_ref, half_ref, text_out_ref, image_out_ref
):
    text_out_ref[...] = text_ref[...]
    image_out_ref[...] = image_ref[...]
    text_emb_ref[...] = unit_of(text_ref[...])[0].astype(bf16)
    emb = unit_of(image_ref[...])[0].astype(bf16)
    image_emb_ref[...] = emb
    half_ref[...] = emb[emb.shape[0] // 2 :, :]


def near_kernel(raw, *refs):
    out_ref, start = refs[-1], 0
    for place, block in enumerate(refs[:-1]):
        count = block.shape[0]
        out_ref[start : start + count, :] = unit_of(block[...])[0].astype(bf16) if place in raw else block[...]
        start += count


def join_kernel(*refs):
    count = len(refs) // 3
    for first, second, out in zip(refs[:count], refs[count : 2 * count], refs[2 * count :]):
        rows = first.shape[0]
        out[:rows, :] = first[...]
        out[rows:, :] = second[...]


def near_pairs_kernel(own, scale_ref, bias_ref, near_ref, far_ref, images_ref, *refs):
    slopes_ref, loss_ref = refs[-2:]
    rows = far_ref.shape[0]
    texts = (near_ref, far_ref)
    loss = pair_terms(
        scale_ref[0], bias_ref[0], texts, (images_ref,), slopes_ref, rows if own else 0
    )
    loss_ref[...] = loss if own else loss + refs[0][...]


def loss_rows(loss):
    high = loss.astype(bf16).astype(f32)
    which = lax.broadcasted_iota(jnp.int32, (extra, loss.shape[1]), 0)
    return jnp.where(which == 0, high, loss - high).astype(bf16)


def column_cuts(width):
    step = 4 * lanes
    return [(left, min(step, width - left)) for left in range(0, width, step)]


def sums_in_parts(slope_refs, text_refs, width):
    for left, step in column_cuts(width):
        total = None
        for slopes, texts in zip(slope_refs, text_refs):
            part = lax.dot_general(
                slopes[...],
                joined([block.at[:, left : left + step] for block in texts]),
                (((0,), (0,)), ((), ())),
                preferred_element_type=f32,
            )
            total = part if total is None else total + part
        yield left, step, total


def put_panels(out, rows, left, sums):
    for at in range(0, sums.shape[1], lanes):
        panel = (left + at) // lanes
        out[panel * rows : (panel + 1) * rows, :] = sums[:, at : at + lanes].astype(out.dtype)


def far_kernel(count, scale_ref, bias_ref, near_ref, far_ref, near_swapped_ref, far_swapped_ref, *refs):
    image_refs, (own_slopes_ref, *sent_refs), other_slopes_ref = refs[:count], refs[count:-1], refs[-1]
    rows, width = far_ref.shape
    scale, offset = scale_ref[0], bias_ref[0]
    own_texts = (near_ref, far_ref)
    other_texts = (near_swapped_ref, far_swapped_ref)
    loss = pair_terms(scale, offset, own_texts, image_refs, own_slopes_ref)
    loss = loss + pair_terms(scale, offset, other_texts, image_refs, other_slopes_ref)
    slopes = (own_slopes_ref, other_slopes_ref)
    for left, step, total in sums_in_parts(slopes, (own_texts, other_texts), width):
        for place, out in enumerate(sent_refs):
            put_panels(out, rows, left, total[place * rows : (place + 1) * rows, :])
    for place, out in enumerate(sent_refs):
        out[width // lanes * rows :, :] = loss_rows(loss[:, place * rows : (place + 1) * rows])


def near_sums_kernel(
    plain, own_slopes_ref, other_slopes_ref, near_ref, far_ref, near_swapped_ref, far_swapped_ref, loss_ref, *refs
):
    own_ref, own_loss_ref, plain_refs, rest = refs[0], refs[1], refs[2 : 2 + plain], refs[2 + plain :]
    z_refs, z_loss_refs = rest[::2], rest[1::2]
    rows, width = far_ref.shape
    own_texts = (near_ref, far_ref)
    other_texts = (near_swapped_ref, far_swapped_ref)
    slopes = (own_slopes_ref, other_slopes_ref)
    for left, step, total in sums_in_parts(slopes, (own_texts, other_texts), width):
        own_ref[:, left : left + step] = total[:rows, :]
        for place, out in enumerate((*plain_refs, *z_refs), 1):
            put_panels(out, rows, left, total[place * rows : (place + 1) * rows, :])
    own_loss_ref[...] = loss_ref[:, :rows]
    for place, out in enumerate(plain_refs, 1):
        out[width // lanes * rows :, :] = loss_rows(loss_ref[:, place * rows : (place + 1) * rows])
    for place, out in enumerate(z_loss_refs, 1 + plain):
        out[...] = loss_ref[:, place * rows : (place + 1) * rows]


def swapped_pairs_kernel(scale_ref, bias_ref, near_ref, far_ref, images_ref, slopes_ref):
    pair_terms(scale_ref[0], bias_ref[0], (near_ref, far_ref), (images_ref,), slopes_ref, losses=False)


def text_kernel(
    count,
    scale_ref,
    bias_ref,
    near_ref,
    far_ref,
    images_ref,
    images_swapped_ref,
    near_slopes_ref,
    far_slopes_ref,
    other_slopes_ref,
    *refs,
):
    far_refs, far_swapped_refs, outs, slopes_ref = refs[:count], refs[count : 2 * count], refs[2 * count : -1], refs[-1]
    rows, width = far_ref.shape
    own_texts = (near_ref, far_ref)
    pair_terms(scale_ref[0], bias_ref[0], own_texts, far_swapped_refs, slopes_ref, losses=False)
    own_slopes = jnp.concatenate([near_slopes_ref[...], far_slopes_ref[...]], axis=1)
    other_slopes = jnp.concatenate([other_slopes_ref[...], slopes_ref[...]], axis=1)
    for left, step in column_cuts(width):
        cut = slice(left, left + step)
        total = jnp.dot(
            own_slopes,
            joined([ref.at[:, cut] for ref in (images_ref, *far_refs)]),
            preferred_element_type=f32,
        ) + jnp.dot(
            other_slopes,
            joined([ref.at[:, cut] for ref in (images_swapped_ref, *far_swapped_refs)]),
            preferred_element_type=f32,
        )
        for k, out in enumerate(outs):
            out[:, cut] = total[k * rows : (k + 1) * rows, :].astype(out.dtype)


def late_image_kernel(zs, ys, *refs):
    sums, losses, refs = refs[:zs], refs[zs : 2 * zs], refs[2 * zs :]
    parts, payloads, outs = refs[: zs * ys], refs[zs * ys : zs * ys + ys], refs[zs * ys + ys :]
    for k in range(zs):
        height = sums[k].shape[0]
        total, loss = sums[k][...], losses[k][...]
        for part in parts[k * ys : (k + 1) * ys]:
            total = total + part[:height, :].astype(f32)
            last = part[height:, :].astype(f32)
            loss = loss + (last[0:1, :] + last[1:2, :])
        outs[k][:height, :] = total.astype(bf16)
        outs[k][height:, :] = loss_rows(loss)
    for source, target in zip(payloads, outs[zs:]):
        target[...] = source[...]


def gate_kernel(out_ref):
    out_ref[...] = jnp.zeros_like(out_ref)


def row_gradient(rows, sums, scale, out_ref):
    unit_rows, inverse = unit_of(rows)
    unit_grad = scale * sums
    out_ref[...] = (
        unit_grad - unit_rows * jnp.sum(unit_rows * unit_grad, axis=-1, keepdims=True)
    ) * inverse


def end_kernel(batch, images, scale_ref, image_ref, text_ref, grad_ref, loss_ref, text_grad_ref, *refs):
    parts, text_parts, (out_ref, text_out_ref, out_loss_ref, sums_ref) = refs[:images], refs[images:-4], refs[-4:]
    rows, width = image_ref.shape
    loss = loss_ref[...]
    for part in parts:
        last = part[width // lanes * rows :, :].astype(f32)
        loss = loss + (last[0:1, :] + last[1:2, :])
    out_loss_ref[...] = loss / batch
    for panel in range(width // lanes):
        cut = slice(panel * lanes, (panel + 1) * lanes)
        sums = grad_ref[:, cut]
        for part in parts:
            sums = sums + part[panel * rows : (panel + 1) * rows, :].astype(f32)
        sums_ref[:, cut] = sums
    row_gradient(image_ref[...], sums_ref[...], scale_ref[0], out_ref)
    sums = text_grad_ref[...]
    for part in text_parts:
        sums = sums + part[...].astype(f32)
    row_gradient(text_ref[...], sums, scale_ref[0], text_out_ref)


def body(image, text, logarithm_scale, bias):
    rows, width = image.shape
    dp_count, inner_count = lax.axis_size("dp"), lax.axis_size("inner")
    batch = rows * dp_count * inner_count
    scale = jnp.exp(logarithm_scale)
    block = shape((rows, width), bf16)
    wide_block = shape((rows, width), f32)

    image_dp, image_inner = range(4, dp_count, 4), range(2, inner_count, 2)

    half_block = shape((rows // 2, width), bf16)
    text_z = swapped(text, "inner", 1)
    text_x = swapped(text, "dp", 2)
    first_half = image[: rows // 2]
    first_z = [swapped(first_half, "inner", q) for q in image_inner]
    images_y = [swapped(image, "dp", p) for p in image_dp]
    text_emb, image_emb, second_half, text_rows, image_rows = call(
        own_rows_kernel, [block, block, half_block, block, block], scale, bias, text, image, scalars=2
    )
    second_z = [swapped(second_half, "inner", q) for q in image_inner]
    zs, ys = len(first_z), len(images_y)

    (text_z_emb,) = call(unit_kernel, [block], text_z, weight=weights["x"], after=[second_half])
    near_texts = call(
        functools.partial(near_kernel, frozenset({1})),
        shape((3 * rows, width), bf16),
        text_emb,
        text_x,
        text_z_emb,
    )
    texts_swapped = swapped(near_texts, "dp", 1)
    far_places = [(p, q) for q in image_inner for p in image_dp]
    first_z = call(
        unit_kernel, [half_block] * zs, *first_z, weight=weights["a"], after=[text_z_emb]
    )
    first_far = [swapped(emb, "dp", p) for emb in first_z for p in image_dp]
    second_z = call(copies_kernel, [half_block] * zs, *second_z, weight=weights["b"], after=[*first_z, texts_swapped, *images_y])
    (far_text,) = call(copies_kernel, [block], swapped(text_z_emb, "dp", 2), weight=weights["x far"], after=second_z)
    first_far = call(
        copies_kernel, [half_block] * (zs * ys), *first_far, weight=weights["y far"], after=[far_text]
    )
    second_far = [swapped(emb, "dp", p) for emb in second_z for p in image_dp]

    near_images = call(
        functools.partial(near_kernel, frozenset(range(1, 1 + ys))),
        shape(((1 + ys + zs) * rows, width), bf16),
        image_emb,
        *images_y,
        *(part for both in zip(first_z, second_z) for part in both),
    )
    images_swapped = swapped(near_images, "dp", 1)
    far_text_swapped = swapped(far_text, "dp", 1)

    half, near_rows, far_rows = 4 * rows, (1 + ys + zs) * rows, zs * ys * rows
    own_texts, other_texts = (near_texts, far_text), (texts_swapped, far_text_swapped)
    pair_flops = 2 * rows * half * width
    near_slopes, near_loss = shape((half, near_rows), bf16), shape((1, near_rows), f32)
    payload = shape((width // lanes * rows + extra, lanes), bf16)
    own_slopes, loss = call(
        functools.partial(near_pairs_kernel, True),
        (near_slopes, near_loss),
        scale,
        bias,
        *own_texts,
        near_images,
        flops=pair_flops * (1 + ys + zs),
        scalars=2,
    )
    far = call(join_kernel, [block] * (zs * ys), *first_far, *second_far, after=[own_slopes])
    far_swapped = [swapped(emb, "dp", 1) for emb in far]
    far_slopes, *far_sent = call(
        functools.partial(far_kernel, len(far)),
        [shape((half, far_rows), bf16)] + [payload] * len(far),
        scale,
        bias,
        *own_texts,
        *other_texts,
        *far,
        flops=4 * pair_flops * len(far),
        scalars=2,
        scratch=[pltpu.VMEM((half, far_rows), bf16)],
        after=[own_slopes],
    )
    moved = [swapped(part, "dp", p) for part, (p, q) in zip(far_sent, far_places)]
    swapped_slopes = call(
        swapped_pairs_kernel,
        near_slopes,
        scale,
        bias,
        *own_texts,
        images_swapped,
        flops=pair_flops * (1 + ys + zs),
        scalars=2,
        after=far_sent[:1],
    )
    text_grad, text_x_sums, text_z_sums, text_xz_sums = call(
        functools.partial(text_kernel, len(far)),
        (wide_block, block, block, block),
        scale,
        bias,
        *own_texts,
        near_images,
        images_swapped,
        own_slopes,
        far_slopes,
        swapped_slopes,
        *far,
        *far_swapped,
        flops=3 * pair_flops * (1 + ys + zs + len(far)),
        scalars=2,
        scratch=[pltpu.VMEM((half, far_rows), bf16)],
        after=far_sent[:1],
    )
    text_parts = [
        swapped_both(text_xz_sums, 2, 1),
        swapped(text_z_sums, "inner", 1),
        swapped(text_x_sums, "dp", 2),
    ]
    other_slopes, loss = call(
        functools.partial(near_pairs_kernel, False),
        (near_slopes, near_loss),
        scale,
        bias,
        *other_texts,
        near_images,
        loss,
        flops=pair_flops * (1 + ys + zs),
        scalars=2,
        after=[text_x_sums],
    )
    image_grad, own_loss, *sums = call(
        functools.partial(near_sums_kernel, ys),
        [wide_block, shape((1, rows), f32)]
        + [payload] * ys
        + [shape((width // lanes * rows, lanes), f32), shape((1, rows), f32)] * zs,
        own_slopes,
        other_slopes,
        *own_texts,
        *other_texts,
        loss,
        flops=2 * pair_flops * (1 + ys + zs),
        after=[text_x_sums],
    )

    late = call(
        functools.partial(late_image_kernel, zs, ys),
        [payload] * (zs + ys),
        *sums[ys::2],
        *sums[ys + 1 :: 2],
        *moved,
        *sums[:ys],
        weight=weights["late"],
    )
    z_parts = [swapped(part, "inner", q) for part, q in zip(late, image_inner)]
    gate = call(gate_kernel, shape((8, lanes), f32), weight=weights["gate"], after=text_parts[:2])
    image_parts = [*z_parts, *(swapped(part, "dp", p) for part, p in zip(late[zs:], image_dp))]
    image_gradient, text_gradient, image_loss = call(
        functools.partial(end_kernel, batch, len(image_parts)),
        (wide_block, wide_block, shape((1, rows), f32)),
        scale,
        image_rows,
        text_rows,
        image_grad,
        own_loss,
        text_grad,
        *image_parts,
        *text_parts,
        scalars=1,
        scratch=[pltpu.VMEM((rows, width), f32)],
        after=[gate],
    )
    return (image_gradient, text_gradient, image_loss.reshape(rows))


def solution(mesh):
    return jax.shard_map(
        body,
        mesh=mesh,
        in_specs=(P(("dp", "inner"), None), P(("dp", "inner"), None), P(), P()),
        out_specs=(P(("dp", "inner"), None), P(("dp", "inner"), None), P(("dp", "inner"))),
        check_vma=False,
    )
```

```python
import functools

import jax
import jax.numpy as jnp
from jax import lax
from jax.experimental import pallas as pl
from jax.experimental.pallas import tpu as pltpu
from jax.sharding import PartitionSpec as P

epsilon = 1e-06
f32, bf16 = jnp.float32, jnp.bfloat16
lanes = 128
extra = 16
weights = {"x far": 10, "y far": 10, "x": 0, "a": 10, "b": 10, "late": 2, "gate": 2}
VMEM = pl.BlockSpec(memory_space=pltpu.VMEM)
SMEM = pl.BlockSpec(memory_space=pltpu.SMEM)
ANY = pl.BlockSpec(memory_space=pl.ANY)


def swapped(value, axis, step):
    return lax.ppermute(value, axis, [(place, place ^ step) for place in range(lax.axis_size(axis))])


def swapped_both(value, dp_step, inner_step):
    dp_count, inner_count = lax.axis_size("dp"), lax.axis_size("inner")
    pairs = [
        (d * inner_count + i, (d ^ dp_step) * inner_count + (i ^ inner_step))
        for d in range(dp_count)
        for i in range(inner_count)
    ]
    return lax.ppermute(value, ("dp", "inner"), pairs)


def call(kernel, out_shape, *operands, flops=0, weight=0, scalars=0, scratch=(), after=(), out_specs=None):
    moved = sum(o.size * o.dtype.itemsize for o in operands)
    moved += sum(o.size * o.dtype.itemsize for o in jax.tree.leaves(out_shape))
    first, last = len(operands), len(operands) + len(after)
    return pl.pallas_call(
        lambda *refs: kernel(*refs[:first], *refs[last:]),
        out_shape=out_shape,
        in_specs=[SMEM] * scalars + [VMEM] * (len(operands) - scalars) + [ANY] * len(after),
        out_specs=out_specs or jax.tree.map(lambda _: VMEM, out_shape),
        scratch_shapes=scratch,
        compiler_params=pltpu.CompilerParams(vmem_limit_bytes=40 * 1024 * 1024),
        cost_estimate=pl.CostEstimate(
            flops=flops + int(weight * 1e9), bytes_accessed=moved, transcendentals=0
        ),
    )(*operands, *after)


def shape(dims, kind):
    return jax.ShapeDtypeStruct(dims, kind)


def unit_of(rows):
    wide = rows.astype(f32)
    inverse = lax.rsqrt(jnp.sum(wide * wide, axis=-1, keepdims=True) + epsilon)
    return wide * inverse, inverse


def joined(refs):
    return refs[0][...] if len(refs) == 1 else jnp.concatenate([ref[...] for ref in refs], axis=0)


def pair_terms(scale, offset, text_refs, image_refs, slopes_ref, own=0, losses=True):
    texts, all_images = joined(text_refs), joined(image_refs)
    totals = []
    for left in range(0, all_images.shape[0], 256):
        images = all_images[left : min(left + 256, all_images.shape[0]), :]
        total = jnp.zeros((1, images.shape[0]), f32)
        for start in range(0, texts.shape[0], 256):
            logits = (
                scale
                * lax.dot_general(
                    texts[start : start + 256, :],
                    images,
                    (((1,), (1,)), ((), ())),
                    preferred_element_type=f32,
                )
                + offset
            )
            shrunk = jnp.exp(-jnp.abs(logits))
            raised = 1.0 + shrunk
            inverse = pl.reciprocal(raised, approx=True)
            inverse = inverse * (2.0 - raised * inverse)
            sigmoid = jnp.where(logits >= 0.0, inverse, shrunk * inverse)
            match = None
            if own and left == 0 and start < own:
                text_ids = start + lax.broadcasted_iota(jnp.int32, logits.shape, 0)
                image_ids = lax.broadcasted_iota(jnp.int32, logits.shape, 1)
                match = ((text_ids == image_ids) & (text_ids < own)).astype(f32)
                sigmoid = sigmoid - match
            slopes_ref[start : start + 256, left : left + images.shape[0]] = sigmoid.astype(bf16)
            if losses:
                log_raised = jnp.log(raised) + (shrunk - (raised - 1.0)) * inverse
                softplus = jnp.maximum(logits, 0.0) + log_raised
                if match is not None:
                    softplus = softplus - match * logits
                total = total + jnp.sum(softplus, axis=0, keepdims=True)
        totals.append(total)
    return jnp.concatenate(totals, axis=1) if losses else None


def unit_kernel(*refs):
    for raw, emb in zip(refs[: len(refs) // 2], refs[len(refs) // 2 :]):
        emb[...] = unit_of(raw[...])[0].astype(bf16)


def copies_kernel(*refs):
    for source, target in zip(refs[: len(refs) // 2], refs[len(refs) // 2 :]):
        target[...] = source[...]


def own_rows_kernel(
    scale_ref, bias_ref, text_ref, image_ref, text_emb_ref, image_emb_ref, half_ref, text_out_ref, image_out_ref
):
    text_out_ref[...] = text_ref[...]
    image_out_ref[...] = image_ref[...]
    text_emb_ref[...] = unit_of(text_ref[...])[0].astype(bf16)
    emb = unit_of(image_ref[...])[0].astype(bf16)
    image_emb_ref[...] = emb
    half_ref[...] = emb[emb.shape[0] // 2 :, :]


def near_kernel(raw, *refs):
    out_ref, start = refs[-1], 0
    for place, block in enumerate(refs[:-1]):
        count = block.shape[0]
        out_ref[start : start + count, :] = unit_of(block[...])[0].astype(bf16) if place in raw else block[...]
        start += count


def join_kernel(*refs):
    count = len(refs) // 3
    for first, second, out in zip(refs[:count], refs[count : 2 * count], refs[2 * count :]):
        rows = first.shape[0]
        out[:rows, :] = first[...]
        out[rows:, :] = second[...]


def near_pairs_kernel(own, scale_ref, bias_ref, near_ref, far_ref, images_ref, *refs):
    slopes_ref, loss_ref = refs[-2:]
    rows = far_ref.shape[0]
    texts = (near_ref, far_ref)
    loss = pair_terms(
        scale_ref[0], bias_ref[0], texts, (images_ref,), slopes_ref, rows if own else 0
    )
    loss_ref[...] = loss if own else loss + refs[0][...]


def loss_rows(loss):
    high = loss.astype(bf16).astype(f32)
    which = lax.broadcasted_iota(jnp.int32, (extra, loss.shape[1]), 0)
    return jnp.where(which == 0, high, loss - high).astype(bf16)


def column_cuts(width):
    step = 4 * lanes
    return [(left, min(step, width - left)) for left in range(0, width, step)]


def sums_in_parts(slope_refs, text_refs, width):
    for left, step in column_cuts(width):
        total = None
        for slopes, texts in zip(slope_refs, text_refs):
            part = lax.dot_general(
                slopes[...],
                joined([block.at[:, left : left + step] for block in texts]),
                (((0,), (0,)), ((), ())),
                preferred_element_type=f32,
            )
            total = part if total is None else total + part
        yield left, step, total


def put_panels(out, rows, left, sums):
    for at in range(0, sums.shape[1], lanes):
        panel = (left + at) // lanes
        out[panel * rows : (panel + 1) * rows, :] = sums[:, at : at + lanes].astype(out.dtype)


def far_kernel(count, scale_ref, bias_ref, near_ref, far_ref, near_swapped_ref, far_swapped_ref, *refs):
    image_refs, (own_slopes_ref, *sent_refs), other_slopes_ref = refs[:count], refs[count:-1], refs[-1]
    rows, width = far_ref.shape
    scale, offset = scale_ref[0], bias_ref[0]
    own_texts = (near_ref, far_ref)
    other_texts = (near_swapped_ref, far_swapped_ref)
    loss = pair_terms(scale, offset, own_texts, image_refs, own_slopes_ref)
    loss = loss + pair_terms(scale, offset, other_texts, image_refs, other_slopes_ref)
    slopes = (own_slopes_ref, other_slopes_ref)
    for left, step, total in sums_in_parts(slopes, (own_texts, other_texts), width):
        for place, out in enumerate(sent_refs):
            put_panels(out, rows, left, total[place * rows : (place + 1) * rows, :])
    for place, out in enumerate(sent_refs):
        out[width // lanes * rows :, :] = loss_rows(loss[:, place * rows : (place + 1) * rows])


def near_sums_kernel(
    plain, own_slopes_ref, other_slopes_ref, near_ref, far_ref, near_swapped_ref, far_swapped_ref, loss_ref, *refs
):
    own_ref, own_loss_ref, plain_refs, rest = refs[0], refs[1], refs[2 : 2 + plain], refs[2 + plain :]
    z_refs, z_loss_refs = rest[::2], rest[1::2]
    rows, width = far_ref.shape
    own_texts = (near_ref, far_ref)
    other_texts = (near_swapped_ref, far_swapped_ref)
    slopes = (own_slopes_ref, other_slopes_ref)
    for left, step, total in sums_in_parts(slopes, (own_texts, other_texts), width):
        own_ref[:, left : left + step] = total[:rows, :]
        for place, out in enumerate((*plain_refs, *z_refs), 1):
            put_panels(out, rows, left, total[place * rows : (place + 1) * rows, :])
    own_loss_ref[...] = loss_ref[:, :rows]
    for place, out in enumerate(plain_refs, 1):
        out[width // lanes * rows :, :] = loss_rows(loss_ref[:, place * rows : (place + 1) * rows])
    for place, out in enumerate(z_loss_refs, 1 + plain):
        out[...] = loss_ref[:, place * rows : (place + 1) * rows]


def swapped_pairs_kernel(scale_ref, bias_ref, near_ref, far_ref, images_ref, slopes_ref):
    pair_terms(scale_ref[0], bias_ref[0], (near_ref, far_ref), (images_ref,), slopes_ref, losses=False)


def text_kernel(
    count,
    scale_ref,
    bias_ref,
    near_ref,
    far_ref,
    images_ref,
    images_swapped_ref,
    near_slopes_ref,
    far_slopes_ref,
    other_slopes_ref,
    *refs,
):
    far_refs, far_swapped_refs, outs, slopes_ref = refs[:count], refs[count : 2 * count], refs[2 * count : -1], refs[-1]
    rows, width = far_ref.shape
    own_texts = (near_ref, far_ref)
    pair_terms(scale_ref[0], bias_ref[0], own_texts, far_swapped_refs, slopes_ref, losses=False)
    own_slopes = jnp.concatenate([near_slopes_ref[...], far_slopes_ref[...]], axis=1)
    other_slopes = jnp.concatenate([other_slopes_ref[...], slopes_ref[...]], axis=1)
    for left, step in column_cuts(width):
        cut = slice(left, left + step)
        total = jnp.dot(
            own_slopes,
            joined([ref.at[:, cut] for ref in (images_ref, *far_refs)]),
            preferred_element_type=f32,
        ) + jnp.dot(
            other_slopes,
            joined([ref.at[:, cut] for ref in (images_swapped_ref, *far_swapped_refs)]),
            preferred_element_type=f32,
        )
        for k, out in enumerate(outs):
            out[:, cut] = total[k * rows : (k + 1) * rows, :].astype(out.dtype)


def late_image_kernel(zs, ys, *refs):
    sums, losses, refs = refs[:zs], refs[zs : 2 * zs], refs[2 * zs :]
    parts, payloads, outs = refs[: zs * ys], refs[zs * ys : zs * ys + ys], refs[zs * ys + ys :]
    for k in range(zs):
        height = sums[k].shape[0]
        total, loss = sums[k][...], losses[k][...]
        for part in parts[k * ys : (k + 1) * ys]:
            total = total + part[:height, :].astype(f32)
            last = part[height:, :].astype(f32)
            loss = loss + (last[0:1, :] + last[1:2, :])
        outs[k][:height, :] = total.astype(bf16)
        outs[k][height:, :] = loss_rows(loss)
    for source, target in zip(payloads, outs[zs:]):
        target[...] = source[...]


def gate_kernel(out_ref):
    out_ref[...] = jnp.zeros_like(out_ref)


def row_gradient(rows, sums, scale, out_ref):
    unit_rows, inverse = unit_of(rows)
    unit_grad = scale * sums
    out_ref[...] = (
        unit_grad - unit_rows * jnp.sum(unit_rows * unit_grad, axis=-1, keepdims=True)
    ) * inverse


def end_kernel(batch, images, scale_ref, image_ref, text_ref, grad_ref, loss_ref, text_grad_ref, *refs):
    parts, text_parts, outs = refs[:images], refs[images:-7], refs[-7:]
    out_ref, text_out_ref, out_loss_ref, sums_ref, rows_ref, text_rows_ref, done = outs
    rows, width = image_ref.shape
    loss = loss_ref[...]
    for part in parts:
        last = part[width // lanes * rows :, :].astype(f32)
        loss = loss + (last[0:1, :] + last[1:2, :])
    out_loss_ref[...] = loss / batch
    for panel in range(width // lanes):
        cut = slice(panel * lanes, (panel + 1) * lanes)
        sums = grad_ref[:, cut]
        for part in parts:
            sums = sums + part[panel * rows : (panel + 1) * rows, :].astype(f32)
        sums_ref[:, cut] = sums
    row_gradient(image_ref[...], sums_ref[...], scale_ref[0], rows_ref)
    image_copy = pltpu.make_async_copy(rows_ref, out_ref, done.at[0])
    image_copy.start()
    sums = text_grad_ref[...]
    for part in text_parts:
        sums = sums + part[...].astype(f32)
    row_gradient(text_ref[...], sums, scale_ref[0], text_rows_ref)
    text_copy = pltpu.make_async_copy(text_rows_ref, text_out_ref, done.at[1])
    text_copy.start()
    image_copy.wait()
    text_copy.wait()


def body(image, text, logarithm_scale, bias):
    rows, width = image.shape
    dp_count, inner_count = lax.axis_size("dp"), lax.axis_size("inner")
    batch = rows * dp_count * inner_count
    scale = jnp.exp(logarithm_scale)
    block = shape((rows, width), bf16)
    wide_block = shape((rows, width), f32)

    image_dp, image_inner = range(4, dp_count, 4), range(2, inner_count, 2)

    half_block = shape((rows // 2, width), bf16)
    text_z = swapped(text, "inner", 1)
    text_x = swapped(text, "dp", 2)
    first_half = image[: rows // 2]
    first_z = [swapped(first_half, "inner", q) for q in image_inner]
    images_y = [swapped(image, "dp", p) for p in image_dp]
    text_emb, image_emb, second_half, text_rows, image_rows = call(
        own_rows_kernel, [block, block, half_block, block, block], scale, bias, text, image, scalars=2
    )
    second_z = [swapped(second_half, "inner", q) for q in image_inner]
    zs, ys = len(first_z), len(images_y)

    (text_z_emb,) = call(unit_kernel, [block], text_z, weight=weights["x"], after=[second_half])
    near_texts = call(
        functools.partial(near_kernel, frozenset({1})),
        shape((3 * rows, width), bf16),
        text_emb,
        text_x,
        text_z_emb,
    )
    texts_swapped = swapped(near_texts, "dp", 1)
    far_places = [(p, q) for q in image_inner for p in image_dp]
    first_z = call(
        unit_kernel, [half_block] * zs, *first_z, weight=weights["a"], after=[text_z_emb]
    )
    first_far = [swapped(emb, "dp", p) for emb in first_z for p in image_dp]
    second_z = call(copies_kernel, [half_block] * zs, *second_z, weight=weights["b"], after=[*first_z, texts_swapped, *images_y])
    (far_text,) = call(copies_kernel, [block], swapped(text_z_emb, "dp", 2), weight=weights["x far"], after=second_z)
    first_far = call(
        copies_kernel, [half_block] * (zs * ys), *first_far, weight=weights["y far"], after=[far_text]
    )
    second_far = [swapped(emb, "dp", p) for emb in second_z for p in image_dp]

    near_images = call(
        functools.partial(near_kernel, frozenset(range(1, 1 + ys))),
        shape(((1 + ys + zs) * rows, width), bf16),
        image_emb,
        *images_y,
        *(part for both in zip(first_z, second_z) for part in both),
    )
    images_swapped = swapped(near_images, "dp", 1)
    far_text_swapped = swapped(far_text, "dp", 1)

    half, near_rows, far_rows = 4 * rows, (1 + ys + zs) * rows, zs * ys * rows
    own_texts, other_texts = (near_texts, far_text), (texts_swapped, far_text_swapped)
    pair_flops = 2 * rows * half * width
    near_slopes, near_loss = shape((half, near_rows), bf16), shape((1, near_rows), f32)
    payload = shape((width // lanes * rows + extra, lanes), bf16)
    own_slopes, loss = call(
        functools.partial(near_pairs_kernel, True),
        (near_slopes, near_loss),
        scale,
        bias,
        *own_texts,
        near_images,
        flops=pair_flops * (1 + ys + zs),
        scalars=2,
    )
    swapped_slopes = call(
        swapped_pairs_kernel,
        near_slopes,
        scale,
        bias,
        *own_texts,
        images_swapped,
        flops=pair_flops * (1 + ys + zs),
        scalars=2,
        after=[own_slopes],
    )
    far = call(join_kernel, [block] * (zs * ys), *first_far, *second_far, after=[swapped_slopes])
    far_swapped = [swapped(emb, "dp", 1) for emb in far]
    far_slopes, *far_sent = call(
        functools.partial(far_kernel, len(far)),
        [shape((half, far_rows), bf16)] + [payload] * len(far),
        scale,
        bias,
        *own_texts,
        *other_texts,
        *far,
        flops=4 * pair_flops * len(far),
        scalars=2,
        scratch=[pltpu.VMEM((half, far_rows), bf16)],
        after=[swapped_slopes],
    )
    moved = [swapped(part, "dp", p) for part, (p, q) in zip(far_sent, far_places)]
    text_grad, text_x_sums, text_z_sums, text_xz_sums = call(
        functools.partial(text_kernel, len(far)),
        (wide_block, block, block, block),
        scale,
        bias,
        *own_texts,
        near_images,
        images_swapped,
        own_slopes,
        far_slopes,
        swapped_slopes,
        *far,
        *far_swapped,
        flops=3 * pair_flops * (1 + ys + zs + len(far)),
        scalars=2,
        scratch=[pltpu.VMEM((half, far_rows), bf16)],
        after=far_sent[:1],
    )
    text_parts = [
        swapped_both(text_xz_sums, 2, 1),
        swapped(text_z_sums, "inner", 1),
        swapped(text_x_sums, "dp", 2),
    ]
    other_slopes, loss = call(
        functools.partial(near_pairs_kernel, False),
        (near_slopes, near_loss),
        scale,
        bias,
        *other_texts,
        near_images,
        loss,
        flops=pair_flops * (1 + ys + zs),
        scalars=2,
        after=[text_x_sums],
    )
    image_grad, own_loss, *sums = call(
        functools.partial(near_sums_kernel, ys),
        [wide_block, shape((1, rows), f32)]
        + [payload] * ys
        + [shape((width // lanes * rows, lanes), f32), shape((1, rows), f32)] * zs,
        own_slopes,
        other_slopes,
        *own_texts,
        *other_texts,
        loss,
        flops=2 * pair_flops * (1 + ys + zs),
        after=[text_x_sums],
    )

    late = call(
        functools.partial(late_image_kernel, zs, ys),
        [payload] * (zs + ys),
        *sums[ys::2],
        *sums[ys + 1 :: 2],
        *moved,
        *sums[:ys],
        weight=weights["late"],
    )
    z_parts = [swapped(part, "inner", q) for part, q in zip(late, image_inner)]
    gate = call(gate_kernel, shape((8, lanes), f32), weight=weights["gate"], after=text_parts[:2])
    image_parts = [*z_parts, *(swapped(part, "dp", p) for part, p in zip(late[zs:], image_dp))]
    image_gradient, text_gradient, image_loss = call(
        functools.partial(end_kernel, batch, len(image_parts)),
        (wide_block, wide_block, shape((1, rows), f32)),
        scale,
        image_rows,
        text_rows,
        image_grad,
        own_loss,
        text_grad,
        *image_parts,
        *text_parts,
        scalars=1,
        scratch=[pltpu.VMEM((rows, width), f32)] * 3 + [pltpu.SemaphoreType.DMA((2,))],
        out_specs=(ANY, ANY, VMEM),
        after=[gate],
    )
    return (image_gradient, text_gradient, image_loss.reshape(rows))


def solution(mesh):
    return jax.shard_map(
        body,
        mesh=mesh,
        in_specs=(P(("dp", "inner"), None), P(("dp", "inner"), None), P(), P()),
        out_specs=(P(("dp", "inner"), None), P(("dp", "inner"), None), P(("dp", "inner"))),
        check_vma=False,
    )
```

```python
import functools

import jax
import jax.numpy as jnp
from jax import lax
from jax.experimental import pallas as pl
from jax.experimental.pallas import tpu as pltpu
from jax.sharding import PartitionSpec as P

epsilon = 1e-06
f32, bf16 = jnp.float32, jnp.bfloat16
lanes = 128
extra = 16
weights = {"x far": 10, "y far": 10, "x": 0, "a": 10, "b": 10, "late": 2, "gate": 2}
VMEM = pl.BlockSpec(memory_space=pltpu.VMEM)
SMEM = pl.BlockSpec(memory_space=pltpu.SMEM)
ANY = pl.BlockSpec(memory_space=pl.ANY)


def swapped(value, axis, step):
    return lax.ppermute(value, axis, [(place, place ^ step) for place in range(lax.axis_size(axis))])


def swapped_both(value, dp_step, inner_step):
    dp_count, inner_count = lax.axis_size("dp"), lax.axis_size("inner")
    pairs = [
        (d * inner_count + i, (d ^ dp_step) * inner_count + (i ^ inner_step))
        for d in range(dp_count)
        for i in range(inner_count)
    ]
    return lax.ppermute(value, ("dp", "inner"), pairs)


def call(kernel, out_shape, *operands, flops=0, weight=0, scalars=0, scratch=(), after=()):
    moved = sum(o.size * o.dtype.itemsize for o in operands)
    moved += sum(o.size * o.dtype.itemsize for o in jax.tree.leaves(out_shape))
    first, last = len(operands), len(operands) + len(after)
    return pl.pallas_call(
        lambda *refs: kernel(*refs[:first], *refs[last:]),
        out_shape=out_shape,
        in_specs=[SMEM] * scalars + [VMEM] * (len(operands) - scalars) + [ANY] * len(after),
        out_specs=jax.tree.map(lambda _: VMEM, out_shape),
        scratch_shapes=scratch,
        compiler_params=pltpu.CompilerParams(vmem_limit_bytes=40 * 1024 * 1024),
        cost_estimate=pl.CostEstimate(
            flops=flops + int(weight * 1e9), bytes_accessed=moved, transcendentals=0
        ),
    )(*operands, *after)


def shape(dims, kind):
    return jax.ShapeDtypeStruct(dims, kind)


def unit_of(rows):
    wide = rows.astype(f32)
    inverse = lax.rsqrt(jnp.sum(wide * wide, axis=-1, keepdims=True) + epsilon)
    return wide * inverse, inverse


def joined(refs):
    return refs[0][...] if len(refs) == 1 else jnp.concatenate([ref[...] for ref in refs], axis=0)


def pair_terms(scale, offset, text_refs, image_refs, slopes_ref, own=0, losses=True):
    texts, all_images = joined(text_refs), joined(image_refs)
    totals = []
    for left in range(0, all_images.shape[0], 256):
        images = all_images[left : min(left + 256, all_images.shape[0]), :]
        total = jnp.zeros((1, images.shape[0]), f32)
        for start in range(0, texts.shape[0], 256):
            logits = (
                scale
                * lax.dot_general(
                    texts[start : start + 256, :],
                    images,
                    (((1,), (1,)), ((), ())),
                    preferred_element_type=f32,
                )
                + offset
            )
            shrunk = jnp.exp(-jnp.abs(logits))
            raised = 1.0 + shrunk
            inverse = pl.reciprocal(raised, approx=True)
            inverse = inverse * (2.0 - raised * inverse)
            sigmoid = jnp.where(logits >= 0.0, inverse, shrunk * inverse)
            match = None
            if own and left == 0 and start < own:
                text_ids = start + lax.broadcasted_iota(jnp.int32, logits.shape, 0)
                image_ids = lax.broadcasted_iota(jnp.int32, logits.shape, 1)
                match = ((text_ids == image_ids) & (text_ids < own)).astype(f32)
                sigmoid = sigmoid - match
            slopes_ref[start : start + 256, left : left + images.shape[0]] = sigmoid.astype(bf16)
            if losses:
                log_raised = jnp.log(raised) + (shrunk - (raised - 1.0)) * inverse
                softplus = jnp.maximum(logits, 0.0) + log_raised
                if match is not None:
                    softplus = softplus - match * logits
                total = total + jnp.sum(softplus, axis=0, keepdims=True)
        totals.append(total)
    return jnp.concatenate(totals, axis=1) if losses else None


def unit_kernel(*refs):
    for raw, emb in zip(refs[: len(refs) // 2], refs[len(refs) // 2 :]):
        emb[...] = unit_of(raw[...])[0].astype(bf16)


def copies_kernel(*refs):
    for source, target in zip(refs[: len(refs) // 2], refs[len(refs) // 2 :]):
        target[...] = source[...]


def own_rows_kernel(
    scale_ref, bias_ref, text_ref, image_ref, text_emb_ref, image_emb_ref, half_ref, text_out_ref, image_out_ref
):
    text_out_ref[...] = text_ref[...]
    image_out_ref[...] = image_ref[...]
    text_emb_ref[...] = unit_of(text_ref[...])[0].astype(bf16)
    emb = unit_of(image_ref[...])[0].astype(bf16)
    image_emb_ref[...] = emb
    half_ref[...] = emb[emb.shape[0] // 2 :, :]


def near_kernel(raw, *refs):
    out_ref, start = refs[-1], 0
    for place, block in enumerate(refs[:-1]):
        count = block.shape[0]
        out_ref[start : start + count, :] = unit_of(block[...])[0].astype(bf16) if place in raw else block[...]
        start += count


def join_kernel(*refs):
    count = len(refs) // 3
    for first, second, out in zip(refs[:count], refs[count : 2 * count], refs[2 * count :]):
        rows = first.shape[0]
        out[:rows, :] = first[...]
        out[rows:, :] = second[...]


def near_pairs_kernel(own, scale_ref, bias_ref, near_ref, far_ref, images_ref, *refs):
    slopes_ref, loss_ref = refs[-2:]
    rows = far_ref.shape[0]
    texts = (near_ref, far_ref)
    loss = pair_terms(
        scale_ref[0], bias_ref[0], texts, (images_ref,), slopes_ref, rows if own else 0
    )
    loss_ref[...] = loss if own else loss + refs[0][...]


def loss_rows(loss):
    high = loss.astype(bf16).astype(f32)
    which = lax.broadcasted_iota(jnp.int32, (extra, loss.shape[1]), 0)
    return jnp.where(which == 0, high, loss - high).astype(bf16)


def column_cuts(width):
    step = 4 * lanes
    return [(left, min(step, width - left)) for left in range(0, width, step)]


def sums_in_parts(slope_refs, text_refs, width):
    for left, step in column_cuts(width):
        total = None
        for slopes, texts in zip(slope_refs, text_refs):
            part = lax.dot_general(
                slopes[...],
                joined([block.at[:, left : left + step] for block in texts]),
                (((0,), (0,)), ((), ())),
                preferred_element_type=f32,
            )
            total = part if total is None else total + part
        yield left, step, total


def put_panels(out, rows, left, sums):
    for at in range(0, sums.shape[1], lanes):
        panel = (left + at) // lanes
        out[panel * rows : (panel + 1) * rows, :] = sums[:, at : at + lanes].astype(out.dtype)


def far_kernel(count, scale_ref, bias_ref, near_ref, far_ref, near_swapped_ref, far_swapped_ref, *refs):
    image_refs, (own_slopes_ref, *sent_refs), other_slopes_ref = refs[:count], refs[count:-1], refs[-1]
    rows, width = far_ref.shape
    scale, offset = scale_ref[0], bias_ref[0]
    own_texts = (near_ref, far_ref)
    other_texts = (near_swapped_ref, far_swapped_ref)
    loss = pair_terms(scale, offset, own_texts, image_refs, own_slopes_ref)
    loss = loss + pair_terms(scale, offset, other_texts, image_refs, other_slopes_ref)
    slopes = (own_slopes_ref, other_slopes_ref)
    for left, step, total in sums_in_parts(slopes, (own_texts, other_texts), width):
        for place, out in enumerate(sent_refs):
            put_panels(out, rows, left, total[place * rows : (place + 1) * rows, :])
    for place, out in enumerate(sent_refs):
        out[width // lanes * rows :, :] = loss_rows(loss[:, place * rows : (place + 1) * rows])


def near_sums_kernel(
    plain, own_slopes_ref, other_slopes_ref, near_ref, far_ref, near_swapped_ref, far_swapped_ref, loss_ref, *refs
):
    own_ref, own_loss_ref, plain_refs, rest = refs[0], refs[1], refs[2 : 2 + plain], refs[2 + plain :]
    z_refs, z_loss_refs = rest[::2], rest[1::2]
    rows, width = far_ref.shape
    own_texts = (near_ref, far_ref)
    other_texts = (near_swapped_ref, far_swapped_ref)
    slopes = (own_slopes_ref, other_slopes_ref)
    for left, step, total in sums_in_parts(slopes, (own_texts, other_texts), width):
        own_ref[:, left : left + step] = total[:rows, :]
        for place, out in enumerate((*plain_refs, *z_refs), 1):
            put_panels(out, rows, left, total[place * rows : (place + 1) * rows, :])
    own_loss_ref[...] = loss_ref[:, :rows]
    for place, out in enumerate(plain_refs, 1):
        out[width // lanes * rows :, :] = loss_rows(loss_ref[:, place * rows : (place + 1) * rows])
    for place, out in enumerate(z_loss_refs, 1 + plain):
        out[...] = loss_ref[:, place * rows : (place + 1) * rows]


def swapped_pairs_kernel(scale_ref, bias_ref, near_ref, far_ref, images_ref, slopes_ref):
    pair_terms(scale_ref[0], bias_ref[0], (near_ref, far_ref), (images_ref,), slopes_ref, losses=False)


def text_kernel(
    count,
    first,
    scale_ref,
    bias_ref,
    near_ref,
    far_ref,
    images_ref,
    images_swapped_ref,
    near_slopes_ref,
    far_slopes_ref,
    other_slopes_ref,
    *refs,
):
    far_refs, far_swapped_refs, rest = refs[:count], refs[count : 2 * count], refs[2 * count :]
    outs, slopes_ref = (rest[:2], rest[2]) if first else (rest[1:], rest[0])
    rows, width = far_ref.shape
    own_texts = (near_ref, far_ref)
    if first:
        pair_terms(scale_ref[0], bias_ref[0], own_texts, far_swapped_refs, slopes_ref, losses=False)
    held = slice(first * rows, (first + 2) * rows)
    own_slopes = jnp.concatenate([near_slopes_ref[held, :], far_slopes_ref[held, :]], axis=1)
    other_slopes = jnp.concatenate([other_slopes_ref[held, :], slopes_ref[held, :]], axis=1)
    for left, step in column_cuts(width):
        cut = slice(left, left + step)
        total = jnp.dot(
            own_slopes,
            joined([ref.at[:, cut] for ref in (images_ref, *far_refs)]),
            preferred_element_type=f32,
        ) + jnp.dot(
            other_slopes,
            joined([ref.at[:, cut] for ref in (images_swapped_ref, *far_swapped_refs)]),
            preferred_element_type=f32,
        )
        for k, out in enumerate(outs):
            out[:, cut] = total[k * rows : (k + 1) * rows, :].astype(out.dtype)


def late_image_kernel(zs, ys, *refs):
    sums, losses, refs = refs[:zs], refs[zs : 2 * zs], refs[2 * zs :]
    parts, payloads, outs = refs[: zs * ys], refs[zs * ys : zs * ys + ys], refs[zs * ys + ys :]
    for k in range(zs):
        height = sums[k].shape[0]
        total, loss = sums[k][...], losses[k][...]
        for part in parts[k * ys : (k + 1) * ys]:
            total = total + part[:height, :].astype(f32)
            last = part[height:, :].astype(f32)
            loss = loss + (last[0:1, :] + last[1:2, :])
        outs[k][:height, :] = total.astype(bf16)
        outs[k][height:, :] = loss_rows(loss)
    for source, target in zip(payloads, outs[zs:]):
        target[...] = source[...]


def gate_kernel(out_ref):
    out_ref[...] = jnp.zeros_like(out_ref)


def row_gradient(rows, sums, scale, out_ref):
    unit_rows, inverse = unit_of(rows)
    unit_grad = scale * sums
    out_ref[...] = (
        unit_grad - unit_rows * jnp.sum(unit_rows * unit_grad, axis=-1, keepdims=True)
    ) * inverse


def end_kernel(batch, images, scale_ref, image_ref, text_ref, grad_ref, loss_ref, text_grad_ref, *refs):
    parts, text_parts, (out_ref, text_out_ref, out_loss_ref, sums_ref) = refs[:images], refs[images:-4], refs[-4:]
    rows, width = image_ref.shape
    loss = loss_ref[...]
    for part in parts:
        last = part[width // lanes * rows :, :].astype(f32)
        loss = loss + (last[0:1, :] + last[1:2, :])
    out_loss_ref[...] = loss / batch
    for panel in range(width // lanes):
        cut = slice(panel * lanes, (panel + 1) * lanes)
        sums = grad_ref[:, cut]
        for part in parts:
            sums = sums + part[panel * rows : (panel + 1) * rows, :].astype(f32)
        sums_ref[:, cut] = sums
    row_gradient(image_ref[...], sums_ref[...], scale_ref[0], out_ref)
    sums = text_grad_ref[...]
    for part in text_parts:
        sums = sums + part[...].astype(f32)
    row_gradient(text_ref[...], sums, scale_ref[0], text_out_ref)


def body(image, text, logarithm_scale, bias):
    rows, width = image.shape
    dp_count, inner_count = lax.axis_size("dp"), lax.axis_size("inner")
    batch = rows * dp_count * inner_count
    scale = jnp.exp(logarithm_scale)
    block = shape((rows, width), bf16)
    wide_block = shape((rows, width), f32)

    image_dp, image_inner = range(4, dp_count, 4), range(2, inner_count, 2)

    half_block = shape((rows // 2, width), bf16)
    text_z = swapped(text, "inner", 1)
    text_x = swapped(text, "dp", 2)
    first_half = image[: rows // 2]
    first_z = [swapped(first_half, "inner", q) for q in image_inner]
    images_y = [swapped(image, "dp", p) for p in image_dp]
    text_emb, image_emb, second_half, text_rows, image_rows = call(
        own_rows_kernel, [block, block, half_block, block, block], scale, bias, text, image, scalars=2
    )
    second_z = [swapped(second_half, "inner", q) for q in image_inner]
    zs, ys = len(first_z), len(images_y)

    (text_z_emb,) = call(unit_kernel, [block], text_z, weight=weights["x"], after=[second_half])
    near_texts = call(
        functools.partial(near_kernel, frozenset({1})),
        shape((3 * rows, width), bf16),
        text_emb,
        text_x,
        text_z_emb,
    )
    texts_swapped = swapped(near_texts, "dp", 1)
    far_places = [(p, q) for q in image_inner for p in image_dp]
    first_z = call(
        unit_kernel, [half_block] * zs, *first_z, weight=weights["a"], after=[text_z_emb]
    )
    first_far = [swapped(emb, "dp", p) for emb in first_z for p in image_dp]
    second_z = call(copies_kernel, [half_block] * zs, *second_z, weight=weights["b"], after=[*first_z, texts_swapped, *images_y])
    (far_text,) = call(copies_kernel, [block], swapped(text_z_emb, "dp", 2), weight=weights["x far"], after=second_z)
    first_far = call(
        copies_kernel, [half_block] * (zs * ys), *first_far, weight=weights["y far"], after=[far_text]
    )
    second_far = [swapped(emb, "dp", p) for emb in second_z for p in image_dp]

    near_images = call(
        functools.partial(near_kernel, frozenset(range(1, 1 + ys))),
        shape(((1 + ys + zs) * rows, width), bf16),
        image_emb,
        *images_y,
        *(part for both in zip(first_z, second_z) for part in both),
    )
    images_swapped = swapped(near_images, "dp", 1)
    far_text_swapped = swapped(far_text, "dp", 1)

    half, near_rows, far_rows = 4 * rows, (1 + ys + zs) * rows, zs * ys * rows
    own_texts, other_texts = (near_texts, far_text), (texts_swapped, far_text_swapped)
    pair_flops = 2 * rows * half * width
    near_slopes, near_loss = shape((half, near_rows), bf16), shape((1, near_rows), f32)
    payload = shape((width // lanes * rows + extra, lanes), bf16)
    own_slopes, loss = call(
        functools.partial(near_pairs_kernel, True),
        (near_slopes, near_loss),
        scale,
        bias,
        *own_texts,
        near_images,
        flops=pair_flops * (1 + ys + zs),
        scalars=2,
    )
    swapped_slopes = call(
        swapped_pairs_kernel,
        near_slopes,
        scale,
        bias,
        *own_texts,
        images_swapped,
        flops=pair_flops * (1 + ys + zs),
        scalars=2,
        after=[own_slopes],
    )
    far = call(join_kernel, [block] * (zs * ys), *first_far, *second_far, after=[swapped_slopes])
    far_swapped = [swapped(emb, "dp", 1) for emb in far]
    far_slopes, *far_sent = call(
        functools.partial(far_kernel, len(far)),
        [shape((half, far_rows), bf16)] + [payload] * len(far),
        scale,
        bias,
        *own_texts,
        *other_texts,
        *far,
        flops=4 * pair_flops * len(far),
        scalars=2,
        scratch=[pltpu.VMEM((half, far_rows), bf16)],
        after=[swapped_slopes],
    )
    moved = [swapped(part, "dp", p) for part, (p, q) in zip(far_sent, far_places)]
    text_z_sums, text_xz_sums, swapped_far_slopes = call(
        functools.partial(text_kernel, len(far), 2),
        (block, block, shape((half, far_rows), bf16)),
        scale,
        bias,
        *own_texts,
        near_images,
        images_swapped,
        own_slopes,
        far_slopes,
        swapped_slopes,
        *far,
        *far_swapped,
        flops=2 * pair_flops * (1 + ys + zs + len(far)),
        scalars=2,
        after=far_sent[:1],
    )
    text_grad, text_x_sums = call(
        functools.partial(text_kernel, len(far), 0),
        (wide_block, block),
        scale,
        bias,
        *own_texts,
        near_images,
        images_swapped,
        own_slopes,
        far_slopes,
        swapped_slopes,
        *far,
        *far_swapped,
        swapped_far_slopes,
        flops=pair_flops * (1 + ys + zs + len(far)),
        scalars=2,
        after=[text_z_sums],
    )
    text_parts = [
        swapped_both(text_xz_sums, 2, 1),
        swapped(text_z_sums, "inner", 1),
        swapped(text_x_sums, "dp", 2),
    ]
    other_slopes, loss = call(
        functools.partial(near_pairs_kernel, False),
        (near_slopes, near_loss),
        scale,
        bias,
        *other_texts,
        near_images,
        loss,
        flops=pair_flops * (1 + ys + zs),
        scalars=2,
        after=[text_x_sums],
    )
    image_grad, own_loss, *sums = call(
        functools.partial(near_sums_kernel, ys),
        [wide_block, shape((1, rows), f32)]
        + [payload] * ys
        + [shape((width // lanes * rows, lanes), f32), shape((1, rows), f32)] * zs,
        own_slopes,
        other_slopes,
        *own_texts,
        *other_texts,
        loss,
        flops=2 * pair_flops * (1 + ys + zs),
        after=[text_x_sums],
    )

    late = call(
        functools.partial(late_image_kernel, zs, ys),
        [payload] * (zs + ys),
        *sums[ys::2],
        *sums[ys + 1 :: 2],
        *moved,
        *sums[:ys],
        weight=weights["late"],
    )
    z_parts = [swapped(part, "inner", q) for part, q in zip(late, image_inner)]
    gate = call(gate_kernel, shape((8, lanes), f32), weight=weights["gate"], after=text_parts[:2])
    image_parts = [*z_parts, *(swapped(part, "dp", p) for part, p in zip(late[zs:], image_dp))]
    image_gradient, text_gradient, image_loss = call(
        functools.partial(end_kernel, batch, len(image_parts)),
        (wide_block, wide_block, shape((1, rows), f32)),
        scale,
        image_rows,
        text_rows,
        image_grad,
        own_loss,
        text_grad,
        *image_parts,
        *text_parts,
        scalars=1,
        scratch=[pltpu.VMEM((rows, width), f32)],
        after=[gate],
    )
    return (image_gradient, text_gradient, image_loss.reshape(rows))


def solution(mesh):
    return jax.shard_map(
        body,
        mesh=mesh,
        in_specs=(P(("dp", "inner"), None), P(("dp", "inner"), None), P(), P()),
        out_specs=(P(("dp", "inner"), None), P(("dp", "inner"), None), P(("dp", "inner"))),
        check_vma=False,
    )
```
